32 devices in a mesh: freq: 4 (over y, x), tile: 8 (over z, core).
Axes of the slice: x: 2, y: 2, z: 4, core: 2. Of those that a mesh axis runs over, the one named last changes fastest.
Arguments:
- u_data: bfloat16 [8, 4096, 128], P('freq', 'tile'), may hold values from -6 to 6
- u_basis: bfloat16 [8, 16, 16, 2, 48, 256], P('freq', 'tile'), may hold values from -0.25 to 0.25
- v_basis: bfloat16 [8, 16, 16, 2, 48, 256], P('freq', None, 'tile'), may hold values from -0.21875 to 0.21875
- ranks: int32 [8, 16, 16], P('freq'), may hold values from 8 to 48, as said below
- time_mask: int32 [64, 64], replicated, may hold values 0 or 1
Outputs:
- result: bfloat16 [8, 4096, 128], P('freq', 'tile')
The draws below stay inside these ranges and needn't reach their ends.
Inputs may be any that keep to these rules, and one draw needn't show every extreme that they name: For every tile and every m, ranks[2 m + 1, i, j] = 56 - ranks[2 m, i, j].
All inputs are finite; a program needn't handle non-finite values.
Results may differ from the reference program's by a relative error of at most 0.006.
Values may be sent and summed in bfloat16 or wider, within the bound.
No kernel may reach another device: no remote copies, remote signals or barrier semaphores. Data moves between devices by JAX's collectives and lax.ppermute only.
A program may use at most 128 MiB of HBM per device.

```python
import math
import jax
import jax.numpy as jnp
from jax import lax

TILE = 256
RANK = 48
SOURCES = 64
TIMES = 64
FREQ = 8
MT = 16
NT = 16
M = 4096


def draw_ranks(key, part):
    lowest = RANK // 6
    even_ranks = jax.random.randint(jax.random.fold_in(key, 17), (FREQ // 2, MT, NT), lowest, RANK + 1, dtype=jnp.int32)
    even_ranks = even_ranks.at[0, 0, 0].set(lowest)
    odd_ranks = lowest + RANK - even_ranks
    return jnp.stack([even_ranks, odd_ranks], axis=1).reshape(FREQ, MT, NT)


def plant(values, own_key, low, largest):
    index_at = [jax.random.randint(jax.random.fold_in(own_key, axis), (), 0, length) for axis, length in enumerate(values.shape)]
    widest = values.shape.index(max(values.shape))
    next_to = index_at[:widest] + [(index_at[widest] + 1) % values.shape[widest]] + index_at[widest + 1:]
    return values.at[tuple(index_at)].set(low).at[tuple(next_to)].set(largest)


def levels(own_key, extent, split, low, top_value):
    def one(dim, shards_of):
        draws = jax.random.uniform(jax.random.fold_in(jax.random.fold_in(own_key, 6), dim), (shards_of,), jnp.float32, low / len(split), top_value / len(split))
        return jnp.repeat(jnp.exp(draws), extent[dim] // shards_of).reshape((-1,) + (1,) * (len(extent) - dim - 1))

    gain = one(*split[0])
    for cut in split[1:]:
        gain = gain * one(*cut)
    return gain


def gaussian(stream_key, extent, width, limit, split=(), held_as=jnp.bfloat16):
    values = width * jax.random.normal(stream_key, extent, jnp.float32)
    if split:
        values = values * levels(stream_key, extent, split, -0.22, 0.18)
    return jnp.clip(values, -limit, limit).astype(held_as)


def setup_inputs(seed: int = 0) -> dict:
    splits = jax.random.split(jax.random.key(seed), 6)
    return {
        "u_data": gaussian(splits[0], (FREQ, M, 2 * SOURCES), 1.0, 6.0, ((0, 4), (1, 8))),
        "u_basis": gaussian(splits[1], (FREQ, MT, NT, 2, RANK, TILE), (2 * TILE) ** -0.5, 0.25, ((0, 4), (1, 8))),
        "v_basis": gaussian(splits[2], (FREQ, MT, NT, 2, RANK, TILE), (RANK * MT) ** -0.5, 0.21875, ((0, 4), (2, 8))),
        "ranks": draw_ranks(jax.random.fold_in(splits[5], 71), 0),
        "time_mask": plant((jax.random.randint(splits[4], (TIMES, SOURCES), 0, 2) < 1).astype(jnp.int32), jax.random.fold_in(splits[4], 1), 0, 1),
    }


first_bin = 3
highest = lax.Precision.HIGHEST

def rotate(values):
    half_width = values.shape[-1] // 2
    return jnp.concatenate([-values[..., half_width:], values[..., :half_width]], axis=-1)

def conj_apply(leading, trailing):
    half_width = leading.shape[-1] // 2
    real_part = leading[..., :half_width] + trailing[..., half_width:]
    imag_part = leading[..., half_width:] - trailing[..., :half_width]
    return jnp.concatenate([real_part, imag_part], axis=-1)

def plain_apply(leading, trailing):
    half_width = leading.shape[-1] // 2
    real_part = leading[..., :half_width] - trailing[..., half_width:]
    imag_part = leading[..., half_width:] + trailing[..., :half_width]
    return jnp.concatenate([real_part, imag_part], axis=-1)

def rank_weights(tile_ranks, slot_count):
    slots = jnp.arange(slot_count, dtype=jnp.int32)
    return (slots < tile_ranks[..., None]).astype(jnp.float32)[..., None]

def dft_tables(freq_count, time_count):
    sample_ids = jnp.arange(time_count, dtype=jnp.int32)
    bin_ids = jnp.arange(freq_count, dtype=jnp.int32) + first_bin
    phase = sample_ids[:, None] * bin_ids[None, :] % time_count
    angle = 2.0 * math.pi / time_count * phase.astype(jnp.float32)
    factor = 1.0 / math.sqrt(time_count)
    return (jnp.cos(angle) * factor, jnp.sin(angle) * factor)

def adjoint_one(inputs):
    u_slab, u_tiles, v_tiles, tile_ranks = inputs
    local_rows = u_slab.reshape(MT, TILE, 2 * SOURCES).astype(jnp.float32)
    product = jnp.einsum('ijckp,ipq->ijckq', u_tiles.astype(jnp.float32), local_rows)
    coeffs = conj_apply(product[:, :, 0], product[:, :, 1]) * rank_weights(tile_ranks, RANK)
    coeffs = lax.optimization_barrier(coeffs.astype(jnp.bfloat16)).astype(jnp.float32)
    image = jnp.einsum('ijckp,ijkq->jcpq', v_tiles.astype(jnp.float32), coeffs)
    columns = plain_apply(image[:, 0], image[:, 1])
    return columns.reshape(NT * TILE, 2 * SOURCES).astype(jnp.bfloat16)

def forward_one(inputs):
    w_slab, u_tiles, v_tiles, tile_ranks = inputs
    local_cols = w_slab.reshape(NT, TILE, 2 * SOURCES).astype(jnp.float32)
    product = jnp.einsum('ijckp,jpq->ijckq', v_tiles.astype(jnp.float32), local_cols)
    coeffs = conj_apply(product[:, :, 0], product[:, :, 1])
    coeffs = lax.optimization_barrier(coeffs.astype(jnp.bfloat16)).astype(jnp.float32)
    coeffs = coeffs * rank_weights(tile_ranks, RANK)
    output = jnp.einsum('ijckp,ijkq->icpq', u_tiles.astype(jnp.float32), coeffs)
    rows_out = plain_apply(output[:, 0], output[:, 1])
    return rows_out.reshape(MT * TILE, 2 * SOURCES).astype(jnp.bfloat16)

def reference(u_data, u_basis, v_basis, ranks, time_mask):
    adjoint = lax.map(adjoint_one, (u_data, u_basis, v_basis, ranks))
    cos_table, sin_table = dft_tables(FREQ, TIMES)
    kept = time_mask.astype(jnp.float32)
    kept = jnp.concatenate([kept, kept], axis=-1)

    def mix_block(block):
        values = block.astype(jnp.float32)
        signal = jnp.einsum('tf,fnq->tnq', cos_table, values, precision=highest)
        signal = signal + jnp.einsum('tf,fnq->tnq', sin_table, rotate(values), precision=highest)
        signal = signal * kept[:, None, :]
        result = jnp.einsum('tf,tnq->fnq', cos_table, signal, precision=highest)
        result = result - jnp.einsum('tf,tnq->fnq', sin_table, rotate(signal), precision=highest)
        return result.astype(jnp.bfloat16)
    blocks = adjoint.reshape(FREQ, NT, TILE, 2 * SOURCES).transpose(1, 0, 2, 3)
    mixed = lax.map(mix_block, blocks).transpose(1, 0, 2, 3).reshape(FREQ, NT * TILE, 2 * SOURCES)
    return lax.map(forward_one, (mixed, u_basis, v_basis, ranks))
```

```python
import functools
import math

import jax
import jax.numpy as jnp
import numpy as np
from jax import lax
from jax.experimental import pallas as pl
from jax.experimental.pallas import tpu as pltpu
from jax.sharding import PartitionSpec as P

first_bin = 3
vmem_limit = 48 * 1024 * 1024
bf16 = jnp.bfloat16
f32 = jnp.float32

whole = pl.BlockSpec(memory_space=pltpu.VMEM)
scalars = pl.BlockSpec(memory_space=pltpu.SMEM)


def params():
    return pltpu.CompilerParams(vmem_limit_bytes=vmem_limit)


def dot(lhs, rhs, lhs_dim, rhs_dim):
    return lax.dot_general(
        lhs, rhs, (((lhs_dim,), (rhs_dim,)), ((), ())), preferred_element_type=f32
    )


def lag_tables(freq_count, time_count, lanes):
    samples = np.arange(time_count)[:, None]
    lags = np.arange(freq_count)[None, :]
    angle = 2.0 * math.pi / time_count * ((samples * lags) % time_count)
    table = np.zeros((time_count, lanes), np.float32)
    table[:, :freq_count] = np.cos(angle) / time_count
    table[:, freq_count : 2 * freq_count] = np.sin(angle) / time_count
    return table


def pack_rows(stage, slot, row, total, rank, first, second):
    size = first.shape[0]
    stage[slot, pl.ds(row * total, size), :] = first
    stage[slot, pl.ds(row * total + rank, size), :] = second


def adjoint_kernel(where, ranks, u_ref, basis, out, turned, stage):
    freqs, rows, block, _, slots, tile = basis.shape
    total = out.shape[2] // rows
    width = u_ref.shape[2]
    half = width // 2
    step = pl.program_id(0)

    @pl.when(step == 0)
    def _():
        for f in range(freqs):
            values = u_ref[f].astype(f32)
            lane = lax.broadcasted_iota(jnp.int32, values.shape, 1)
            rolled = pltpu.roll(values, half, 1)
            turned[f] = jnp.where(lane < half, rolled, -rolled).astype(bf16)

    for m in range(freqs // 2):
        for i in range(rows):
            pair = []
            for f in (2 * m, 2 * m + 1):
                real = basis[f, i, :, 0].reshape(block * slots, tile)
                imag = basis[f, i, :, 1].reshape(block * slots, tile)
                span = pl.ds(i * tile, tile)
                pair.append(
                    dot(real, u_ref[f, span, :], 1, 0) + dot(imag, turned[f, span, :], 1, 0)
                )
            for j in range(block):
                rank = ranks[2 * m, where[0] * rows + i, step * block + j]
                cut = slice(j * slots, (j + 1) * slots)
                pack_rows(stage, m * block + j, i, total, rank, pair[0][cut], pair[1][cut])
        for j in range(block):
            out[m, j] = stage[m * block + j, pl.ds(0, rows * total), :].astype(bf16)


def forward_kernel(where, ranks, w_ref, basis, out, stage):
    freqs, block, cols, _, slots, tile = basis.shape
    _, _, rows, packed, width = out.shape
    total = packed // cols
    half = width // 2
    step = pl.program_id(0)
    parts = w_ref.shape[0]
    per = w_ref.shape[3]
    for m in range(freqs // 2):
        for j in range(cols):
            pair = []
            for f in (2 * m, 2 * m + 1):
                ids = range(j * tile // per, (j + 1) * tile // per)
                w = jnp.concatenate([w_ref[c, f] for c in ids], axis=1)
                turned = jnp.concatenate([w[half:], -w[:half]], axis=0)
                real = basis[f, :, j, 0].reshape(block * slots, tile)
                imag = basis[f, :, j, 1].reshape(block * slots, tile)
                pair.append(dot(real, w, 1, 1) + dot(imag, turned, 1, 1))
            for i in range(block):
                rank = ranks[2 * m, step * block + i, where[0] * cols + j]
                cut = slice(i * slots, (i + 1) * slots)
                pack_rows(stage, m * block + i, j, total, rank, pair[0][cut], pair[1][cut])
        for i in range(block):
            out[m, i // rows, i % rows] = stage[m * block + i, pl.ds(0, packed), :].astype(bf16)


def unpack_rows(packed, stage, slot, coeffs, count, total, slots, rank_of, base):
    stage[slot, pl.ds(0, count * total), :] = packed.astype(f32)
    row = lax.broadcasted_iota(jnp.int32, (slots, packed.shape[1]), 0)
    for n in range(count):
        rank = rank_of(n)
        first = stage[slot, pl.ds(n * total, slots), :]
        second = stage[slot, pl.ds(n * total + rank, slots), :]
        at = pl.ds(base + n * slots, slots)
        coeffs[0, at, :] = jnp.where(row < rank, first, 0.0).astype(bf16)
        coeffs[1, at, :] = jnp.where(row < total - rank, second, 0.0).astype(bf16)


def plain_product(coeffs, real, imag):
    half = coeffs.shape[1] // 2
    lead = dot(coeffs, real, 0, 0)
    trail = dot(coeffs, imag, 0, 0)
    return jnp.concatenate([lead[:half] - trail[half:], lead[half:] + trail[:half]], axis=0)


def image_kernel(where, ranks, packed, basis, out, stage, coeffs):
    freqs, row_tiles, cols, _, slots, tile = basis.shape
    sources, pairs, _, rows_total, _ = packed.shape
    rows = row_tiles // sources
    total = rows_total // rows
    per = out.shape[3]
    for m in range(pairs):
        for j in range(cols):
            for d in range(sources):
                unpack_rows(
                    packed[d, m, j], stage, d % 2, coeffs, rows, total, slots,
                    lambda n: ranks[2 * m, d * rows + n, where[0] * cols + j],
                    d * rows * slots,
                )
            for f in range(2):
                real = basis[2 * m + f, :, j, 0].reshape(row_tiles * slots, tile)
                imag = basis[2 * m + f, :, j, 1].reshape(row_tiles * slots, tile)
                z = plain_product(coeffs[f], real, imag).astype(bf16)
                for c in range(tile // per):
                    out[j * tile // per + c, 2 * m + f] = z[:, c * per : (c + 1) * per]


def result_kernel(where, ranks, packed, basis, out, stage, coeffs):
    freqs, rows, col_tiles, _, slots, tile = basis.shape
    sources, pairs, _, cols_total, _ = packed.shape
    cols = col_tiles // sources
    total = cols_total // cols
    for m in range(pairs):
        for i in range(rows):
            for d in range(sources):
                unpack_rows(
                    packed[d, m, i], stage, d % 2, coeffs, cols, total, slots,
                    lambda n: ranks[2 * m, where[0] * rows + i, d * cols + n],
                    d * cols * slots,
                )
            for f in range(2):
                real = basis[2 * m + f, i, :, 0].reshape(col_tiles * slots, tile)
                imag = basis[2 * m + f, i, :, 1].reshape(col_tiles * slots, tile)
                r = plain_product(coeffs[f], real, imag)
                out[2 * m + f, pl.ds(i * tile, tile), :] = r.T.astype(bf16)


def mix_kernel(mask, table, z_ref, out):
    owners, freqs, width, per = z_ref.shape
    count = owners * freqs
    half = width // 2
    lags = lax.dot_general(
        mask[...].astype(f32), table[...], (((0,), (0,)), ((), ())),
        precision=lax.Precision.HIGHEST, preferred_element_type=f32,
    )
    cos = [jnp.broadcast_to(lags[:, d : d + 1], (half, per)) for d in range(count)]
    sin = [jnp.broadcast_to(lags[:, count + d : count + d + 1], (half, per)) for d in range(count)]
    z = [z_ref[g // freqs, g % freqs].astype(f32) for g in range(count)]
    for f in range(count):
        real = jnp.zeros((half, per), f32)
        imag = jnp.zeros((half, per), f32)
        for g in range(count):
            c = cos[abs(g - f)]
            s = sin[abs(g - f)]
            zr, zi = z[g][:half], z[g][half:]
            if g >= f:
                real, imag = real + c * zr - s * zi, imag + c * zi + s * zr
            else:
                real, imag = real + c * zr + s * zi, imag + c * zi - s * zr
        out[f // freqs, f % freqs] = jnp.concatenate([real, imag], axis=0).astype(bf16)


def local(u_data, u_basis, v_basis, ranks, time_mask):
    freqs, row_count, width = u_data.shape
    rows, col_tiles, _, slots, tile = u_basis.shape[1:]
    row_tiles, cols = v_basis.shape[1:3]
    total = slots // 6 + slots
    pairs = freqs // 2
    devices = row_tiles // rows
    owners = lax.axis_size("freq")
    per = cols * tile // owners
    where = lax.axis_index("tile").astype(jnp.int32)[None]
    spare = total + 2 * slots

    block = math.gcd(col_tiles, 4)
    packed = pl.pallas_call(
        adjoint_kernel,
        grid=(col_tiles // block,),
        in_specs=[
            scalars,
            scalars,
            pl.BlockSpec((freqs, row_count, width), lambda s: (0, 0, 0)),
            pl.BlockSpec((freqs, rows, block, 2, slots, tile), lambda s: (0, 0, s, 0, 0, 0)),
        ],
        out_specs=pl.BlockSpec((pairs, block, rows * total, width), lambda s: (0, s, 0, 0)),
        out_shape=jax.ShapeDtypeStruct((pairs, col_tiles, rows * total, width), bf16),
        scratch_shapes=[
            pltpu.VMEM((freqs, row_count, width), bf16),
            pltpu.VMEM((pairs * block, rows * total + spare, width), f32),
        ],
        compiler_params=params(),
        name="adjoint",
    )(where, ranks, u_data, u_basis)
    packed = packed.reshape(pairs, devices, cols, rows * total, width).transpose(1, 0, 2, 3, 4)
    landed = lax.all_to_all(packed, "tile", split_axis=0, concat_axis=0, tiled=True)

    image = pl.pallas_call(
        image_kernel,
        in_specs=[scalars, scalars, whole, whole],
        out_specs=whole,
        out_shape=jax.ShapeDtypeStruct((owners, freqs, width, per), bf16),
        scratch_shapes=[
            pltpu.VMEM((2, rows * total + spare, width), f32),
            pltpu.VMEM((2, row_tiles * slots, width), bf16),
        ],
        compiler_params=params(),
        name="image",
    )(where, ranks, landed, v_basis)
    spread = lax.all_to_all(image, "freq", split_axis=0, concat_axis=0, tiled=True)

    table = jnp.asarray(lag_tables(owners * freqs, time_mask.shape[0], 128))
    mixed = pl.pallas_call(
        mix_kernel,
        in_specs=[whole, whole, whole],
        out_specs=whole,
        out_shape=jax.ShapeDtypeStruct((owners, freqs, width, per), bf16),
        compiler_params=params(),
        name="mix",
    )(time_mask, table, spread)
    back = lax.all_to_all(mixed, "freq", split_axis=0, concat_axis=0, tiled=True)

    block = math.gcd(row_tiles, 4 * rows)
    packed = pl.pallas_call(
        forward_kernel,
        grid=(row_tiles // block,),
        in_specs=[
            scalars,
            scalars,
            pl.BlockSpec((owners, freqs, width, per), lambda s: (0, 0, 0, 0)),
            pl.BlockSpec((freqs, block, cols, 2, slots, tile), lambda s: (0, s, 0, 0, 0, 0)),
        ],
        out_specs=pl.BlockSpec(
            (pairs, block // rows, rows, cols * total, width), lambda s: (0, s, 0, 0, 0)
        ),
        out_shape=jax.ShapeDtypeStruct((pairs, devices, rows, cols * total, width), bf16),
        scratch_shapes=[pltpu.VMEM((pairs * block, cols * total + spare, width), f32)],
        compiler_params=params(),
        name="forward",
    )(where, ranks, back, v_basis)
    packed = packed.transpose(1, 0, 2, 3, 4)
    landed = lax.all_to_all(packed, "tile", split_axis=0, concat_axis=0, tiled=True)

    return pl.pallas_call(
        result_kernel,
        in_specs=[scalars, scalars, whole, whole],
        out_specs=whole,
        out_shape=jax.ShapeDtypeStruct((freqs, row_count, width), bf16),
        scratch_shapes=[
            pltpu.VMEM((2, cols * total + spare, width), f32),
            pltpu.VMEM((2, col_tiles * slots, width), bf16),
        ],
        compiler_params=params(),
        name="result",
    )(where, ranks, landed, u_basis)


def solution(mesh):
    placed = (
        P("freq", "tile", None),
        P("freq", "tile", None, None, None, None),
        P("freq", None, "tile", None, None, None),
        P("freq", None, None),
        P(),
    )
    return jax.shard_map(
        local, mesh=mesh, in_specs=placed, out_specs=P("freq", "tile", None), check_vma=False
    )
```

```python
import functools
import math

import jax
import jax.numpy as jnp
import numpy as np
from jax import lax
from jax.experimental import pallas as pl
from jax.experimental.pallas import tpu as pltpu
from jax.sharding import PartitionSpec as P

vmem_limit = 48 * 1024 * 1024
chunk_cols = 2
bf16 = jnp.bfloat16
f32 = jnp.float32

whole = pl.BlockSpec(memory_space=pltpu.VMEM)
scalars = pl.BlockSpec(memory_space=pltpu.SMEM)
far = pl.BlockSpec(memory_space=pltpu.HBM)


def call(kernel, name, ins, outs, scratch):
    specs = [spec for spec, _ in ins]
    shapes = [jax.ShapeDtypeStruct(shape, kind) for shape, kind in outs]
    return pl.pallas_call(
        kernel,
        in_specs=specs,
        out_specs=[whole] * len(outs),
        out_shape=shapes,
        scratch_shapes=scratch,
        compiler_params=pltpu.CompilerParams(vmem_limit_bytes=vmem_limit),
        name=name,
    )(*[value for _, value in ins])


def dot(lhs, rhs, lhs_dim, rhs_dim):
    return lax.dot_general(
        lhs, rhs, (((lhs_dim,), (rhs_dim,)), ((), ())), preferred_element_type=f32
    )


def lag_tables(freq_count, time_count, lanes):
    samples = np.arange(time_count)[:, None]
    lags = np.arange(freq_count)[None, :]
    angle = 2.0 * math.pi / time_count * ((samples * lags) % time_count)
    table = np.zeros((time_count, lanes), np.float32)
    table[:, :freq_count] = np.cos(angle) / time_count
    table[:, freq_count : 2 * freq_count] = np.sin(angle) / time_count
    return table


def pack_rows(stage, slot, row, rank, first, second):
    size = first.shape[0]
    stage[slot, pl.ds(row, size), :] = first
    stage[slot, pl.ds(row + rank, size), :] = second


def unpack_rows(stage, slot, row, rank, total, coeffs, base):
    slots = total - total // 7
    first = stage[slot, pl.ds(row, slots), :]
    second = stage[slot, pl.ds(row + rank, slots), :]
    ids = lax.broadcasted_iota(jnp.int32, first.shape, 0)
    at = pl.ds(pl.multiple_of(base, 16), slots)
    coeffs[0, at, :] = jnp.where(ids < rank, first, 0.0).astype(bf16)
    coeffs[1, at, :] = jnp.where(ids < total - rank, second, 0.0).astype(bf16)


def plain_product(coeffs, real, imag):
    half = coeffs.shape[1] // 2
    lead = dot(coeffs, real, 0, 0)
    trail = dot(coeffs, imag, 0, 0)
    return jnp.concatenate([lead[:half] - trail[half:], lead[half:] + trail[:half]], axis=0)


def adjoint_kernel(devices, chunk, span, where, ranks_far, u_far, basis_far, *rest):
    outs = rest[:devices]
    ranks, u_ref, basis, turned, stage, sems = rest[devices:]
    freqs, rows, _, cols, _, slots, tile = basis_far.shape
    total = slots + slots // 6
    half = u_ref.shape[2] // 2
    me = where[0]
    rank_copy = pltpu.make_async_copy(ranks_far, ranks, sems.at[devices])
    data_copy = pltpu.make_async_copy(u_far, u_ref, sems.at[devices + 1])
    data_copy.start()
    copies = []
    for s in range(devices):
        copies.append(
            pltpu.make_async_copy(
                basis_far.at[:, :, me ^ s, pl.ds(chunk * span, span)], basis.at[s], sems.at[s]
            )
        )
        copies[-1].start()
    rank_copy.start()
    data_copy.wait()
    for f in range(freqs):
        values = u_ref[f].astype(f32)
        lane = lax.broadcasted_iota(jnp.int32, values.shape, 1)
        rolled = pltpu.roll(values, half, 1)
        turned[f] = jnp.where(lane < half, rolled, -rolled).astype(bf16)
    rank_copy.wait()
    group = math.gcd(devices, 4)
    for start in range(0, devices, group):
        for s in range(start, start + group):
            copies[s].wait()
        for m in range(freqs // 2):
            for i in range(rows):
                pair = []
                at = pl.ds(i * tile, tile)
                for f in (2 * m, 2 * m + 1):
                    shape = (group * span * slots, tile)
                    real = basis[pl.ds(start, group), f, i, :, 0].reshape(shape)
                    imag = basis[pl.ds(start, group), f, i, :, 1].reshape(shape)
                    pair.append(dot(real, u_ref[f, at, :], 1, 0) + dot(imag, turned[f, at, :], 1, 0))
                for n in range(group):
                    s = start + n
                    for c in range(span):
                        rank = ranks[2 * m, me * rows + i, (me ^ s) * cols + chunk * span + c]
                        cut = slice((n * span + c) * slots, (n * span + c + 1) * slots)
                        row = (c * rows + i) * total
                        pack_rows(stage, (m * devices + s) * span + c, row, rank, pair[0][cut], pair[1][cut])
            for s in range(start, start + group):
                for c in range(span):
                    at = pl.ds(c * rows * total, rows * total)
                    slot = (m * devices + s) * span + c
                    outs[s][m, at, :] = stage[slot, at, :].astype(bf16)


def image_kernel(devices, owners, chunk, span, where, ranks, basis, *rest):
    packed = rest[:devices]
    outs = rest[devices : devices + owners]
    stage, coeffs, z = rest[devices + owners :]
    freqs, _, rows, cols, _, slots, tile = basis.shape
    total = slots + slots // 6
    width = coeffs.shape[2]
    half = width // 2
    quarter = half // owners
    me, mine = where[0], where[1]
    flat = (devices * rows * slots, tile)
    for m in range(freqs // 2):
        for c in range(span):
            for s in range(devices):
                at = pl.ds(c * rows * total, rows * total)
                stage[s % 4, pl.ds(0, rows * total), :] = packed[s][m, at, :].astype(f32)
                d = me ^ s
                for i in range(rows):
                    rank = ranks[2 * m, d * rows + i, me * cols + chunk * span + c]
                    unpack_rows(stage, s % 4, i * total, rank, total, coeffs, (d * rows + i) * slots)
            for n in range(2):
                f = 2 * m + n
                real = basis[f, :, :, chunk * span + c, 0].reshape(flat)
                imag = basis[f, :, :, chunk * span + c, 1].reshape(flat)
                z[f, :, c * tile : (c + 1) * tile] = plain_product(coeffs[n], real, imag)
    for r in range(owners):
        low = pl.multiple_of((mine ^ r) * quarter, quarter)
        for f in range(freqs):
            real = z[f, pl.ds(low, quarter), :]
            imag = z[f, pl.ds(half + low, quarter), :]
            outs[r][f] = jnp.concatenate([real, imag], axis=0).astype(bf16)


def window_kernel(owners, where, mask, table, out, full):
    full[...] = lax.dot_general(
        mask[...].astype(f32), table[...], (((0,), (0,)), ((), ())),
        precision=lax.Precision.HIGHEST, preferred_element_type=f32,
    )
    quarter = full.shape[0] // owners
    out[...] = full[pl.ds(pl.multiple_of(where[1] * quarter, quarter), quarter), :]


def mix_kernel(owners, where, lags, *rest):
    arrived = rest[:owners]
    outs = rest[owners : 2 * owners]
    z, w = rest[2 * owners :]
    freqs, rows, span = arrived[0].shape
    count = owners * freqs
    quarter = rows // 2
    mine = where[1]
    for r in range(owners):
        for f in range(freqs):
            z[(mine ^ r) * freqs + f] = arrived[r][f].astype(f32)
    shape = (quarter, span)
    cos = [jnp.broadcast_to(lags[:, d : d + 1], shape) for d in range(count)]
    sin = [jnp.broadcast_to(lags[:, count + d : count + d + 1], shape) for d in range(count)]
    for f in range(count):
        real = jnp.zeros(shape, f32)
        imag = jnp.zeros(shape, f32)
        for g in range(count):
            c, s = cos[abs(g - f)], sin[abs(g - f)]
            zr, zi = z[g, :quarter], z[g, quarter:]
            if g >= f:
                real, imag = real + c * zr - s * zi, imag + c * zi + s * zr
            else:
                real, imag = real + c * zr + s * zi, imag + c * zi - s * zr
        w[f, :quarter] = real
        w[f, quarter:] = imag
    for r in range(owners):
        for f in range(freqs):
            outs[r][f] = w[(mine ^ r) * freqs + f].astype(bf16)


def forward_kernel(devices, owners, chunk, span, where, ranks, basis, *rest):
    arrived = rest[:owners]
    outs = rest[owners : owners + devices]
    w, turned, stage = rest[owners + devices :]
    freqs, _, rows, cols, _, slots, tile = basis.shape
    total = slots + slots // 6
    half = w.shape[1] // 2
    quarter = half // owners
    me, mine = where[0], where[1]
    for r in range(owners):
        low = pl.multiple_of((mine ^ r) * quarter, quarter)
        for f in range(freqs):
            real, imag = arrived[r][f, :quarter], arrived[r][f, quarter:]
            w[f, pl.ds(low, quarter), :] = real
            w[f, pl.ds(half + low, quarter), :] = imag
            turned[f, pl.ds(low, quarter), :] = imag
            turned[f, pl.ds(half + low, quarter), :] = -real
    flat = (devices * rows * slots, tile)
    for m in range(freqs // 2):
        for c in range(span):
            at = pl.ds(c * tile, tile)
            pair = []
            for f in (2 * m, 2 * m + 1):
                real = basis[f, :, :, chunk * span + c, 0].reshape(flat)
                imag = basis[f, :, :, chunk * span + c, 1].reshape(flat)
                pair.append(dot(real, w[f, :, at], 1, 1) + dot(imag, turned[f, :, at], 1, 1))
            for d in range(devices):
                for i in range(rows):
                    rank = ranks[2 * m, d * rows + i, me * cols + chunk * span + c]
                    cut = slice((d * rows + i) * slots, (d * rows + i + 1) * slots)
                    row = (c * rows + i) * total
                    pack_rows(stage, (m * devices + d) * span + c, row, rank, pair[0][cut], pair[1][cut])
        for s in range(devices):
            for c in range(span):
                at = pl.ds(c * rows * total, rows * total)
                slot = (m * devices + (me ^ s)) * span + c
                outs[s][m, at, :] = stage[slot, at, :].astype(bf16)


def result_kernel(devices, chunk, span, first, last, where, ranks, basis, *rest):
    packed = rest[:devices]
    rest = rest[devices:]
    if not first:
        before, rest = rest[0], rest[1:]
    out, stage, coeffs = rest
    freqs, rows, _, cols, _, slots, tile = basis.shape
    total = slots + slots // 6
    me = where[0]
    flat = (devices * span * slots, tile)
    for m in range(freqs // 2):
        for i in range(rows):
            for s in range(devices):
                d = me ^ s
                for c in range(span):
                    slot = (s * span + c) % 4
                    at = pl.ds((c * rows + i) * total, total)
                    stage[slot, pl.ds(0, total), :] = packed[s][m, at, :].astype(f32)
                    rank = ranks[2 * m, me * rows + i, d * cols + chunk * span + c]
                    unpack_rows(stage, slot, 0, rank, total, coeffs, (d * span + c) * slots)
            for n in range(2):
                f = 2 * m + n
                cols_at = pl.ds(chunk * span, span)
                real = basis[f, i, :, cols_at, 0].reshape(flat)
                imag = basis[f, i, :, cols_at, 1].reshape(flat)
                r = plain_product(coeffs[n], real, imag)
                if not first:
                    r = r + before[f, i]
                if last:
                    out[f, pl.ds(i * tile, tile), :] = r.T.astype(bf16)
                else:
                    out[f, i] = r


def exchange(values, axis):
    size = lax.axis_size(axis)
    landed = list(values)
    for s in sorted(range(1, size), reverse=True):
        landed[s] = lax.ppermute(values[s], axis, [(d, d ^ s) for d in range(size)])
    return landed


def local(u_data, u_basis, v_basis, ranks, time_mask):
    freqs, row_count, width = u_data.shape
    rows, col_tiles, _, slots, tile = u_basis.shape[1:]
    row_tiles, cols = v_basis.shape[1:3]
    total = slots // 6 + slots
    pairs = freqs // 2
    devices = lax.axis_size("tile")
    owners = lax.axis_size("freq")
    where = jnp.stack([lax.axis_index("tile"), lax.axis_index("freq")]).astype(jnp.int32)
    spare = 2 * slots
    span = math.gcd(cols, chunk_cols)
    chunks = cols // span
    depth = span * rows * total
    quarter = width // owners
    by_cols = u_basis.reshape(freqs, rows, devices, cols, 2, slots, tile)
    by_rows = v_basis.reshape(freqs, devices, rows, cols, 2, slots, tile)

    table = jnp.asarray(lag_tables(owners * freqs, time_mask.shape[0], 128))
    [lags] = call(
        functools.partial(window_kernel, owners),
        "window",
        [(scalars, where), (whole, time_mask), (whole, table)],
        [((width // 2 // owners, 128), f32)],
        [pltpu.VMEM((width // 2, 128), f32)],
    )

    total_out = None
    for k in range(chunks):
        packed = call(
            functools.partial(adjoint_kernel, devices, k, span),
            "adjoint",
            [(scalars, where), (far, ranks), (far, u_data), (far, by_cols)],
            [((pairs, depth, width), bf16)] * devices,
            [
                pltpu.SMEM(ranks.shape, jnp.int32),
                pltpu.VMEM((freqs, row_count, width), bf16),
                pltpu.VMEM((devices, freqs, rows, span, 2, slots, tile), bf16),
                pltpu.VMEM((freqs, row_count, width), bf16),
                pltpu.VMEM((pairs * devices * span, depth + spare, width), f32),
                pltpu.SemaphoreType.DMA((devices + 2,)),
            ],
        )
        landed = exchange(packed, "tile")
        images = call(
            functools.partial(image_kernel, devices, owners, k, span),
            "image",
            [(scalars, where), (scalars, ranks), (whole, by_rows)] + [(whole, x) for x in landed],
            [((freqs, quarter, span * tile), bf16)] * owners,
            [
                pltpu.VMEM((4, rows * total + spare, width), f32),
                pltpu.VMEM((2, row_tiles * slots, width), bf16),
                pltpu.VMEM((freqs, width, span * tile), f32),
            ],
        )
        spread = exchange(images, "freq")
        mixed = call(
            functools.partial(mix_kernel, owners),
            "mix",
            [(scalars, where), (whole, lags)] + [(whole, x) for x in spread],
            [((freqs, quarter, span * tile), bf16)] * owners,
            [pltpu.VMEM((owners * freqs, quarter, span * tile), f32)] * 2,
        )
        back = exchange(mixed, "freq")
        packed = call(
            functools.partial(forward_kernel, devices, owners, k, span),
            "forward",
            [(scalars, where), (scalars, ranks), (whole, by_rows)] + [(whole, x) for x in back],
            [((pairs, depth, width), bf16)] * devices,
            [
                pltpu.VMEM((freqs, width, span * tile), bf16),
                pltpu.VMEM((freqs, width, span * tile), bf16),
                pltpu.VMEM((pairs * devices * span, depth + spare, width), f32),
            ],
        )
        landed = exchange(packed, "tile")
        first, last = k == 0, k == chunks - 1
        out_shape = (freqs, row_count, width) if last else (freqs, rows, width, tile)
        [total_out] = call(
            functools.partial(result_kernel, devices, k, span, first, last),
            "result",
            [(scalars, where), (scalars, ranks), (whole, by_cols)]
            + [(whole, x) for x in landed]
            + ([] if first else [(whole, total_out)]),
            [(out_shape, bf16 if last else f32)],
            [
                pltpu.VMEM((4, total + spare, width), f32),
                pltpu.VMEM((2, devices * span * slots, width), bf16),
            ],
        )
    return total_out


def solution(mesh):
    placed = (
        P("freq", "tile", None),
        P("freq", "tile", None, None, None, None),
        P("freq", None, "tile", None, None, None),
        P("freq", None, None),
        P(),
    )
    return jax.shard_map(
        local, mesh=mesh, in_specs=placed, out_specs=P("freq", "tile", None), check_vma=False
    )
```

```python
import functools
import math

import jax
import jax.numpy as jnp
import numpy as np
from jax import lax
from jax.experimental import pallas as pl
from jax.experimental.pallas import tpu as pltpu
from jax.sharding import PartitionSpec as P

vmem_limit = 48 * 1024 * 1024
chunk_cols = 2
bf16 = jnp.bfloat16
f32 = jnp.float32

whole = pl.BlockSpec(memory_space=pltpu.VMEM)
scalars = pl.BlockSpec(memory_space=pltpu.SMEM)
far = pl.BlockSpec(memory_space=pltpu.HBM)
anywhere = pl.BlockSpec(memory_space=pl.ANY)


def hold(value):
    return pltpu.with_memory_space_constraint(value, pltpu.HBM)


def call(kernel, name, ins, outs, scratch, flops=0, moved=0):
    specs = [spec for spec, _ in ins]
    shapes = [jax.ShapeDtypeStruct(shape, kind) for shape, kind in outs]
    return pl.pallas_call(
        kernel,
        in_specs=specs,
        out_specs=[whole] * len(outs),
        out_shape=shapes,
        scratch_shapes=scratch,
        compiler_params=pltpu.CompilerParams(vmem_limit_bytes=vmem_limit),
        cost_estimate=pl.CostEstimate(flops=flops, bytes_accessed=moved, transcendentals=0),
        name=name,
    )(*[value for _, value in ins])


def dot(lhs, rhs, lhs_dim, rhs_dim):
    return lax.dot_general(
        lhs, rhs, (((lhs_dim,), (rhs_dim,)), ((), ())), preferred_element_type=f32
    )


def lag_tables(freq_count, time_count, lanes):
    samples = np.arange(time_count)[:, None]
    lags = np.arange(freq_count)[None, :]
    angle = 2.0 * math.pi / time_count * ((samples * lags) % time_count)
    table = np.zeros((time_count, lanes), np.float32)
    table[:, :freq_count] = np.cos(angle) / time_count
    table[:, freq_count : 2 * freq_count] = np.sin(angle) / time_count
    return table


def pack_rows(stage, slot, row, rank, first, second):
    size = first.shape[0]
    stage[slot, pl.ds(row, size), :] = first
    stage[slot, pl.ds(row + rank, size), :] = second


def unpack_rows(stage, slot, row, rank, total, coeffs, base):
    slots = total - total // 7
    first = stage[slot, pl.ds(row, slots), :]
    second = stage[slot, pl.ds(row + rank, slots), :]
    ids = lax.broadcasted_iota(jnp.int32, first.shape, 0)
    at = pl.ds(pl.multiple_of(base, 16), slots)
    coeffs[0, at, :] = jnp.where(ids < rank, first, 0.0).astype(bf16)
    coeffs[1, at, :] = jnp.where(ids < total - rank, second, 0.0).astype(bf16)


def plain_product(coeffs, real, imag):
    half = coeffs.shape[1] // 2
    lead = dot(coeffs, real, 0, 0)
    trail = dot(coeffs, imag, 0, 0)
    return jnp.concatenate([lead[:half] - trail[half:], lead[half:] + trail[:half]], axis=0)


def adjoint_kernel(devices, group, g, chunk, span, where, ranks_far, u_far, basis_far, *rest):
    outs = rest[-group - 6 : -6]
    ranks, u_ref, basis, turned, stage, sems = rest[-6:]
    freqs, rows, _, cols, _, slots, tile = basis_far.shape
    total = slots + slots // 6
    half = u_ref.shape[2] // 2
    me = where[0]
    base = group_base(me, group, g)
    rank_copy = pltpu.make_async_copy(ranks_far, ranks, sems.at[0])
    data_copy = pltpu.make_async_copy(u_far, u_ref, sems.at[1])
    data_copy.start()
    copies = {}
    for f in range(freqs):
        for i in range(rows):
            copies[f, i] = pltpu.make_async_copy(
                basis_far.at[f, i, pl.ds(base, group), pl.ds(chunk * span, span)],
                basis.at[f, i],
                sems.at[2 + f * rows + i],
            )
            copies[f, i].start()
    rank_copy.start()
    data_copy.wait()
    for f in range(freqs):
        values = u_ref[f].astype(f32)
        lane = lax.broadcasted_iota(jnp.int32, values.shape, 1)
        rolled = pltpu.roll(values, half, 1)
        turned[f] = jnp.where(lane < half, rolled, -rolled).astype(bf16)
    rank_copy.wait()
    shape = (group * span * slots, tile)
    for m in range(freqs // 2):
        for i in range(rows):
            pair = []
            at = pl.ds(i * tile, tile)
            for f in (2 * m, 2 * m + 1):
                copies[f, i].wait()
                real = basis[f, i, :, :, 0].reshape(shape)
                imag = basis[f, i, :, :, 1].reshape(shape)
                pair.append(dot(real, u_ref[f, at, :], 1, 0) + dot(imag, turned[f, at, :], 1, 0))
            for n in range(group):
                for c in range(span):
                    rank = ranks[2 * m, me * rows + i, (base + n) * cols + chunk * span + c]
                    cut = slice((n * span + c) * slots, (n * span + c + 1) * slots)
                    pack_rows(stage, (m * group + n) * span + c, i * total, rank, pair[0][cut], pair[1][cut])
        unstage(outs, stage, m, group, g, span, rows * total, me)


def unstage(outs, stage, m, group, g, span, size, me):
    for n in range(group):
        place = (me ^ (g * group + n)) & (group - 1)
        for c in range(span):
            slot = (m * group + place) * span + c
            outs[n][m, pl.ds(c * size, size), :] = stage[slot, pl.ds(0, size), :].astype(bf16)


def group_base(me, group, g):
    return (me ^ (g * group)) & ~(group - 1)


def image_kernel(group, owners, g, last, chunk, span, where, ranks, basis, *rest):
    packed = rest[:group][::-1]
    rest = rest[group:]
    if g > 0:
        before, rest = rest[0], rest[1:]
    stage, coeffs, z = rest[-3:]
    freqs, _, rows, cols, _, slots, tile = basis.shape
    total = slots + slots // 6
    width = coeffs.shape[2]
    half = width // 2
    quarter = half // owners
    me, mine = where[0], where[1]
    base = group_base(me, group, g)
    flat = (group * rows * slots, tile)
    for m in range(freqs // 2):
        for c in range(span):
            for n in range(group):
                at = pl.ds(c * rows * total, rows * total)
                stage[n, pl.ds(0, rows * total), :] = packed[n][m, at, :].astype(f32)
                place = (me ^ (g * group + n)) & (group - 1)
                for i in range(rows):
                    rank = ranks[2 * m, (base + place) * rows + i, me * cols + chunk * span + c]
                    unpack_rows(stage, n, i * total, rank, total, coeffs, (place * rows + i) * slots)
            for n in range(2):
                f = 2 * m + n
                real = basis[f, pl.ds(base, group), :, chunk * span + c, 0].reshape(flat)
                imag = basis[f, pl.ds(base, group), :, chunk * span + c, 1].reshape(flat)
                part = plain_product(coeffs[n], real, imag)
                at = pl.ds(c * tile, tile)
                if g > 0:
                    part = part + before[f, :, at]
                if last:
                    z[f, :, at] = part
                else:
                    rest[0][f, :, at] = part
    if last:
        outs = rest[:owners]
        for r in range(owners):
            low = pl.multiple_of((mine ^ r) * quarter, quarter)
            for f in range(freqs):
                real = z[f, pl.ds(low, quarter), :]
                imag = z[f, pl.ds(half + low, quarter), :]
                outs[r][f] = jnp.concatenate([real, imag], axis=0).astype(bf16)


def window_kernel(owners, where, mask, table, out, full):
    full[...] = lax.dot_general(
        mask[...].astype(f32), table[...], (((0,), (0,)), ((), ())),
        precision=lax.Precision.HIGHEST, preferred_element_type=f32,
    )
    quarter = full.shape[0] // owners
    out[...] = full[pl.ds(pl.multiple_of(where[1] * quarter, quarter), quarter), :]


def mix_kernel(owners, where, lags, *rest):
    arrived = rest[:owners][::-1]
    outs = rest[owners : 2 * owners]
    z, w = rest[2 * owners :]
    freqs, rows, span = arrived[0].shape
    count = owners * freqs
    quarter = rows // 2
    mine = where[1]
    for r in range(owners):
        for f in range(freqs):
            z[(mine ^ r) * freqs + f] = arrived[r][f].astype(f32)
    shape = (quarter, span)
    cos = [jnp.broadcast_to(lags[:, d : d + 1], shape) for d in range(count)]
    sin = [jnp.broadcast_to(lags[:, count + d : count + d + 1], shape) for d in range(count)]
    for f in range(count):
        real = jnp.zeros(shape, f32)
        imag = jnp.zeros(shape, f32)
        for g in range(count):
            c, s = cos[abs(g - f)], sin[abs(g - f)]
            zr, zi = z[g, :quarter], z[g, quarter:]
            if g >= f:
                real, imag = real + c * zr - s * zi, imag + c * zi + s * zr
            else:
                real, imag = real + c * zr + s * zi, imag + c * zi - s * zr
        w[f, :quarter] = real
        w[f, quarter:] = imag
    for r in range(owners):
        for f in range(freqs):
            outs[r][f] = w[(mine ^ r) * freqs + f].astype(bf16)


def forward_kernel(group, owners, g, chunk, span, where, ranks, basis, *rest):
    arrived = rest[:owners][::-1]
    outs = rest[-group - 3 : -3]
    w, turned, stage = rest[-3:]
    freqs, _, rows, cols, _, slots, tile = basis.shape
    total = slots + slots // 6
    half = w.shape[1] // 2
    quarter = half // owners
    me, mine = where[0], where[1]
    base = group_base(me, group, g)
    for r in range(owners):
        low = pl.multiple_of((mine ^ r) * quarter, quarter)
        for f in range(freqs):
            real, imag = arrived[r][f, :quarter], arrived[r][f, quarter:]
            w[f, pl.ds(low, quarter), :] = real
            w[f, pl.ds(half + low, quarter), :] = imag
            turned[f, pl.ds(low, quarter), :] = imag
            turned[f, pl.ds(half + low, quarter), :] = -real
    flat = (group * rows * slots, tile)
    for m in range(freqs // 2):
        for c in range(span):
            at = pl.ds(c * tile, tile)
            pair = []
            for f in (2 * m, 2 * m + 1):
                real = basis[f, pl.ds(base, group), :, chunk * span + c, 0].reshape(flat)
                imag = basis[f, pl.ds(base, group), :, chunk * span + c, 1].reshape(flat)
                pair.append(dot(real, w[f, :, at], 1, 1) + dot(imag, turned[f, :, at], 1, 1))
            for n in range(group):
                for i in range(rows):
                    rank = ranks[2 * m, (base + n) * rows + i, me * cols + chunk * span + c]
                    cut = slice((n * rows + i) * slots, (n * rows + i + 1) * slots)
                    pack_rows(stage, (m * group + n) * span + c, i * total, rank, pair[0][cut], pair[1][cut])
        unstage(outs, stage, m, group, g, span, rows * total, me)


def result_kernel(group, g, chunk, span, first, last, where, ranks, basis, *rest):
    packed = rest[:group][::-1]
    rest = rest[group:]
    if not first:
        before, rest = rest[0], rest[1:]
    out, stage, coeffs = rest
    freqs, rows, _, cols, _, slots, tile = basis.shape
    total = slots + slots // 6
    me = where[0]
    base = group_base(me, group, g)
    flat = (group * span * slots, tile)
    for m in range(freqs // 2):
        for i in range(rows):
            for n in range(group):
                place = (me ^ (g * group + n)) & (group - 1)
                for c in range(span):
                    at = pl.ds((c * rows + i) * total, total)
                    stage[n, pl.ds(0, total), :] = packed[n][m, at, :].astype(f32)
                    rank = ranks[2 * m, me * rows + i, (base + place) * cols + chunk * span + c]
                    unpack_rows(stage, n, 0, rank, total, coeffs, (place * span + c) * slots)
            for n in range(2):
                f = 2 * m + n
                cols_at = pl.ds(chunk * span, span)
                real = basis[f, i, pl.ds(base, group), cols_at, 0].reshape(flat)
                imag = basis[f, i, pl.ds(base, group), cols_at, 1].reshape(flat)
                r = plain_product(coeffs[n], real, imag)
                if not first:
                    r = r + before[f, i]
                if last:
                    out[f, pl.ds(i * tile, tile), :] = r.T.astype(bf16)
                else:
                    out[f, i] = r


def send(value, axis, s):
    if s == 0:
        return value
    return lax.ppermute(value, axis, [(d, d ^ s) for d in range(lax.axis_size(axis))])


def local(u_data, u_basis, v_basis, ranks, time_mask):
    freqs, row_count, width = u_data.shape
    rows, col_tiles, _, slots, tile = u_basis.shape[1:]
    row_tiles, cols = v_basis.shape[1:3]
    total = slots // 6 + slots
    pairs = freqs // 2
    devices = lax.axis_size("tile")
    owners = lax.axis_size("freq")
    where = jnp.stack([lax.axis_index("tile"), lax.axis_index("freq")]).astype(jnp.int32)
    spare = 2 * slots
    span = math.gcd(cols, chunk_cols)
    chunks = cols // span
    depth = span * rows * total
    quarter = width // owners
    group = devices
    groups = devices // group
    by_cols = u_basis.reshape(freqs, rows, devices, cols, 2, slots, tile)
    by_rows = v_basis.reshape(freqs, devices, rows, cols, 2, slots, tile)
    packed_out = [((pairs, depth, width), bf16)] * group
    work = {"flops": 4 * row_count * slots * width * col_tiles * freqs * 2, "moved": u_basis.size * 2}
    share = {name: value // groups for name, value in work.items()}
    image_scratch = pltpu.VMEM((freqs, width, span * tile), f32)

    table = jnp.asarray(lag_tables(owners * freqs, time_mask.shape[0], 128))
    [lags] = call(
        functools.partial(window_kernel, owners),
        "window",
        [(scalars, where), (whole, time_mask), (whole, table)],
        [((width // 2 // owners, 128), f32)],
        [pltpu.VMEM((width // 2, 128), f32)],
    )

    total_out = None
    for k in range(chunks):
        landed = {}
        after = []
        for g in reversed(range(groups)):
            packed = call(
                functools.partial(adjoint_kernel, devices, group, g, k, span),
                "adjoint",
                [(scalars, where), (far, hold(ranks)), (far, hold(u_data)), (far, hold(by_cols))] + after,
                packed_out,
                [
                    pltpu.SMEM(ranks.shape, jnp.int32),
                    pltpu.VMEM((freqs, row_count, width), bf16),
                    pltpu.VMEM((freqs, rows, group, span, 2, slots, tile), bf16),
                    pltpu.VMEM((freqs, row_count, width), bf16),
                    pltpu.VMEM((pairs * group * span, rows * total + spare, width), f32),
                    pltpu.SemaphoreType.DMA((2 + freqs * rows,)),
                ],
                **share,
            )
            landed[g] = [send(packed[n], "tile", g * group + n) for n in range(group)]
            after = [(anywhere, packed[-1])]
        image = []
        landed = [x for g in range(groups) for x in landed[g]]
        for g in range(1):
            last = True
            image = call(
                functools.partial(image_kernel, devices, owners, g, last, k, span),
                "image",
                [(scalars, where), (scalars, ranks), (whole, by_rows)]
                + [(whole, x) for x in reversed(landed)]
                + [(whole, x) for x in image],
                [((freqs, quarter, span * tile), bf16)] * owners
                if last
                else [((freqs, width, span * tile), f32)],
                [
                    pltpu.VMEM((devices, rows * total + spare, width), f32),
                    pltpu.VMEM((2, devices * rows * slots, width), bf16),
                    image_scratch,
                ],
                **work,
            )
        spread = [send(image[r], "freq", r) for r in range(owners)]
        mixed = call(
            functools.partial(mix_kernel, owners),
            "mix",
            [(scalars, where), (whole, lags)] + [(whole, x) for x in reversed(spread)],
            [((freqs, quarter, span * tile), bf16)] * owners,
            [pltpu.VMEM((owners * freqs, quarter, span * tile), f32)] * 2,
        )
        back = [send(mixed[r], "freq", r) for r in range(owners)]
        landed = {}
        after = []
        for g in reversed(range(groups)):
            packed = call(
                functools.partial(forward_kernel, group, owners, g, k, span),
                "forward",
                [(scalars, where), (scalars, ranks), (whole, by_rows)]
                + [(whole, x) for x in reversed(back)]
                + after,
                packed_out,
                [
                    pltpu.VMEM((freqs, width, span * tile), bf16),
                    pltpu.VMEM((freqs, width, span * tile), bf16),
                    pltpu.VMEM((pairs * group * span, rows * total + spare, width), f32),
                ],
                **share,
            )
            landed[g] = [send(packed[n], "tile", g * group + n) for n in range(group)]
            after = [(anywhere, packed[-1])]
        landed = [x for g in range(groups) for x in landed[g]]
        for g in range(1):
            first, last = k == 0, k == chunks - 1
            out_shape = (freqs, row_count, width) if last else (freqs, rows, width, tile)
            [total_out] = call(
                functools.partial(result_kernel, devices, g, k, span, first, last),
                "result",
                [(scalars, where), (scalars, ranks), (whole, by_cols)]
                + [(whole, x) for x in reversed(landed)]
                + ([] if first else [(whole, total_out)]),
                [(out_shape, bf16 if last else f32)],
                [
                    pltpu.VMEM((devices, total + spare, width), f32),
                    pltpu.VMEM((2, devices * span * slots, width), bf16),
                ],
                **work,
            )
    return total_out


def solution(mesh):
    placed = (
        P("freq", "tile", None),
        P("freq", "tile", None, None, None, None),
        P("freq", None, "tile", None, None, None),
        P("freq", None, None),
        P(),
    )
    return jax.shard_map(
        local, mesh=mesh, in_specs=placed, out_specs=P("freq", "tile", None), check_vma=False
    )
```

```python
import functools
import math

import jax
import jax.numpy as jnp
import numpy as np
from jax import lax
from jax.experimental import pallas as pl
from jax.experimental.pallas import tpu as pltpu
from jax.sharding import PartitionSpec as P

vmem_limit = 48 * 1024 * 1024
cores = 2
bf16 = jnp.bfloat16
f32 = jnp.float32

whole = pl.BlockSpec(memory_space=pltpu.VMEM)
scalars = pl.BlockSpec(memory_space=pltpu.SMEM)
far = pl.BlockSpec(memory_space=pltpu.HBM)
anywhere = pl.BlockSpec(memory_space=pl.ANY)


def hold(value):
    return pltpu.with_memory_space_constraint(value, pltpu.HBM)


def call(kernel, name, ins, outs, scratch, flops=0, moved=0):
    specs = [spec for spec, _ in ins]
    shapes = [jax.ShapeDtypeStruct(shape, kind) for shape, kind in outs]
    return pl.pallas_call(
        kernel,
        in_specs=specs,
        out_specs=[whole] * len(outs),
        out_shape=shapes,
        scratch_shapes=scratch,
        compiler_params=pltpu.CompilerParams(vmem_limit_bytes=vmem_limit),
        cost_estimate=pl.CostEstimate(flops=flops, bytes_accessed=moved, transcendentals=0),
        name=name,
    )(*[value for _, value in ins])


def dot(lhs, rhs, lhs_dim, rhs_dim, precision=None):
    return lax.dot_general(
        lhs, rhs, (((lhs_dim,), (rhs_dim,)), ((), ())),
        precision=precision, preferred_element_type=f32,
    )


def lag_tables(count, time_count, lanes):
    samples = np.arange(time_count)[:, None]
    lags = np.arange(count)[None, :]
    angle = 2.0 * math.pi / time_count * ((samples * lags) % time_count)
    table = np.zeros((time_count, lanes), np.float32)
    table[:, :count] = np.cos(angle) / time_count
    table[:, count : 2 * count] = np.sin(angle) / time_count
    return table


def lag_choice(count, quarter):
    side = count * 2 * quarter
    choice = np.zeros((2 * count, count, 2, count, 2, quarter), np.float32)
    for f in range(count):
        for g in range(count):
            sign = 1.0 if g >= f else -1.0
            lag = abs(g - f)
            choice[lag, f, 0, g, 0] = 1.0
            choice[lag, f, 1, g, 1] = 1.0
            choice[count + lag, f, 0, g, 1] = -sign
            choice[count + lag, f, 1, g, 0] = sign
    same = np.arange(quarter)[:, None] == np.arange(side)[None, :] % quarter
    return choice.reshape(2 * count, 2 * count * side), same.astype(np.float32)


def pack_rows(stage, slot, row, rank, first, second):
    size = first.shape[0]
    stage[slot, pl.ds(row, size), :] = first
    stage[slot, pl.ds(row + rank, size), :] = second


def unpack_rows(stage, slot, row, rank, total, coeffs, base):
    slots = total - total // 7
    first = stage[slot, pl.ds(row, slots), :]
    second = stage[slot, pl.ds(row + rank, slots), :]
    ids = lax.broadcasted_iota(jnp.int32, first.shape, 0)
    at = pl.ds(pl.multiple_of(base, 16), slots)
    coeffs[0, at, :] = jnp.where(ids < rank, first, 0.0).astype(bf16)
    coeffs[1, at, :] = jnp.where(ids < total - rank, second, 0.0).astype(bf16)


def side_by_side(real, imag):
    flat = (-1, real.shape[-1])
    return jnp.concatenate([real.reshape(flat), imag.reshape(flat)], axis=1)


def plain_product(coeffs, both):
    half, tile = coeffs.shape[1] // 2, both.shape[1] // 2
    product = dot(coeffs, both, 0, 0)
    lead, trail = product[:, :tile], product[:, tile:]
    return jnp.concatenate([lead[:half] - trail[half:], lead[half:] + trail[:half]], axis=0)


def unstage(outs, stage, m, size, chip):
    for q in range(len(outs)):
        for c in range(cores):
            block = stage[(m * len(outs) + (chip ^ q)) * cores + c, pl.ds(0, size), :]
            outs[q][m, pl.ds(c * size, size), :] = block.astype(bf16)


def adjoint_kernel(chips, k, where, ranks_far, u_far, basis_far, *rest):
    outs = rest[-chips - 6 : -6]
    ranks, u_ref, basis, turned, stage, sems = rest[-6:]
    freqs, rows, devices, cols, _, slots, tile = basis_far.shape
    total = slots + slots // 6
    half = u_ref.shape[2] // 2
    me = where[0]
    rank_copy = pltpu.make_async_copy(ranks_far, ranks, sems.at[0])
    data_copy = pltpu.make_async_copy(u_far, u_ref, sems.at[1])
    data_copy.start()
    copies = {}
    for i in range(rows):
        for f in range(freqs):
            copies[f, i] = pltpu.make_async_copy(
                basis_far.at[f, i, :, k], basis.at[f, i], sems.at[2 + f * rows + i]
            )
            copies[f, i].start()
    rank_copy.start()
    data_copy.wait()
    for f in range(freqs):
        values = u_ref[f].astype(f32)
        lane = lax.broadcasted_iota(jnp.int32, values.shape, 1)
        rolled = pltpu.roll(values, half, 1)
        turned[f] = jnp.where(lane < half, rolled, -rolled).astype(bf16)
    rank_copy.wait()
    for m in range(freqs // 2):
        for i in range(rows):
            pair = []
            at = pl.ds(i * tile, tile)
            for f in (2 * m, 2 * m + 1):
                copies[f, i].wait()
                both = side_by_side(basis[f, i, :, 0], basis[f, i, :, 1])
                data = jnp.concatenate([u_ref[f, at, :], turned[f, at, :]], axis=0)
                pair.append(dot(both, data, 1, 0))
            for d in range(devices):
                rank = ranks[2 * m, me * rows + i, d * cols + k]
                cut = slice(d * slots, (d + 1) * slots)
                pack_rows(stage, m * devices + d, i * total, rank, pair[0][cut], pair[1][cut])
        unstage(outs, stage, m, rows * total, me // cores)


def split_kernel(chips, where, *rest):
    packed, out = rest[:chips][::-1], rest[-1]
    pairs, size = out.shape[0], out.shape[1] // chips
    other = pl.multiple_of((1 - where[0] % cores) * size, 16)
    for m in range(pairs):
        for q in range(chips):
            out[m, pl.ds(q * size, size), :] = packed[q][m, pl.ds(other, size), :]


def arrived_block(packed, own, m, q, size, core):
    if own:
        return packed[q][m, pl.ds(pl.multiple_of(core * size, 16), size), :]
    return packed[0][m, pl.ds(q * size, size), :]


def image_kernel(chips, owners, own, k, where, ranks, basis, *rest):
    count = chips if own else 1
    packed, rest = rest[:count][::-1], rest[count:]
    if not own:
        before, rest = rest[0], rest[1:]
    stage, coeffs, z = rest[-3:]
    freqs, _, _, rows, cols, _, slots, tile = basis.shape
    total = slots + slots // 6
    half = coeffs.shape[2] // 2
    quarter = half // owners
    me, mine = where[0], where[1]
    chip, core = me // cores, me % cores
    side = core if own else 1 - core
    for m in range(freqs // 2):
        for q in range(chips):
            block = arrived_block(packed, own, m, q, rows * total, core)
            stage[q, pl.ds(0, rows * total), :] = block.astype(f32)
            for i in range(rows):
                row = ((chip ^ q) * cores + side) * rows + i
                rank = ranks[2 * m, row, me * cols + k]
                unpack_rows(stage, q, i * total, rank, total, coeffs, ((chip ^ q) * rows + i) * slots)
        for n in range(2):
            f = 2 * m + n
            both = side_by_side(basis[f, :, side, :, k, 0], basis[f, :, side, :, k, 1])
            part = plain_product(coeffs[n], both)
            if own:
                rest[0][f] = part
            else:
                z[f] = part + before[f]
    if not own:
        outs = rest[:owners]
        for r in range(owners):
            low = pl.multiple_of((mine ^ r) * quarter, quarter)
            for f in range(freqs):
                real = z[f, pl.ds(low, quarter), :]
                imag = z[f, pl.ds(half + low, quarter), :]
                outs[r][f] = jnp.concatenate([real, imag], axis=0).astype(bf16)


def window_kernel(owners, where, mask, table, choice, same, high, low, full):
    exact = lax.Precision.HIGHEST
    full[...] = dot(mask[...].astype(f32), table[...], 0, 0, exact)
    quarter, side = same.shape
    mine = full[pl.ds(pl.multiple_of(where[1] * quarter, quarter), quarter), :]
    entries = dot(mine[:, : choice.shape[0]], choice[...], 1, 0, exact)
    for n in range(side // quarter):
        block = entries[:, n * side : (n + 1) * side] * same[...]
        upper = block.astype(bf16)
        high[n * quarter : (n + 1) * quarter, :] = upper
        low[n * quarter : (n + 1) * quarter, :] = (block - upper.astype(f32)).astype(bf16)


def mix_kernel(owners, where, high, low, *rest):
    arrived = rest[:owners][::-1]
    outs = rest[owners : 2 * owners]
    z, w = rest[2 * owners :]
    freqs, rows, span = arrived[0].shape
    mine = where[1]
    size = freqs * rows
    for r in range(owners):
        z[pl.ds(pl.multiple_of((mine ^ r) * size, 16), size), :] = arrived[r][...].reshape(size, span)
    w[...] = dot(high[...], z[...], 1, 0) + dot(low[...], z[...], 1, 0)
    for r in range(owners):
        block = w[pl.ds(pl.multiple_of((mine ^ r) * size, 16), size), :]
        outs[r][...] = block.reshape(freqs, rows, span).astype(bf16)


def forward_kernel(chips, owners, k, where, ranks, basis, *rest):
    arrived = rest[:owners][::-1]
    outs = rest[-chips - 2 : -2]
    w, stage = rest[-2:]
    freqs, _, _, rows, cols, _, slots, tile = basis.shape
    devices = chips * cores
    total = slots + slots // 6
    half = w.shape[1] // 2
    quarter = half // owners
    me, mine = where[0], where[1]
    for r in range(owners):
        low = pl.multiple_of((mine ^ r) * quarter, quarter)
        for f in range(freqs):
            real, imag = arrived[r][f, :quarter], arrived[r][f, quarter:]
            w[f, pl.ds(low, quarter), :tile] = real
            w[f, pl.ds(half + low, quarter), :tile] = imag
            w[f, pl.ds(low, quarter), tile:] = imag
            w[f, pl.ds(half + low, quarter), tile:] = -real
    for m in range(freqs // 2):
        pair = []
        for f in (2 * m, 2 * m + 1):
            both = side_by_side(basis[f, :, :, :, k, 0], basis[f, :, :, :, k, 1])
            pair.append(dot(both, w[f], 1, 1))
        for d in range(devices):
            for i in range(rows):
                rank = ranks[2 * m, d * rows + i, me * cols + k]
                cut = slice((d * rows + i) * slots, (d * rows + i + 1) * slots)
                pack_rows(stage, m * devices + d, i * total, rank, pair[0][cut], pair[1][cut])
        unstage(outs, stage, m, rows * total, me // cores)


def result_kernel(chips, own, k, first, last, where, ranks, basis, *rest):
    count = chips if own else 1
    packed, rest = rest[:count][::-1], rest[count:]
    if not first:
        before, rest = rest[0], rest[1:]
    out, stage, coeffs = rest
    freqs, rows, _, _, cols, _, slots, tile = basis.shape
    total = slots + slots // 6
    me = where[0]
    chip, core = me // cores, me % cores
    side = core if own else 1 - core
    for m in range(freqs // 2):
        for q in range(chips):
            block = arrived_block(packed, own, m, q, rows * total, core)
            stage[q, pl.ds(0, rows * total), :] = block.astype(f32)
        for i in range(rows):
            for q in range(chips):
                col = ((chip ^ q) * cores + side) * cols + k
                rank = ranks[2 * m, me * rows + i, col]
                unpack_rows(stage, q, i * total, rank, total, coeffs.at[i], (chip ^ q) * slots)
            for n in range(2):
                f = 2 * m + n
                both = side_by_side(basis[f, i, :, side, k, 0], basis[f, i, :, side, k, 1])
                r = plain_product(coeffs[i, n], both)
                if not first:
                    r = r + before[f, i]
                if last:
                    out[f, pl.ds(i * tile, tile), :] = r.T.astype(bf16)
                else:
                    out[f, i] = r


def send(value, axis, s):
    if s == 0:
        return value
    return lax.ppermute(value, axis, [(d, d ^ s) for d in range(lax.axis_size(axis))])


def local(u_data, u_basis, v_basis, ranks, time_mask):
    freqs, row_count, width = u_data.shape
    rows, col_tiles, _, slots, tile = u_basis.shape[1:]
    row_tiles, cols = v_basis.shape[1:3]
    total = slots // 6 + slots
    pairs = freqs // 2
    devices = lax.axis_size("tile")
    chips = devices // cores
    owners = lax.axis_size("freq")
    where = jnp.stack([lax.axis_index("tile"), lax.axis_index("freq")]).astype(jnp.int32)
    depth = rows * total
    stage_rows = depth + 2 * slots
    quarter = width // 2 // owners
    count = owners * freqs
    side = count * 2 * quarter
    by_cols = u_basis.reshape(freqs, rows, devices, cols, 2, slots, tile)
    by_chip_cols = u_basis.reshape(freqs, rows, chips, cores, cols, 2, slots, tile)
    by_chip_rows = v_basis.reshape(freqs, chips, cores, rows, cols, 2, slots, tile)
    per_chip = [((pairs, cores * depth, width), bf16)] * chips
    per_owner = [((freqs, 2 * quarter, tile), bf16)] * owners
    work = {
        "flops": 4 * row_count * slots * width * col_tiles * freqs * 2 // cols,
        "moved": u_basis.size * 2 // cols,
    }
    part = {name: value // 2 for name, value in work.items()}

    def over_chips(packed):
        return [send(packed[q], "tile", q * cores) for q in range(chips)]

    def to_sibling(landed, after):
        [other] = call(
            functools.partial(split_kernel, chips),
            "split",
            [(scalars, where)]
            + [(whole, x) for x in reversed(landed)]
            + [(anywhere, x) for x in after],
            [((pairs, chips * depth, width), bf16)],
            [],
        )
        return send(other, "tile", 1)

    table = lag_tables(count, time_mask.shape[0], 128)
    choice, same = lag_choice(count, quarter)
    window = call(
        functools.partial(window_kernel, owners),
        "window",
        [(scalars, where)] + [(whole, jnp.asarray(x)) for x in (time_mask, table, choice, same)],
        [((side, side), bf16)] * 2,
        [pltpu.VMEM((width // 2, 128), f32)],
    )

    def adjoint(k, after):
        return call(
            functools.partial(adjoint_kernel, chips, k),
            "adjoint",
            [(scalars, where), (far, hold(ranks)), (far, hold(u_data)), (far, hold(by_cols))]
            + [(anywhere, x) for x in after],
            per_chip,
            [
                pltpu.SMEM(ranks.shape, jnp.int32),
                pltpu.VMEM((freqs, row_count, width), bf16),
                pltpu.VMEM((freqs, rows, devices, 2, slots, tile), bf16),
                pltpu.VMEM((freqs, row_count, width), bf16),
                pltpu.VMEM((pairs * devices, stage_rows, width), f32),
                pltpu.SemaphoreType.DMA((2 + freqs * rows,)),
            ],
            **work,
        )

    def image(k, landed, after):
        other = to_sibling(landed, after)
        scratch = [
            pltpu.VMEM((chips, stage_rows, width), f32),
            pltpu.VMEM((2, chips * rows * slots, width), bf16),
            pltpu.VMEM((freqs, width, tile), f32),
        ]
        basics = [(scalars, where), (scalars, ranks), (whole, by_chip_rows)]
        here = call(
            functools.partial(image_kernel, chips, owners, True, k),
            "image",
            basics + [(whole, x) for x in reversed(landed)],
            [((freqs, width, tile), f32)],
            scratch,
            **part,
        )
        return call(
            functools.partial(image_kernel, chips, owners, False, k),
            "image",
            basics + [(whole, other), (whole, here[0])],
            per_owner,
            scratch,
            **part,
        )

    def over_owners(values):
        return [send(values[r], "freq", r) for r in range(owners)]

    def mix(spread):
        return call(
            functools.partial(mix_kernel, owners),
            "mix",
            [(scalars, where)] + [(whole, x) for x in window] + [(whole, x) for x in reversed(spread)],
            per_owner,
            [pltpu.VMEM((side, tile), bf16), pltpu.VMEM((side, tile), f32)],
            flops=4 * side * side * tile,
        )

    def forward(k, back):
        return call(
            functools.partial(forward_kernel, chips, owners, k),
            "forward",
            [(scalars, where), (scalars, ranks), (whole, by_chip_rows)]
            + [(whole, x) for x in reversed(back)],
            per_chip,
            [
                pltpu.VMEM((freqs, width, 2 * tile), bf16),
                pltpu.VMEM((pairs * devices, stage_rows, width), f32),
            ],
            **work,
        )

    def result(k, landed, before):
        other = to_sibling(landed, [] if before is None else [before])
        for own in (True, False):
            first, last = k == 0 and own, k == cols - 1 and not own
            out_shape = (freqs, row_count, width) if last else (freqs, rows, width, tile)
            [before] = call(
                functools.partial(result_kernel, chips, own, k, first, last),
                "result",
                [(scalars, where), (scalars, ranks), (whole, by_chip_cols)]
                + [(whole, x) for x in (reversed(landed) if own else [other])]
                + ([] if first else [(whole, before)]),
                [(out_shape, bf16 if last else f32)],
                [
                    pltpu.VMEM((chips, stage_rows, width), f32),
                    pltpu.VMEM((rows, 2, chips * slots, width), bf16),
                ],
                **part,
            )
        return before

    packed, after = [], []
    for k in range(cols):
        packed.append(adjoint(k, after))
        after = [packed[k][-1]]
    landed = [over_chips(x) for x in packed]
    images, after = [], []
    for k in range(cols):
        images.append(image(k, landed[k], after))
        after = [images[k][0]]
    spread = [over_owners(x) for x in images]
    back = [over_owners(mix(x)) for x in spread]
    landed = [over_chips(forward(k, x)) for k, x in enumerate(back)]
    before = None
    for k in range(cols):
        before = result(k, landed[k], before)
    return before


def solution(mesh):
    placed = (
        P("freq", "tile", None),
        P("freq", "tile", None, None, None, None),
        P("freq", None, "tile", None, None, None),
        P("freq", None, None),
        P(),
    )
    return jax.shard_map(
        local, mesh=mesh, in_specs=placed, out_specs=P("freq", "tile", None), check_vma=False
    )
```

```python
import functools
import math

import jax
import jax.numpy as jnp
import numpy as np
from jax import lax
from jax.experimental import pallas as pl
from jax.experimental.pallas import tpu as pltpu
from jax.sharding import PartitionSpec as P

vmem_limit = 48 * 1024 * 1024
bf16 = jnp.bfloat16
f32 = jnp.float32

whole = pl.BlockSpec(memory_space=pltpu.VMEM)
scalars = pl.BlockSpec(memory_space=pltpu.SMEM)
far = pl.BlockSpec(memory_space=pltpu.HBM)
anywhere = pl.BlockSpec(memory_space=pl.ANY)


def hold(value):
    return pltpu.with_memory_space_constraint(value, pltpu.HBM)


def call(kernel, name, ins, outs, scratch, flops=0, moved=0):
    specs = [spec for spec, _ in ins]
    shapes = [jax.ShapeDtypeStruct(shape, kind) for shape, kind in outs]
    return pl.pallas_call(
        kernel,
        in_specs=specs,
        out_specs=[whole] * len(outs),
        out_shape=shapes,
        scratch_shapes=scratch,
        compiler_params=pltpu.CompilerParams(vmem_limit_bytes=vmem_limit),
        cost_estimate=pl.CostEstimate(flops=flops, bytes_accessed=moved, transcendentals=0),
        name=name,
    )(*[value for _, value in ins])


def dot(lhs, rhs, lhs_dim, rhs_dim, precision=None):
    return lax.dot_general(
        lhs, rhs, (((lhs_dim,), (rhs_dim,)), ((), ())),
        precision=precision, preferred_element_type=f32,
    )


def lag_tables(count, time_count, lanes):
    samples = np.arange(time_count)[:, None]
    lags = np.arange(count)[None, :]
    angle = 2.0 * math.pi / time_count * ((samples * lags) % time_count)
    table = np.zeros((time_count, lanes), np.float32)
    table[:, :count] = np.cos(angle) / time_count
    table[:, count : 2 * count] = np.sin(angle) / time_count
    return table


def lag_choice(count, quarter):
    side = count * 2 * quarter
    choice = np.zeros((2 * count, count, 2, count, 2, quarter), np.float32)
    for f in range(count):
        for g in range(count):
            sign = 1.0 if g >= f else -1.0
            lag = abs(g - f)
            choice[lag, f, 0, g, 0] = 1.0
            choice[lag, f, 1, g, 1] = 1.0
            choice[count + lag, f, 0, g, 1] = -sign
            choice[count + lag, f, 1, g, 0] = sign
    same = np.arange(quarter)[:, None] == np.arange(side)[None, :] % quarter
    return choice.reshape(2 * count, 2 * count * side), same.astype(np.float32)


def pack_rows(stage, slot, row, rank, first, second):
    size = first.shape[0]
    stage[slot, pl.ds(row, size), :] = first
    stage[slot, pl.ds(row + rank, size), :] = second


def unpack_rows(stage, slot, row, rank, total, coeffs, base):
    slots = total - total // 7
    first = stage[slot, pl.ds(row, slots), :]
    second = stage[slot, pl.ds(row + rank, slots), :]
    ids = lax.broadcasted_iota(jnp.int32, first.shape, 0)
    at = pl.ds(pl.multiple_of(base, 16), slots)
    coeffs[0, at, :] = jnp.where(ids < rank, first, 0.0).astype(bf16)
    coeffs[1, at, :] = jnp.where(ids < total - rank, second, 0.0).astype(bf16)


def side_by_side(real, imag):
    flat = (-1, real.shape[-1])
    return jnp.concatenate([real.reshape(flat), imag.reshape(flat)], axis=1)


def plain_product(coeffs, both):
    half, tile = coeffs.shape[1] // 2, both.shape[1] // 2
    product = dot(coeffs, both, 0, 0)
    lead, trail = product[:, :tile], product[:, tile:]
    return jnp.concatenate([lead[:half] - trail[half:], lead[half:] + trail[:half]], axis=0)


def unstage(outs, stage, m, span, size, me):
    for s in range(len(outs)):
        for c in range(span):
            block = stage[(m * len(outs) + (me ^ s)) * span + c, pl.ds(0, size), :]
            outs[s][m, pl.ds(c * size, size), :] = block.astype(bf16)


def adjoint_kernel(devices, parts, ranks_far, u_far, basis_far, other_far, *rest):
    outs, other = rest[:devices], rest[devices]
    ranks, u_ref, basis, turned, stage, sems = rest[devices + 1 :]
    freqs, rows, _, cols, _, slots, tile = basis_far.shape
    total = slots + slots // 6
    half = u_ref.shape[2] // 2
    per = devices // parts
    me = lax.axis_index("tile")
    rank_copy = pltpu.make_async_copy(ranks_far, ranks, sems.at[0])
    data_copy = pltpu.make_async_copy(u_far, u_ref, sems.at[1])
    other_copy = pltpu.make_async_copy(other_far, other, sems.at[2])
    data_copy.start()
    rank_copy.start()
    copies = {}
    for i in range(rows):
        for p in range(parts):
            for f in range(freqs):
                at = pl.ds(p * per, per)
                copies[f, i, p] = pltpu.make_async_copy(
                    basis_far.at[f, i, at], basis.at[f, i, at], sems.at[3 + (f * rows + i) * parts + p]
                )
                copies[f, i, p].start()
    other_copy.start()
    data_copy.wait()
    for f in range(freqs):
        values = u_ref[f].astype(f32)
        lane = lax.broadcasted_iota(jnp.int32, values.shape, 1)
        rolled = pltpu.roll(values, half, 1)
        turned[f] = jnp.where(lane < half, rolled, -rolled).astype(bf16)
    waited = False
    for m in range(freqs // 2):
        for i in range(rows):
            here = pl.ds(i * tile, tile)
            for p in range(parts):
                pair = []
                at = pl.ds(p * per, per)
                for f in (2 * m, 2 * m + 1):
                    copies[f, i, p].wait()
                    both = side_by_side(basis[f, i, at, :, 0], basis[f, i, at, :, 1])
                    data = jnp.concatenate([u_ref[f, here, :], turned[f, here, :]], axis=0)
                    pair.append(dot(both, data, 1, 0))
                if not waited:
                    rank_copy.wait()
                    waited = True
                for n in range(per * cols):
                    col = p * per * cols + n
                    rank = ranks[2 * m, me * rows + i, col]
                    cut = slice(n * slots, (n + 1) * slots)
                    pack_rows(stage, m * devices * cols + col, i * total, rank, pair[0][cut], pair[1][cut])
        unstage(outs, stage, m, cols, rows * total, me)
    other_copy.wait()


def image_kernel(devices, owners, ranks_near, basis, *rest):
    packed = rest[:devices][::-1]
    outs = rest[-owners - 5 : -5]
    ranks, stage, coeffs, z, sem = rest[-5:]
    freqs, _, rows, cols, _, slots, tile = basis.shape
    total = slots + slots // 6
    half = coeffs.shape[3] // 2
    quarter = half // owners
    size = rows * total
    me, mine = lax.axis_index("tile"), lax.axis_index("freq")
    rank_copy = pltpu.make_async_copy(ranks_near, ranks, sem)
    rank_copy.start()
    for m in range(freqs // 2):
        for s in range(devices):
            for c in range(cols):
                block = packed[s][m, pl.ds(c * size, size), :]
                stage[(m * devices + s) * cols + c, pl.ds(0, size), :] = block.astype(f32)
    rank_copy.wait()
    for m in range(freqs // 2):
        for c in range(cols):
            for s in range(devices):
                for i in range(rows):
                    row = (me ^ s) * rows + i
                    rank = ranks[2 * m, row, me * cols + c]
                    slot = (m * devices + s) * cols + c
                    unpack_rows(stage, slot, i * total, rank, total, coeffs.at[c], row * slots)
            for n in range(2):
                f = 2 * m + n
                both = side_by_side(basis[f, :, :, c, 0], basis[f, :, :, c, 1])
                z[f, :, pl.ds(c * tile, tile)] = plain_product(coeffs[c, n], both)
    for r in range(owners):
        low = pl.multiple_of((mine ^ r) * quarter, quarter)
        for f in range(freqs):
            real = z[f, pl.ds(low, quarter), :]
            imag = z[f, pl.ds(half + low, quarter), :]
            outs[r][f] = jnp.concatenate([real, imag], axis=0).astype(bf16)


def window_kernel(mask, table, choice, same, high, low, full):
    exact = lax.Precision.HIGHEST
    full[...] = dot(mask[...].astype(f32), table[...], 0, 0, exact)
    quarter, side = same.shape
    mine = full[pl.ds(pl.multiple_of(lax.axis_index("freq") * quarter, quarter), quarter), :]
    entries = dot(mine[:, : choice.shape[0]], choice[...], 1, 0, exact)
    for n in range(side // quarter):
        block = entries[:, n * side : (n + 1) * side] * same[...]
        upper = block.astype(bf16)
        high[n * quarter : (n + 1) * quarter, :] = upper
        low[n * quarter : (n + 1) * quarter, :] = (block - upper.astype(f32)).astype(bf16)


def mix_kernel(owners, high, low, *rest):
    arrived = rest[:owners][::-1]
    outs = rest[owners : 2 * owners]
    z, w = rest[2 * owners :]
    freqs, rows, span = arrived[0].shape
    mine = lax.axis_index("freq")
    size = freqs * rows
    for r in range(owners):
        z[pl.ds(pl.multiple_of((mine ^ r) * size, 16), size), :] = arrived[r][...].reshape(size, span)
    w[...] = dot(high[...], z[...], 1, 0) + dot(low[...], z[...], 1, 0)
    for r in range(owners):
        block = w[pl.ds(pl.multiple_of((mine ^ r) * size, 16), size), :]
        outs[r][...] = block.reshape(freqs, rows, span).astype(bf16)


def forward_kernel(devices, owners, ranks_near, basis, *rest):
    arrived = rest[:owners][::-1]
    outs = rest[owners : owners + devices]
    ranks, w, stage, sem = rest[owners + devices :]
    freqs, _, rows, cols, _, slots, tile = basis.shape
    total = slots + slots // 6
    half = w.shape[2] // 2
    quarter = half // owners
    me, mine = lax.axis_index("tile"), lax.axis_index("freq")
    rank_copy = pltpu.make_async_copy(ranks_near, ranks, sem)
    rank_copy.start()
    for r in range(owners):
        low = pl.multiple_of((mine ^ r) * quarter, quarter)
        for f in range(freqs):
            for c in range(cols):
                at = slice(c * tile, (c + 1) * tile)
                real, imag = arrived[r][f, :quarter, at], arrived[r][f, quarter:, at]
                w[f, c, pl.ds(low, quarter), :tile] = real
                w[f, c, pl.ds(half + low, quarter), :tile] = imag
                w[f, c, pl.ds(low, quarter), tile:] = imag
                w[f, c, pl.ds(half + low, quarter), tile:] = -real
    rank_copy.wait()
    for m in range(freqs // 2):
        for c in range(cols):
            pair = []
            for f in (2 * m, 2 * m + 1):
                both = side_by_side(basis[f, :, :, c, 0], basis[f, :, :, c, 1])
                pair.append(dot(both, w[f, c], 1, 1))
            for d in range(devices):
                for i in range(rows):
                    rank = ranks[2 * m, d * rows + i, me * cols + c]
                    cut = slice((d * rows + i) * slots, (d * rows + i + 1) * slots)
                    slot = (m * devices + d) * cols + c
                    pack_rows(stage, slot, i * total, rank, pair[0][cut], pair[1][cut])
        unstage(outs, stage, m, cols, rows * total, me)


def result_kernel(devices, ranks_near, basis, *rest):
    packed = rest[:devices][::-1]
    out, ranks, stage, coeffs, sem = rest[devices:]
    freqs, rows, _, cols, _, slots, tile = basis.shape
    total = slots + slots // 6
    size = rows * total
    me = lax.axis_index("tile")
    rank_copy = pltpu.make_async_copy(ranks_near, ranks, sem)
    rank_copy.start()
    for m in range(freqs // 2):
        for s in range(devices):
            for c in range(cols):
                block = packed[s][m, pl.ds(c * size, size), :]
                stage[(m * devices + s) * cols + c, pl.ds(0, size), :] = block.astype(f32)
    rank_copy.wait()
    for m in range(freqs // 2):
        for i in range(rows):
            for s in range(devices):
                for c in range(cols):
                    col = (me ^ s) * cols + c
                    rank = ranks[2 * m, me * rows + i, col]
                    slot = (m * devices + s) * cols + c
                    unpack_rows(stage, slot, i * total, rank, total, coeffs.at[i], col * slots)
            for n in range(2):
                f = 2 * m + n
                both = side_by_side(basis[f, i, :, :, 0], basis[f, i, :, :, 1])
                r = plain_product(coeffs[i, n], both)
                out[f, pl.ds(i * tile, tile), :] = r.T.astype(bf16)


def send(value, axis, s):
    if s == 0:
        return value
    return lax.ppermute(value, axis, [(d, d ^ s) for d in range(lax.axis_size(axis))])


def spread(values, axis):
    return [(whole, send(values[s], axis, s)) for s in reversed(range(len(values)))]


def local(u_data, u_basis, v_basis, ranks, time_mask):
    freqs, row_count, width = u_data.shape
    rows, col_tiles, _, slots, tile = u_basis.shape[1:]
    row_tiles, cols = v_basis.shape[1:3]
    total = slots // 6 + slots
    pairs = freqs // 2
    devices = lax.axis_size("tile")
    owners = lax.axis_size("freq")
    stage_rows = rows * total + 2 * slots
    quarter = width // 2 // owners
    count = owners * freqs
    side = count * 2 * quarter
    by_cols = u_basis.reshape(freqs, rows, devices, cols, 2, slots, tile)
    by_rows = v_basis.reshape(freqs, devices, rows, cols, 2, slots, tile)
    per_device = [((pairs, cols * rows * total, width), bf16)] * devices
    per_owner = [((freqs, 2 * quarter, cols * tile), bf16)] * owners
    work = {"flops": 4 * row_count * slots * width * col_tiles * freqs * 2, "moved": u_basis.size * 2}
    ranks_here = pltpu.SMEM(ranks.shape, jnp.int32)
    stage = pltpu.VMEM((pairs * devices * cols, stage_rows, width), f32)
    one = pltpu.SemaphoreType.DMA

    table = lag_tables(count, time_mask.shape[0], 128)
    choice, same = lag_choice(count, quarter)
    window = call(
        window_kernel,
        "window",
        [(whole, jnp.asarray(x)) for x in (time_mask, table, choice, same)],
        [((side, side), bf16)] * 2,
        [pltpu.VMEM((width // 2, 128), f32)],
        flops=6 * quarter * 2 * count * 2 * count * side,
    )

    parts = math.gcd(devices, 2)
    *packed, near = call(
        functools.partial(adjoint_kernel, devices, parts),
        "adjoint",
        [(far, hold(x)) for x in (ranks, u_data, by_cols, by_rows)],
        per_device + [(by_rows.shape, bf16)],
        [
            ranks_here,
            pltpu.VMEM((freqs, row_count, width), bf16),
            pltpu.VMEM(by_cols.shape, bf16),
            pltpu.VMEM((freqs, row_count, width), bf16),
            stage,
            one((3 + freqs * rows * parts,)),
        ],
        **work,
    )
    images = call(
        functools.partial(image_kernel, devices, owners),
        "image",
        [(whole, ranks), (whole, near)] + spread(packed, "tile") + [(anywhere, window[0])],
        per_owner,
        [
            ranks_here,
            stage,
            pltpu.VMEM((cols, 2, row_tiles * slots, width), bf16),
            pltpu.VMEM((freqs, width, cols * tile), f32),
            one,
        ],
        **work,
    )
    mixed = call(
        functools.partial(mix_kernel, owners),
        "mix",
        [(whole, x) for x in window] + spread(images, "freq"),
        per_owner,
        [pltpu.VMEM((side, cols * tile), bf16), pltpu.VMEM((side, cols * tile), f32)],
        flops=4 * side * side * cols * tile,
    )
    packed = call(
        functools.partial(forward_kernel, devices, owners),
        "forward",
        [(whole, ranks), (whole, near)] + spread(mixed, "freq"),
        per_device,
        [ranks_here, pltpu.VMEM((freqs, cols, width, 2 * tile), bf16), stage, one],
        **work,
    )
    [out] = call(
        functools.partial(result_kernel, devices),
        "result",
        [(whole, ranks), (whole, by_cols)] + spread(packed, "tile"),
        [((freqs, row_count, width), bf16)],
        [ranks_here, stage, pltpu.VMEM((rows, 2, col_tiles * slots, width), bf16), one],
        **work,
    )
    return out


def solution(mesh):
    placed = (
        P("freq", "tile", None),
        P("freq", "tile", None, None, None, None),
        P("freq", None, "tile", None, None, None),
        P("freq", None, None),
        P(),
    )
    return jax.shard_map(
        local, mesh=mesh, in_specs=placed, out_specs=P("freq", "tile", None), check_vma=False
    )
```

```python
import functools
import math

import jax
import jax.numpy as jnp
import numpy as np
from jax import lax
from jax.experimental import pallas as pl
from jax.experimental.pallas import tpu as pltpu
from jax.sharding import PartitionSpec as P

vmem_limit = 48 * 1024 * 1024
bf16 = jnp.bfloat16
f32 = jnp.float32

whole = pl.BlockSpec(memory_space=pltpu.VMEM)
scalars = pl.BlockSpec(memory_space=pltpu.SMEM)
far = pl.BlockSpec(memory_space=pltpu.HBM)
anywhere = pl.BlockSpec(memory_space=pl.ANY)


def hold(value):
    return pltpu.with_memory_space_constraint(value, pltpu.HBM)


def call(kernel, name, ins, outs, scratch, flops=0, moved=0):
    specs = [spec for spec, _ in ins]
    shapes = [jax.ShapeDtypeStruct(shape, kind) for shape, kind in outs]
    return pl.pallas_call(
        kernel,
        in_specs=specs,
        out_specs=[whole] * len(outs),
        out_shape=shapes,
        scratch_shapes=scratch,
        compiler_params=pltpu.CompilerParams(vmem_limit_bytes=vmem_limit),
        cost_estimate=pl.CostEstimate(flops=flops, bytes_accessed=moved, transcendentals=0),
        name=name,
    )(*[value for _, value in ins])


def dot(lhs, rhs, lhs_dim, rhs_dim, precision=None):
    return lax.dot_general(
        lhs, rhs, (((lhs_dim,), (rhs_dim,)), ((), ())),
        precision=precision, preferred_element_type=f32,
    )


def lag_tables(count, time_count, lanes):
    samples = np.arange(time_count)[:, None]
    lags = np.arange(count)[None, :]
    angle = 2.0 * math.pi / time_count * ((samples * lags) % time_count)
    table = np.zeros((time_count, lanes), np.float32)
    table[:, :count] = np.cos(angle) / time_count
    table[:, count : 2 * count] = np.sin(angle) / time_count
    return table


def pack_rows(stage, slot, row, rank, first, second):
    size = first.shape[0]
    stage[slot, pl.ds(row, size), :] = first
    stage[slot, pl.ds(row + rank, size), :] = second


def unpack_rows(stage, slot, row, rank, total, coeffs, base):
    slots = total - total // 7
    first = stage[slot, pl.ds(row, slots), :]
    second = stage[slot, pl.ds(row + rank, slots), :]
    ids = lax.broadcasted_iota(jnp.int32, first.shape, 0)
    at = pl.ds(pl.multiple_of(base, 16), slots)
    coeffs[0, at, :] = jnp.where(ids < rank, first, 0.0).astype(bf16)
    coeffs[1, at, :] = jnp.where(ids < total - rank, second, 0.0).astype(bf16)


def side_by_side(real, imag):
    flat = (-1, real.shape[-1])
    return jnp.concatenate([real.reshape(flat), imag.reshape(flat)], axis=1)


def plain_product(coeffs, both):
    half, tile = coeffs.shape[1] // 2, both.shape[1] // 2
    product = dot(coeffs, both, 0, 0)
    lead, trail = product[:, :tile], product[:, tile:]
    return jnp.concatenate([lead[:half] - trail[half:], lead[half:] + trail[:half]], axis=0)


def unstage(outs, stage, m, span, size, me):
    for s in range(len(outs)):
        for c in range(span):
            block = stage[(m * len(outs) + (me ^ s)) * span + c, pl.ds(0, size), :]
            outs[s][m, pl.ds(c * size, size), :] = block.astype(bf16)


def adjoint_kernel(devices, parts, ranks_far, u_far, basis_far, other_far, *rest):
    outs, other = rest[:devices], rest[devices]
    ranks, u_ref, basis, turned, stage, sems = rest[devices + 1 :]
    freqs, rows, _, cols, _, slots, tile = basis_far.shape
    total = slots + slots // 6
    half = u_ref.shape[2] // 2
    per = devices // parts
    me = lax.axis_index("tile")
    rank_copy = pltpu.make_async_copy(ranks_far, ranks, sems.at[0])
    data_copy = pltpu.make_async_copy(u_far, u_ref, sems.at[1])
    other_copy = pltpu.make_async_copy(other_far, other, sems.at[2])
    data_copy.start()
    rank_copy.start()
    copies = {}
    for i in range(rows):
        for p in range(parts):
            for f in range(freqs):
                at = pl.ds(p * per, per)
                copies[f, i, p] = pltpu.make_async_copy(
                    basis_far.at[f, i, at], basis.at[f, i, at], sems.at[3 + (f * rows + i) * parts + p]
                )
                copies[f, i, p].start()
    other_copy.start()
    data_copy.wait()
    for f in range(freqs):
        values = u_ref[f].astype(f32)
        lane = lax.broadcasted_iota(jnp.int32, values.shape, 1)
        rolled = pltpu.roll(values, half, 1)
        turned[f] = jnp.where(lane < half, rolled, -rolled).astype(bf16)
    waited = False
    for m in range(freqs // 2):
        for i in range(rows):
            here = pl.ds(i * tile, tile)
            for p in range(parts):
                pair = []
                at = pl.ds(p * per, per)
                for f in (2 * m, 2 * m + 1):
                    copies[f, i, p].wait()
                    both = side_by_side(basis[f, i, at, :, 0], basis[f, i, at, :, 1])
                    data = jnp.concatenate([u_ref[f, here, :], turned[f, here, :]], axis=0)
                    pair.append(dot(both, data, 1, 0))
                if not waited:
                    rank_copy.wait()
                    waited = True
                for n in range(per * cols):
                    col = p * per * cols + n
                    rank = ranks[2 * m, me * rows + i, col]
                    cut = slice(n * slots, (n + 1) * slots)
                    pack_rows(stage, m * devices * cols + col, i * total, rank, pair[0][cut], pair[1][cut])
        unstage(outs, stage, m, cols, rows * total, me)
    other_copy.wait()


def image_kernel(devices, ranks_near, basis, *rest):
    packed = rest[:devices][::-1]
    out, ranks, stage, coeffs, sem = rest[-5:]
    freqs, _, rows, cols, _, slots, tile = basis.shape
    total = slots + slots // 6
    size = rows * total
    me = lax.axis_index("tile")
    rank_copy = pltpu.make_async_copy(ranks_near, ranks, sem)
    rank_copy.start()
    for m in range(freqs // 2):
        for s in range(devices):
            for c in range(cols):
                block = packed[s][m, pl.ds(c * size, size), :]
                stage[(m * devices + s) * cols + c, pl.ds(0, size), :] = block.astype(f32)
    rank_copy.wait()
    for m in range(freqs // 2):
        for c in range(cols):
            for s in range(devices):
                for i in range(rows):
                    row = (me ^ s) * rows + i
                    rank = ranks[2 * m, row, me * cols + c]
                    slot = (m * devices + s) * cols + c
                    unpack_rows(stage, slot, i * total, rank, total, coeffs.at[c], row * slots)
            for n in range(2):
                f = 2 * m + n
                both = side_by_side(basis[f, :, :, c, 0], basis[f, :, :, c, 1])
                out[f, :, pl.ds(c * tile, tile)] = plain_product(coeffs[c, n], both).astype(bf16)


def window_kernel(mask, table, out):
    lags = dot(mask[...].astype(f32), table[...], 0, 0, lax.Precision.HIGHEST)
    spans = out.shape[0] // 2
    count = (spans + 1) // 2
    for n in range(spans):
        lag = abs(n + 1 - count)
        sign = 1.0 if n + 1 >= count else -1.0
        out[n] = jnp.broadcast_to(lags[:, lag : lag + 1], out.shape[1:])
        out[spans + n] = sign * jnp.broadcast_to(lags[:, count + lag : count + lag + 1], out.shape[1:])


def forward_kernel(devices, ranks_near, basis, window, z, *rest):
    outs = rest[:devices]
    ranks, w, stage, sem = rest[devices:]
    freqs, _, rows, cols, _, slots, tile = basis.shape
    total = slots + slots // 6
    half = w.shape[2] // 2
    me, mine = lax.axis_index("tile"), lax.axis_index("freq")
    rank_copy = pltpu.make_async_copy(ranks_near, ranks, sem)
    rank_copy.start()
    count = z.shape[0]
    spans = window.shape[0] // 2
    step = window.shape[2]
    for f in range(freqs):
        first = count - 1 - (mine * freqs + f)
        for n in range(cols * tile // step):
            at = slice(n * step, (n + 1) * step)
            real = jnp.zeros((half, step), f32)
            imag = jnp.zeros((half, step), f32)
            for g in range(count):
                c, s = window[first + g], window[spans + first + g]
                zr, zi = z[g, :half, at].astype(f32), z[g, half:, at].astype(f32)
                real, imag = real + (c * zr - s * zi), imag + (c * zi + s * zr)
            col, low = n * step // tile, n * step % tile
            w[f, col, :half, low : low + step] = real.astype(bf16)
            w[f, col, half:, low : low + step] = imag.astype(bf16)
            w[f, col, :half, tile + low : tile + low + step] = imag.astype(bf16)
            w[f, col, half:, tile + low : tile + low + step] = (-real).astype(bf16)
    rank_copy.wait()
    for m in range(freqs // 2):
        for c in range(cols):
            pair = []
            for f in (2 * m, 2 * m + 1):
                both = side_by_side(basis[f, :, :, c, 0], basis[f, :, :, c, 1])
                pair.append(dot(both, w[f, c], 1, 1))
            for d in range(devices):
                for i in range(rows):
                    rank = ranks[2 * m, d * rows + i, me * cols + c]
                    cut = slice((d * rows + i) * slots, (d * rows + i + 1) * slots)
                    slot = (m * devices + d) * cols + c
                    pack_rows(stage, slot, i * total, rank, pair[0][cut], pair[1][cut])
        unstage(outs, stage, m, cols, rows * total, me)


def result_kernel(devices, ranks_near, basis, *rest):
    packed = rest[:devices][::-1]
    out, ranks, stage, coeffs, sem = rest[devices:]
    freqs, rows, _, cols, _, slots, tile = basis.shape
    total = slots + slots // 6
    size = rows * total
    me = lax.axis_index("tile")
    rank_copy = pltpu.make_async_copy(ranks_near, ranks, sem)
    rank_copy.start()
    for m in range(freqs // 2):
        for s in range(devices):
            for c in range(cols):
                block = packed[s][m, pl.ds(c * size, size), :]
                stage[(m * devices + s) * cols + c, pl.ds(0, size), :] = block.astype(f32)
    rank_copy.wait()
    for m in range(freqs // 2):
        for i in range(rows):
            for s in range(devices):
                for c in range(cols):
                    col = (me ^ s) * cols + c
                    rank = ranks[2 * m, me * rows + i, col]
                    slot = (m * devices + s) * cols + c
                    unpack_rows(stage, slot, i * total, rank, total, coeffs.at[i], col * slots)
            for n in range(2):
                f = 2 * m + n
                both = side_by_side(basis[f, i, :, :, 0], basis[f, i, :, :, 1])
                r = plain_product(coeffs[i, n], both)
                out[f, pl.ds(i * tile, tile), :] = r.T.astype(bf16)


def send(value, axis, s):
    if s == 0:
        return value
    return lax.ppermute(value, axis, [(d, d ^ s) for d in range(lax.axis_size(axis))])


def spread(values, axis):
    return [(whole, send(values[s], axis, s)) for s in reversed(range(len(values)))]


def local(u_data, u_basis, v_basis, ranks, time_mask):
    freqs, row_count, width = u_data.shape
    rows, col_tiles, _, slots, tile = u_basis.shape[1:]
    row_tiles, cols = v_basis.shape[1:3]
    total = slots // 6 + slots
    pairs = freqs // 2
    devices = lax.axis_size("tile")
    owners = lax.axis_size("freq")
    stage_rows = rows * total + 2 * slots
    count = owners * freqs
    by_cols = u_basis.reshape(freqs, rows, devices, cols, 2, slots, tile)
    by_rows = v_basis.reshape(freqs, devices, rows, cols, 2, slots, tile)
    per_device = [((pairs, cols * rows * total, width), bf16)] * devices
    work = {"flops": 4 * row_count * slots * width * col_tiles * freqs * 2, "moved": u_basis.size * 2}
    ranks_here = pltpu.SMEM(ranks.shape, jnp.int32)
    stage = pltpu.VMEM((pairs * devices * cols, stage_rows, width), f32)
    one = pltpu.SemaphoreType.DMA

    table = jnp.asarray(lag_tables(count, time_mask.shape[0], 128))
    [window] = call(
        window_kernel,
        "window",
        [(whole, time_mask), (whole, table)],
        [((4 * count - 2, width // 2, 128), f32)],
        [],
    )

    parts = math.gcd(devices, 2)
    *packed, near = call(
        functools.partial(adjoint_kernel, devices, parts),
        "adjoint",
        [(far, hold(x)) for x in (ranks, u_data, by_cols, by_rows)],
        per_device + [(by_rows.shape, bf16)],
        [
            ranks_here,
            pltpu.VMEM((freqs, row_count, width), bf16),
            pltpu.VMEM(by_cols.shape, bf16),
            pltpu.VMEM((freqs, row_count, width), bf16),
            stage,
            one((3 + freqs * rows * parts,)),
        ],
        **work,
    )
    [image] = call(
        functools.partial(image_kernel, devices),
        "image",
        [(whole, ranks), (whole, near)] + spread(packed, "tile") + [(anywhere, window)],
        [((freqs, width, cols * tile), bf16)],
        [ranks_here, stage, pltpu.VMEM((cols, 2, row_tiles * slots, width), bf16), one],
        **work,
    )
    images = lax.all_gather(image, "freq", axis=0, tiled=True)
    packed = call(
        functools.partial(forward_kernel, devices),
        "forward",
        [(whole, ranks), (whole, near), (whole, window), (whole, images)],
        per_device,
        [ranks_here, pltpu.VMEM((freqs, cols, width, 2 * tile), bf16), stage, one],
        **work,
    )
    [out] = call(
        functools.partial(result_kernel, devices),
        "result",
        [(whole, ranks), (whole, by_cols)] + spread(packed, "tile"),
        [((freqs, row_count, width), bf16)],
        [ranks_here, stage, pltpu.VMEM((rows, 2, col_tiles * slots, width), bf16), one],
        **work,
    )
    return out


def solution(mesh):
    placed = (
        P("freq", "tile", None),
        P("freq", "tile", None, None, None, None),
        P("freq", None, "tile", None, None, None),
        P("freq", None, None),
        P(),
    )
    return jax.shard_map(
        local, mesh=mesh, in_specs=placed, out_specs=P("freq", "tile", None), check_vma=False
    )
```

```python
import functools
import math

import jax
import jax.numpy as jnp
import numpy as np
from jax import lax
from jax.experimental import pallas as pl
from jax.experimental.pallas import tpu as pltpu
from jax.sharding import PartitionSpec as P

vmem_limit = 48 * 1024 * 1024
bf16 = jnp.bfloat16
f32 = jnp.float32

whole = pl.BlockSpec(memory_space=pltpu.VMEM)
scalars = pl.BlockSpec(memory_space=pltpu.SMEM)
far = pl.BlockSpec(memory_space=pltpu.HBM)
anywhere = pl.BlockSpec(memory_space=pl.ANY)


def hold(value):
    return pltpu.with_memory_space_constraint(value, pltpu.HBM)


def call(kernel, name, ins, outs, scratch, flops=0, moved=0):
    specs = [spec for spec, _ in ins]
    shapes = [jax.ShapeDtypeStruct(shape, kind) for shape, kind in outs]
    return pl.pallas_call(
        kernel,
        in_specs=specs,
        out_specs=[whole] * len(outs),
        out_shape=shapes,
        scratch_shapes=scratch,
        compiler_params=pltpu.CompilerParams(vmem_limit_bytes=vmem_limit),
        cost_estimate=pl.CostEstimate(flops=flops, bytes_accessed=moved, transcendentals=0),
        name=name,
    )(*[value for _, value in ins])


def dot(lhs, rhs, lhs_dim, rhs_dim, precision=None):
    return lax.dot_general(
        lhs, rhs, (((lhs_dim,), (rhs_dim,)), ((), ())),
        precision=precision, preferred_element_type=f32,
    )


def lag_tables(count, time_count, lanes):
    samples = np.arange(time_count)[:, None]
    lags = np.arange(count)[None, :]
    angle = 2.0 * math.pi / time_count * ((samples * lags) % time_count)
    table = np.zeros((time_count, lanes), np.float32)
    table[:, :count] = np.cos(angle) / time_count
    table[:, count : 2 * count] = np.sin(angle) / time_count
    return table


def lag_choice(count, quarter):
    side = count * 2 * quarter
    choice = np.zeros((2 * count, count, 2, count, 2, quarter), np.float32)
    for f in range(count):
        for g in range(count):
            sign = 1.0 if g >= f else -1.0
            lag = abs(g - f)
            choice[lag, f, 0, g, 0] = 1.0
            choice[lag, f, 1, g, 1] = 1.0
            choice[count + lag, f, 0, g, 1] = -sign
            choice[count + lag, f, 1, g, 0] = sign
    same = np.arange(quarter)[:, None] == np.arange(side)[None, :] % quarter
    return choice.reshape(2 * count, 2 * count * side), same.astype(np.float32)


def pack_rows(stage, slot, row, rank, first, second):
    size = first.shape[0]
    stage[slot, pl.ds(row, size), :] = first
    stage[slot, pl.ds(row + rank, size), :] = second


def unpack_rows(stage, slot, row, rank, total, coeffs, base):
    slots = total - total // 7
    first = stage[slot, pl.ds(row, slots), :]
    second = stage[slot, pl.ds(row + rank, slots), :]
    ids = lax.broadcasted_iota(jnp.int32, first.shape, 0)
    at = pl.ds(pl.multiple_of(base, 16), slots)
    coeffs[0, at, :] = jnp.where(ids < rank, first, 0.0).astype(bf16)
    coeffs[1, at, :] = jnp.where(ids < total - rank, second, 0.0).astype(bf16)


def side_by_side(real, imag):
    flat = (-1, real.shape[-1])
    return jnp.concatenate([real.reshape(flat), imag.reshape(flat)], axis=1)


def plain_product(coeffs, both):
    half, tile = coeffs.shape[1] // 2, both.shape[1] // 2
    product = dot(coeffs, both, 0, 0)
    lead, trail = product[:, :tile], product[:, tile:]
    return jnp.concatenate([lead[:half] - trail[half:], lead[half:] + trail[:half]], axis=0)


def split_blocks(devices):
    part = devices // 4
    return [(3 * part, part), (0, 2 * part), (2 * part, part)]


def block_base(me, block):
    first, size = block
    return (me ^ first) & ~(size - 1)


def unstage(outs, stage, m, slots, span, size, places):
    for out, place in zip(outs, places):
        for c in range(span):
            rows = stage[(m * slots + place) * span + c, pl.ds(0, size), :]
            out[m, pl.ds(c * size, size), :] = rows.astype(bf16)


def adjoint_kernel(blocks, bring, ranks_far, u_far, basis_far, other_far, *rest):
    partners = sum(size for _, size in blocks)
    ranks, u_ref, basis, turned, stage, sems = rest[-6:]
    outs = rest[-6 - partners - bring : -6 - bring]
    freqs, rows, _, cols, _, slots, tile = basis_far.shape
    total = slots + slots // 6
    half = u_ref.shape[2] // 2
    me = lax.axis_index("tile")
    rank_copy = pltpu.make_async_copy(ranks_far, ranks, sems.at[0])
    data_copy = pltpu.make_async_copy(u_far, u_ref, sems.at[1])
    data_copy.start()
    rank_copy.start()
    copies = {}
    at = 0
    for b, block in enumerate(blocks):
        for i in range(rows):
            for f in range(freqs):
                copies[b, i, f] = pltpu.make_async_copy(
                    basis_far.at[f, i, pl.ds(block_base(me, block), block[1])],
                    basis.at[f, i, pl.ds(at, block[1])],
                    sems.at[3 + (b * rows + i) * freqs + f],
                )
                copies[b, i, f].start()
        at += block[1]
    if bring:
        other_copy = pltpu.make_async_copy(other_far, rest[-7], sems.at[2])
        other_copy.start()
    data_copy.wait()
    for f in range(freqs):
        values = u_ref[f].astype(f32)
        lane = lax.broadcasted_iota(jnp.int32, values.shape, 1)
        rolled = pltpu.roll(values, half, 1)
        turned[f] = jnp.where(lane < half, rolled, -rolled).astype(bf16)
    rank_copy.wait()
    at = 0
    for b, block in enumerate(blocks):
        first, size = block
        base = block_base(me, block)
        for m in range(freqs // 2):
            for i in range(rows):
                here = pl.ds(i * tile, tile)
                pair = []
                for f in (2 * m, 2 * m + 1):
                    copies[b, i, f].wait()
                    both = side_by_side(basis[f, i, at : at + size, :, 0], basis[f, i, at : at + size, :, 1])
                    data = jnp.concatenate([u_ref[f, here, :], turned[f, here, :]], axis=0)
                    pair.append(dot(both, data, 1, 0))
                for n in range(size * cols):
                    rank = ranks[2 * m, me * rows + i, base * cols + n]
                    cut = slice(n * slots, (n + 1) * slots)
                    slot = (m * partners + at) * cols + n
                    pack_rows(stage, slot, i * total, rank, pair[0][cut], pair[1][cut])
            places = [at + ((me ^ (first + n)) & (size - 1)) for n in range(size)]
            unstage(outs[at : at + size], stage, m, partners, cols, rows * total, places)
        at += size
    if bring:
        other_copy.wait()


def image_kernel(block, owners, first, last, ranks_near, basis, *rest):
    packed, rest = rest[: block[1]][::-1], rest[block[1] :]
    if not first:
        before, rest = rest[0], rest[1:]
    ranks, stage, coeffs, z, sem = rest[-5:]
    freqs, _, rows, cols, _, slots, tile = basis.shape
    total = slots + slots // 6
    half = coeffs.shape[3] // 2
    quarter = half // owners
    size = rows * total
    start, count = block
    me, mine = lax.axis_index("tile"), lax.axis_index("freq")
    near = pl.ds(block_base(me, block), count)
    rank_copy = pltpu.make_async_copy(ranks_near, ranks, sem)
    rank_copy.start()
    for m in range(freqs // 2):
        for n in range(count):
            for c in range(cols):
                rows_in = packed[n][m, pl.ds(c * size, size), :]
                stage[(m * count + n) * cols + c, pl.ds(0, size), :] = rows_in.astype(f32)
    rank_copy.wait()
    for m in range(freqs // 2):
        for c in range(cols):
            for n in range(count):
                partner = me ^ (start + n)
                for i in range(rows):
                    rank = ranks[2 * m, partner * rows + i, me * cols + c]
                    slot = (m * count + n) * cols + c
                    place = ((partner & (count - 1)) * rows + i) * slots
                    unpack_rows(stage, slot, i * total, rank, total, coeffs.at[c], place)
            for n in range(2):
                f = 2 * m + n
                both = side_by_side(basis[f, near, :, c, 0], basis[f, near, :, c, 1])
                part = plain_product(coeffs[c, n], both)
                at = pl.ds(c * tile, tile)
                if not first:
                    part = part + before[f, :, at]
                if last:
                    z[f, :, at] = part
                else:
                    rest[-6][f, :, at] = part
    if last:
        outs = rest[-5 - owners : -5]
        for r in range(owners):
            low = pl.multiple_of((mine ^ r) * quarter, quarter)
            for f in range(freqs):
                real = z[f, pl.ds(low, quarter), :]
                imag = z[f, pl.ds(half + low, quarter), :]
                outs[r][f] = jnp.concatenate([real, imag], axis=0).astype(bf16)


def window_kernel(mask, table, choice, same, high, low, full):
    exact = lax.Precision.HIGHEST
    full[...] = dot(mask[...].astype(f32), table[...], 0, 0, exact)
    quarter, side = same.shape
    mine = full[pl.ds(pl.multiple_of(lax.axis_index("freq") * quarter, quarter), quarter), :]
    entries = dot(mine[:, : choice.shape[0]], choice[...], 1, 0, exact)
    for n in range(side // quarter):
        block = entries[:, n * side : (n + 1) * side] * same[...]
        upper = block.astype(bf16)
        high[n * quarter : (n + 1) * quarter, :] = upper
        low[n * quarter : (n + 1) * quarter, :] = (block - upper.astype(f32)).astype(bf16)


def mix_kernel(owners, high, low, *rest):
    arrived = rest[:owners][::-1]
    outs = rest[owners : 2 * owners]
    z, w = rest[2 * owners :]
    freqs, rows, span = arrived[0].shape
    mine = lax.axis_index("freq")
    size = freqs * rows
    for r in range(owners):
        z[pl.ds(pl.multiple_of((mine ^ r) * size, 16), size), :] = arrived[r][...].reshape(size, span)
    w[...] = dot(high[...], z[...], 1, 0) + dot(low[...], z[...], 1, 0)
    for r in range(owners):
        block = w[pl.ds(pl.multiple_of((mine ^ r) * size, 16), size), :]
        outs[r][...] = block.reshape(freqs, rows, span).astype(bf16)


def forward_kernel(blocks, owners, ranks_near, basis, *rest):
    partners = sum(size for _, size in blocks)
    ranks, stage, sem = rest[-3:]
    if owners:
        arrived = rest[:owners][::-1]
        outs, w = rest[-4 - partners : -4], rest[-4]
    else:
        outs, w = rest[-3 - partners : -3], rest[0]
    freqs, _, rows, cols, _, slots, tile = basis.shape
    total = slots + slots // 6
    half = w.shape[2] // 2
    me, mine = lax.axis_index("tile"), lax.axis_index("freq")
    rank_copy = pltpu.make_async_copy(ranks_near, ranks, sem)
    rank_copy.start()
    for r in range(owners):
        quarter = half // owners
        low = pl.multiple_of((mine ^ r) * quarter, quarter)
        for f in range(freqs):
            for c in range(cols):
                at = slice(c * tile, (c + 1) * tile)
                real, imag = arrived[r][f, :quarter, at], arrived[r][f, quarter:, at]
                w[f, c, pl.ds(low, quarter), :tile] = real
                w[f, c, pl.ds(half + low, quarter), :tile] = imag
                w[f, c, pl.ds(low, quarter), tile:] = imag
                w[f, c, pl.ds(half + low, quarter), tile:] = -real
    rank_copy.wait()
    at = 0
    for block in blocks:
        first, size = block
        base = block_base(me, block)
        near = pl.ds(base, size)
        for m in range(freqs // 2):
            for c in range(cols):
                pair = []
                for f in (2 * m, 2 * m + 1):
                    both = side_by_side(basis[f, near, :, c, 0], basis[f, near, :, c, 1])
                    pair.append(dot(both, w[f, c], 1, 1))
                for n in range(size):
                    for i in range(rows):
                        rank = ranks[2 * m, (base + n) * rows + i, me * cols + c]
                        cut = slice((n * rows + i) * slots, (n * rows + i + 1) * slots)
                        slot = (m * partners + at + n) * cols + c
                        pack_rows(stage, slot, i * total, rank, pair[0][cut], pair[1][cut])
            places = [at + ((me ^ (first + n)) & (size - 1)) for n in range(size)]
            unstage(outs[at : at + size], stage, m, partners, cols, rows * total, places)
        at += size


def result_kernel(block, first, last, ranks_near, basis, *rest):
    packed, rest = rest[: block[1]][::-1], rest[block[1] :]
    if not first:
        before, rest = rest[0], rest[1:]
    out, ranks, stage, coeffs, sem = rest
    freqs, rows, _, cols, _, slots, tile = basis.shape
    total = slots + slots // 6
    size = rows * total
    start, count = block
    me = lax.axis_index("tile")
    near = pl.ds(block_base(me, block), count)
    rank_copy = pltpu.make_async_copy(ranks_near, ranks, sem)
    rank_copy.start()
    for m in range(freqs // 2):
        for n in range(count):
            for c in range(cols):
                rows_in = packed[n][m, pl.ds(c * size, size), :]
                stage[(m * count + n) * cols + c, pl.ds(0, size), :] = rows_in.astype(f32)
    rank_copy.wait()
    for m in range(freqs // 2):
        for i in range(rows):
            for n in range(count):
                partner = me ^ (start + n)
                for c in range(cols):
                    rank = ranks[2 * m, me * rows + i, partner * cols + c]
                    slot = (m * count + n) * cols + c
                    place = ((partner & (count - 1)) * cols + c) * slots
                    unpack_rows(stage, slot, i * total, rank, total, coeffs.at[i], place)
            for n in range(2):
                f = 2 * m + n
                both = side_by_side(basis[f, i, near, :, 0], basis[f, i, near, :, 1])
                part = plain_product(coeffs[i, n], both)
                if not first:
                    part = part + before[f, i]
                if last:
                    out[f, pl.ds(i * tile, tile), :] = part.T.astype(bf16)
                else:
                    out[f, i] = part


def send(value, axis, s):
    if s == 0:
        return value
    return lax.ppermute(value, axis, [(d, d ^ s) for d in range(lax.axis_size(axis))])


def spread(values, axis, first=0):
    return [(whole, send(values[n], axis, first + n)) for n in reversed(range(len(values)))]


def local(u_data, u_basis, v_basis, ranks, time_mask):
    freqs, row_count, width = u_data.shape
    rows, col_tiles, _, slots, tile = u_basis.shape[1:]
    row_tiles, cols = v_basis.shape[1:3]
    total = slots // 6 + slots
    pairs = freqs // 2
    devices = lax.axis_size("tile")
    owners = lax.axis_size("freq")
    stage_rows = rows * total + 2 * slots
    quarter = width // 2 // owners
    count = owners * freqs
    side = count * 2 * quarter
    by_cols = u_basis.reshape(freqs, rows, devices, cols, 2, slots, tile)
    by_rows = v_basis.reshape(freqs, devices, rows, cols, 2, slots, tile)
    per_owner = [((freqs, 2 * quarter, cols * tile), bf16)] * owners
    work = {"flops": 4 * row_count * slots * width * col_tiles * freqs * 2, "moved": u_basis.size * 2}
    ranks_here = pltpu.SMEM(ranks.shape, jnp.int32)
    one = pltpu.SemaphoreType.DMA
    packed_kind = ((pairs, cols * rows * total, width), bf16)
    blocks = split_blocks(devices)

    def stage(partners):
        return pltpu.VMEM((pairs * partners * cols, stage_rows, width), f32)

    def share(partners):
        return {name: value * partners // devices for name, value in work.items()}

    table = lag_tables(count, time_mask.shape[0], 128)
    choice, same = lag_choice(count, quarter)
    window = call(
        window_kernel,
        "window",
        [(whole, jnp.asarray(x)) for x in (time_mask, table, choice, same)],
        [((side, side), bf16)] * 2,
        [pltpu.VMEM((width // 2, 128), f32)],
        flops=6 * quarter * 2 * count * 2 * count * side,
    )

    packed, after = {}, []
    for part in (blocks[:1], blocks[1:]):
        partners = sum(size for _, size in part)
        bring = len(part) > 1
        made = call(
            functools.partial(adjoint_kernel, part, int(bring)),
            "adjoint",
            [(far, hold(x)) for x in (ranks, u_data, by_cols, by_rows)] + after,
            [packed_kind] * partners + ([(by_rows.shape, bf16)] if bring else []),
            [
                ranks_here,
                pltpu.VMEM((freqs, row_count, width), bf16),
                pltpu.VMEM((freqs, rows, partners, cols, 2, slots, tile), bf16),
                pltpu.VMEM((freqs, row_count, width), bf16),
                stage(partners),
                one((3 + freqs * rows * len(part),)),
            ],
            **share(partners),
        )
        for block in part:
            packed[block], made = made[: block[1]], made[block[1] :]
        after = [(anywhere, packed[blocks[0]][0])]
    [near] = made
    images = []
    for n, block in enumerate(blocks):
        first, last = n == 0, n == len(blocks) - 1
        images = call(
            functools.partial(image_kernel, block, owners, first, last),
            "image",
            [(whole, ranks), (whole, near)]
            + spread(packed[block], "tile", block[0])
            + [(whole, x) for x in images]
            + ([(anywhere, window[0])] if first else []),
            per_owner if last else [((freqs, width, cols * tile), f32)],
            [
                ranks_here,
                stage(block[1]),
                pltpu.VMEM((cols, 2, block[1] * rows * slots, width), bf16),
                pltpu.VMEM((freqs, width, cols * tile), f32),
                one,
            ],
            **share(block[1]),
        )
    mixed = call(
        functools.partial(mix_kernel, owners),
        "mix",
        [(whole, x) for x in window] + spread(images, "freq"),
        per_owner,
        [pltpu.VMEM((side, cols * tile), bf16), pltpu.VMEM((side, cols * tile), f32)],
        flops=4 * side * side * cols * tile,
    )
    *made, w = call(
        functools.partial(forward_kernel, blocks[:1], owners),
        "forward",
        [(whole, ranks), (whole, near)] + spread(mixed, "freq"),
        [packed_kind] * blocks[0][1] + [((freqs, cols, width, 2 * tile), bf16)],
        [ranks_here, stage(blocks[0][1]), one],
        **share(blocks[0][1]),
    )
    partners = devices - blocks[0][1]
    made += call(
        functools.partial(forward_kernel, blocks[1:], 0),
        "forward",
        [(whole, ranks), (whole, near), (whole, w)],
        [packed_kind] * partners,
        [ranks_here, stage(partners), one],
        **share(partners),
    )
    out = []
    for n, block in enumerate(blocks):
        first, last = n == 0, n == len(blocks) - 1
        packed, made = made[: block[1]], made[block[1] :]
        out = call(
            functools.partial(result_kernel, block, first, last),
            "result",
            [(whole, ranks), (whole, by_cols)]
            + spread(packed, "tile", block[0])
            + [(whole, x) for x in out],
            [((freqs, row_count, width), bf16) if last else ((freqs, rows, width, tile), f32)],
            [
                ranks_here,
                stage(block[1]),
                pltpu.VMEM((rows, 2, block[1] * cols * slots, width), bf16),
                one,
            ],
            **share(block[1]),
        )
    return out[0]


def solution(mesh):
    placed = (
        P("freq", "tile", None),
        P("freq", "tile", None, None, None, None),
        P("freq", None, "tile", None, None, None),
        P("freq", None, None),
        P(),
    )
    return jax.shard_map(
        local, mesh=mesh, in_specs=placed, out_specs=P("freq", "tile", None), check_vma=False
    )
```

```python
import functools
import math

import jax
import jax.numpy as jnp
import numpy as np
from jax import lax
from jax.experimental import pallas as pl
from jax.experimental.pallas import tpu as pltpu
from jax.sharding import PartitionSpec as P

vmem_limit = 48 * 1024 * 1024
bf16 = jnp.bfloat16
f32 = jnp.float32

whole = pl.BlockSpec(memory_space=pltpu.VMEM)
scalars = pl.BlockSpec(memory_space=pltpu.SMEM)
far = pl.BlockSpec(memory_space=pltpu.HBM)
anywhere = pl.BlockSpec(memory_space=pl.ANY)


def hold(value):
    return pltpu.with_memory_space_constraint(value, pltpu.HBM)


def call(kernel, name, ins, outs, scratch, flops=0, moved=0, specs=None):
    shapes = [jax.ShapeDtypeStruct(shape, kind) for shape, kind in outs]
    return pl.pallas_call(
        kernel,
        in_specs=[spec for spec, _ in ins],
        out_specs=specs or [whole] * len(outs),
        out_shape=shapes,
        scratch_shapes=scratch,
        compiler_params=pltpu.CompilerParams(vmem_limit_bytes=vmem_limit),
        cost_estimate=pl.CostEstimate(flops=flops, bytes_accessed=moved, transcendentals=0),
        name=name,
    )(*[value for _, value in ins])


def dot(lhs, rhs, lhs_dim, rhs_dim, precision=None):
    return lax.dot_general(
        lhs, rhs, (((lhs_dim,), (rhs_dim,)), ((), ())),
        precision=precision, preferred_element_type=f32,
    )


def lag_tables(count, time_count, lanes):
    samples = np.arange(time_count)[:, None]
    lags = np.arange(count)[None, :]
    angle = 2.0 * math.pi / time_count * ((samples * lags) % time_count)
    table = np.zeros((time_count, lanes), np.float32)
    table[:, :count] = np.cos(angle) / time_count
    table[:, count : 2 * count] = np.sin(angle) / time_count
    return table


def lag_choice(count, quarter):
    side = count * 2 * quarter
    choice = np.zeros((2 * count, count, 2, count, 2, quarter), np.float32)
    for f in range(count):
        for g in range(count):
            sign = 1.0 if g >= f else -1.0
            lag = abs(g - f)
            choice[lag, f, 0, g, 0] = 1.0
            choice[lag, f, 1, g, 1] = 1.0
            choice[count + lag, f, 0, g, 1] = -sign
            choice[count + lag, f, 1, g, 0] = sign
    same = np.arange(quarter)[:, None] == np.arange(side)[None, :] % quarter
    return choice.reshape(2 * count, 2 * count * side), same.astype(np.float32)


def pack_rows(stage, slot, row, rank, first, second):
    size = first.shape[0]
    stage[slot, pl.ds(row, size), :] = first
    stage[slot, pl.ds(row + rank, size), :] = second


def unpack_rows(stage, slot, row, rank, total, coeffs, base):
    slots = total - total // 7
    first = stage[slot, pl.ds(row, slots), :]
    second = stage[slot, pl.ds(row + rank, slots), :]
    ids = lax.broadcasted_iota(jnp.int32, first.shape, 0)
    at = pl.ds(pl.multiple_of(base, 16), slots)
    coeffs[0, at, :] = jnp.where(ids < rank, first, 0.0).astype(bf16)
    coeffs[1, at, :] = jnp.where(ids < total - rank, second, 0.0).astype(bf16)


def side_by_side(real, imag):
    flat = (-1, real.shape[-1])
    return jnp.concatenate([real.reshape(flat), imag.reshape(flat)], axis=1)


def plain_product(coeffs, both):
    half, tile = coeffs.shape[1] // 2, both.shape[1] // 2
    product = dot(coeffs, both, 0, 0)
    lead, trail = product[:, :tile], product[:, tile:]
    return jnp.concatenate([lead[:half] - trail[half:], lead[half:] + trail[:half]], axis=0)


def unstage(outs, stage, m, span, size, me):
    for s in range(len(outs)):
        for c in range(span):
            block = stage[(m * len(outs) + (me ^ s)) * span + c, pl.ds(0, size), :]
            outs[s][m, pl.ds(c * size, size), :] = block.astype(bf16)


def adjoint_kernel(devices, parts, ranks_far, u_far, basis_far, *rest):
    outs = rest[:devices]
    ranks, u_ref, basis, turned, stage, sems = rest[devices:]
    freqs, rows, _, cols, _, slots, tile = basis_far.shape
    total = slots + slots // 6
    half = u_ref.shape[2] // 2
    per = devices // parts
    me = lax.axis_index("tile")
    rank_copy = pltpu.make_async_copy(ranks_far, ranks, sems.at[0])
    data_copy = pltpu.make_async_copy(u_far, u_ref, sems.at[1])
    data_copy.start()
    rank_copy.start()
    copies = {}
    for i in range(rows):
        for p in range(parts):
            for f in range(freqs):
                at = pl.ds(p * per, per)
                copies[f, i, p] = pltpu.make_async_copy(
                    basis_far.at[f, i, at], basis.at[f, i, at], sems.at[2 + (f * rows + i) * parts + p]
                )
                copies[f, i, p].start()
    data_copy.wait()
    for f in range(freqs):
        values = u_ref[f].astype(f32)
        lane = lax.broadcasted_iota(jnp.int32, values.shape, 1)
        rolled = pltpu.roll(values, half, 1)
        turned[f] = jnp.where(lane < half, rolled, -rolled).astype(bf16)
    waited = False
    for m in range(freqs // 2):
        for i in range(rows):
            here = pl.ds(i * tile, tile)
            for p in range(parts):
                pair = []
                at = pl.ds(p * per, per)
                for f in (2 * m, 2 * m + 1):
                    copies[f, i, p].wait()
                    both = side_by_side(basis[f, i, at, :, 0], basis[f, i, at, :, 1])
                    data = jnp.concatenate([u_ref[f, here, :], turned[f, here, :]], axis=0)
                    pair.append(dot(both, data, 1, 0))
                if not waited:
                    rank_copy.wait()
                    waited = True
                for n in range(per * cols):
                    col = p * per * cols + n
                    rank = ranks[2 * m, me * rows + i, col]
                    cut = slice(n * slots, (n + 1) * slots)
                    pack_rows(stage, m * devices * cols + col, i * total, rank, pair[0][cut], pair[1][cut])
        unstage(outs, stage, m, cols, rows * total, me)


def image_kernel(devices, owners, ranks_near, basis, *rest):
    packed = rest[:devices][::-1]
    outs = rest[-owners - 5 : -5]
    ranks, stage, coeffs, z, sem = rest[-5:]
    freqs, _, rows, cols, _, slots, tile = basis.shape
    total = slots + slots // 6
    half = coeffs.shape[3] // 2
    quarter = half // owners
    size = rows * total
    me, mine = lax.axis_index("tile"), lax.axis_index("freq")
    rank_copy = pltpu.make_async_copy(ranks_near, ranks, sem)
    rank_copy.start()
    for m in range(freqs // 2):
        for s in range(devices):
            for c in range(cols):
                block = packed[s][m, pl.ds(c * size, size), :]
                stage[(m * devices + s) * cols + c, pl.ds(0, size), :] = block.astype(f32)
    rank_copy.wait()
    for m in range(freqs // 2):
        for c in range(cols):
            for s in range(devices):
                for i in range(rows):
                    row = (me ^ s) * rows + i
                    rank = ranks[0, (m * devices * rows + row) * cols + c]
                    slot = (m * devices + s) * cols + c
                    unpack_rows(stage, slot, i * total, rank, total, coeffs.at[c], row * slots)
            for n in range(2):
                f = 2 * m + n
                both = side_by_side(basis[f, :, :, c, 0], basis[f, :, :, c, 1])
                z[f, :, pl.ds(c * tile, tile)] = plain_product(coeffs[c, n], both)
    for r in range(owners):
        low = pl.multiple_of((mine ^ r) * quarter, quarter)
        for f in range(freqs):
            real = z[f, pl.ds(low, quarter), :]
            imag = z[f, pl.ds(half + low, quarter), :]
            outs[r][f] = jnp.concatenate([real, imag], axis=0).astype(bf16)


def prepare_kernel(ranks_far, basis_far, mask, table, choice, same, *rest):
    basis, short, high, low, ranks, full, sems = rest[-7:]
    freqs, devices, rows, cols = basis_far.shape[:4]
    row_tiles, col_tiles = ranks.shape[1:]
    me = lax.axis_index("tile")
    basis_copy = pltpu.make_async_copy(basis_far, basis, sems.at[0])
    rank_copy = pltpu.make_async_copy(ranks_far, ranks, sems.at[1])
    rank_copy.start()
    basis_copy.start()
    exact = lax.Precision.HIGHEST
    full[...] = dot(mask[...].astype(f32), table[...], 0, 0, exact)
    quarter, side = same.shape
    mine = full[pl.ds(pl.multiple_of(lax.axis_index("freq") * quarter, quarter), quarter), :]
    entries = dot(mine[:, : choice.shape[0]], choice[...], 1, 0, exact)
    for n in range(side // quarter):
        block = entries[:, n * side : (n + 1) * side] * same[...]
        upper = block.astype(bf16)
        high[n * quarter : (n + 1) * quarter, :] = upper
        low[n * quarter : (n + 1) * quarter, :] = (block - upper.astype(f32)).astype(bf16)
    rank_copy.wait()
    at = 0
    for m in range(freqs // 2):
        for row in range(row_tiles):
            for c in range(cols):
                short[0, at] = ranks[2 * m, row, me * cols + c]
                at += 1
    for m in range(freqs // 2):
        for i in range(rows):
            for col in range(col_tiles):
                short[0, at] = ranks[2 * m, me * rows + i, col]
                at += 1
    basis_copy.wait()


def mix_kernel(owners, high, low, *rest):
    arrived = rest[:owners][::-1]
    outs = rest[owners : 2 * owners]
    z, w = rest[2 * owners :]
    freqs, rows, span = arrived[0].shape
    mine = lax.axis_index("freq")
    size = freqs * rows
    for r in range(owners):
        z[pl.ds(pl.multiple_of((mine ^ r) * size, 16), size), :] = arrived[r][...].reshape(size, span)
    w[...] = dot(high[...], z[...], 1, 0) + dot(low[...], z[...], 1, 0)
    for r in range(owners):
        block = w[pl.ds(pl.multiple_of((mine ^ r) * size, 16), size), :]
        outs[r][...] = block.reshape(freqs, rows, span).astype(bf16)


def forward_kernel(devices, owners, ranks_near, basis, *rest):
    arrived = rest[:owners][::-1]
    outs = rest[owners : owners + devices]
    ranks, w, stage, sem = rest[owners + devices :]
    freqs, _, rows, cols, _, slots, tile = basis.shape
    total = slots + slots // 6
    half = w.shape[2] // 2
    quarter = half // owners
    me, mine = lax.axis_index("tile"), lax.axis_index("freq")
    rank_copy = pltpu.make_async_copy(ranks_near, ranks, sem)
    rank_copy.start()
    for r in range(owners):
        low = pl.multiple_of((mine ^ r) * quarter, quarter)
        for f in range(freqs):
            for c in range(cols):
                at = slice(c * tile, (c + 1) * tile)
                real, imag = arrived[r][f, :quarter, at], arrived[r][f, quarter:, at]
                w[f, c, pl.ds(low, quarter), :tile] = real
                w[f, c, pl.ds(half + low, quarter), :tile] = imag
                w[f, c, pl.ds(low, quarter), tile:] = imag
                w[f, c, pl.ds(half + low, quarter), tile:] = -real
    rank_copy.wait()
    for m in range(freqs // 2):
        for c in range(cols):
            pair = []
            for f in (2 * m, 2 * m + 1):
                both = side_by_side(basis[f, :, :, c, 0], basis[f, :, :, c, 1])
                pair.append(dot(both, w[f, c], 1, 1))
            for d in range(devices):
                for i in range(rows):
                    rank = ranks[0, (m * devices * rows + d * rows + i) * cols + c]
                    cut = slice((d * rows + i) * slots, (d * rows + i + 1) * slots)
                    slot = (m * devices + d) * cols + c
                    pack_rows(stage, slot, i * total, rank, pair[0][cut], pair[1][cut])
        unstage(outs, stage, m, cols, rows * total, me)


def result_kernel(devices, ranks_near, basis, *rest):
    packed = rest[:devices][::-1]
    out, ranks, stage, coeffs, sem = rest[devices:]
    freqs, rows, _, cols, _, slots, tile = basis.shape
    total = slots + slots // 6
    size = rows * total
    before = freqs // 2 * devices * rows * cols
    me = lax.axis_index("tile")
    rank_copy = pltpu.make_async_copy(ranks_near, ranks, sem)
    rank_copy.start()
    for m in range(freqs // 2):
        for s in range(devices):
            for c in range(cols):
                block = packed[s][m, pl.ds(c * size, size), :]
                stage[(m * devices + s) * cols + c, pl.ds(0, size), :] = block.astype(f32)
    rank_copy.wait()
    for m in range(freqs // 2):
        for i in range(rows):
            for s in range(devices):
                for c in range(cols):
                    col = (me ^ s) * cols + c
                    rank = ranks[0, before + (m * rows + i) * devices * cols + col]
                    slot = (m * devices + s) * cols + c
                    unpack_rows(stage, slot, i * total, rank, total, coeffs.at[i], col * slots)
            for n in range(2):
                f = 2 * m + n
                both = side_by_side(basis[f, i, :, :, 0], basis[f, i, :, :, 1])
                r = plain_product(coeffs[i, n], both)
                out[f, pl.ds(i * tile, tile), :] = r.T.astype(bf16)


def send(value, axis, s):
    if s == 0:
        return value
    return lax.ppermute(value, axis, [(d, d ^ s) for d in range(lax.axis_size(axis))])


def spread(values, axis):
    return [(whole, send(values[s], axis, s)) for s in reversed(range(len(values)))]


def local(u_data, u_basis, v_basis, ranks, time_mask):
    freqs, row_count, width = u_data.shape
    rows, col_tiles, _, slots, tile = u_basis.shape[1:]
    row_tiles, cols = v_basis.shape[1:3]
    total = slots // 6 + slots
    pairs = freqs // 2
    devices = lax.axis_size("tile")
    owners = lax.axis_size("freq")
    stage_rows = rows * total + 2 * slots
    quarter = width // 2 // owners
    count = owners * freqs
    side = count * 2 * quarter
    by_cols = u_basis.reshape(freqs, rows, devices, cols, 2, slots, tile)
    by_rows = v_basis.reshape(freqs, devices, rows, cols, 2, slots, tile)
    per_device = [((pairs, cols * rows * total, width), bf16)] * devices
    per_owner = [((freqs, 2 * quarter, cols * tile), bf16)] * owners
    work = {"flops": 4 * row_count * slots * width * col_tiles * freqs * 2, "moved": u_basis.size * 2}
    count_short = pairs * (row_tiles * cols + rows * col_tiles)
    ranks_here = pltpu.SMEM((1, count_short), jnp.int32)
    stage = pltpu.VMEM((pairs * devices * cols, stage_rows, width), f32)
    one = pltpu.SemaphoreType.DMA

    table = lag_tables(count, time_mask.shape[0], 128)
    choice, same = lag_choice(count, quarter)
    parts = math.gcd(devices, 2)
    packed = call(
        functools.partial(adjoint_kernel, devices, parts),
        "adjoint",
        [(far, hold(x)) for x in (ranks, u_data, by_cols)],
        per_device,
        [
            pltpu.SMEM(ranks.shape, jnp.int32),
            pltpu.VMEM((freqs, row_count, width), bf16),
            pltpu.VMEM(by_cols.shape, bf16),
            pltpu.VMEM((freqs, row_count, width), bf16),
            stage,
            one((2 + freqs * rows * parts,)),
        ],
        **work,
    )
    near, short, *window = call(
        prepare_kernel,
        "prepare",
        [(far, hold(ranks)), (far, hold(by_rows))]
        + [(whole, jnp.asarray(x)) for x in (time_mask, table, choice, same)]
        + [(anywhere, packed[0])],
        [(by_rows.shape, bf16), ((1, count_short), jnp.int32)] + [((side, side), bf16)] * 2,
        [pltpu.SMEM(ranks.shape, jnp.int32), pltpu.VMEM((width // 2, 128), f32), one((2,))],
        specs=[whole, scalars, whole, whole],
        moved=u_basis.size * 2,
    )
    images = call(
        functools.partial(image_kernel, devices, owners),
        "image",
        [(whole, short), (whole, near)] + spread(packed, "tile"),
        per_owner,
        [
            ranks_here,
            stage,
            pltpu.VMEM((cols, 2, row_tiles * slots, width), bf16),
            pltpu.VMEM((freqs, width, cols * tile), f32),
            one,
        ],
        **work,
    )
    mixed = call(
        functools.partial(mix_kernel, owners),
        "mix",
        [(whole, x) for x in window] + spread(images, "freq"),
        per_owner,
        [pltpu.VMEM((side, cols * tile), bf16), pltpu.VMEM((side, cols * tile), f32)],
        flops=4 * side * side * cols * tile,
    )
    packed = call(
        functools.partial(forward_kernel, devices, owners),
        "forward",
        [(whole, short), (whole, near)] + spread(mixed, "freq"),
        per_device,
        [ranks_here, pltpu.VMEM((freqs, cols, width, 2 * tile), bf16), stage, one],
        **work,
    )
    [out] = call(
        functools.partial(result_kernel, devices),
        "result",
        [(whole, short), (whole, by_cols)] + spread(packed, "tile"),
        [((freqs, row_count, width), bf16)],
        [ranks_here, stage, pltpu.VMEM((rows, 2, col_tiles * slots, width), bf16), one],
        **work,
    )
    return out


def solution(mesh):
    placed = (
        P("freq", "tile", None),
        P("freq", "tile", None, None, None, None),
        P("freq", None, "tile", None, None, None),
        P("freq", None, None),
        P(),
    )
    return jax.shard_map(
        local, mesh=mesh, in_specs=placed, out_specs=P("freq", "tile", None), check_vma=False
    )
```

```python
import functools
import math

import jax
import jax.numpy as jnp
import numpy as np
from jax import lax
from jax.experimental import pallas as pl
from jax.experimental.pallas import tpu as pltpu
from jax.sharding import PartitionSpec as P

vmem_limit = 48 * 1024 * 1024
bf16 = jnp.bfloat16
f32 = jnp.float32

whole = pl.BlockSpec(memory_space=pltpu.VMEM)
scalars = pl.BlockSpec(memory_space=pltpu.SMEM)
far = pl.BlockSpec(memory_space=pltpu.HBM)
anywhere = pl.BlockSpec(memory_space=pl.ANY)


def hold(value):
    return pltpu.with_memory_space_constraint(value, pltpu.HBM)


def call(kernel, name, ins, outs, scratch, flops=0, moved=0, specs=None):
    shapes = [jax.ShapeDtypeStruct(shape, kind) for shape, kind in outs]
    return pl.pallas_call(
        kernel,
        in_specs=[spec for spec, _ in ins],
        out_specs=specs or [whole] * len(outs),
        out_shape=shapes,
        scratch_shapes=scratch,
        compiler_params=pltpu.CompilerParams(vmem_limit_bytes=vmem_limit),
        cost_estimate=pl.CostEstimate(flops=flops, bytes_accessed=moved, transcendentals=0),
        name=name,
    )(*[value for _, value in ins])


def dot(lhs, rhs, lhs_dim, rhs_dim, precision=None):
    return lax.dot_general(
        lhs, rhs, (((lhs_dim,), (rhs_dim,)), ((), ())),
        precision=precision, preferred_element_type=f32,
    )


def lag_tables(count, time_count, lanes):
    samples = np.arange(time_count)[:, None]
    lags = np.arange(count)[None, :]
    angle = 2.0 * math.pi / time_count * ((samples * lags) % time_count)
    table = np.zeros((time_count, lanes), np.float32)
    table[:, :count] = np.cos(angle) / time_count
    table[:, count : 2 * count] = np.sin(angle) / time_count
    return table


def lag_choice(count, quarter):
    side = count * 2 * quarter
    choice = np.zeros((2 * count, count, 2, count, 2, quarter), np.float32)
    for f in range(count):
        for g in range(count):
            sign = 1.0 if g >= f else -1.0
            lag = abs(g - f)
            choice[lag, f, 0, g, 0] = 1.0
            choice[lag, f, 1, g, 1] = 1.0
            choice[count + lag, f, 0, g, 1] = -sign
            choice[count + lag, f, 1, g, 0] = sign
    same = np.arange(quarter)[:, None] == np.arange(side)[None, :] % quarter
    return choice.reshape(2 * count, 2 * count * side), same.astype(np.float32)


def pack_rows(stage, slot, row, rank, first, second):
    size = first.shape[0]
    stage[slot, pl.ds(row, size), :] = first
    stage[slot, pl.ds(row + rank, size), :] = second


def unpack_rows(stage, slot, row, rank, total, coeffs, base):
    slots = total - total // 7
    first = stage[slot, pl.ds(row, slots), :]
    second = stage[slot, pl.ds(row + rank, slots), :]
    ids = lax.broadcasted_iota(jnp.int32, first.shape, 0)
    at = pl.ds(pl.multiple_of(base, 16), slots)
    coeffs[0, at, :] = jnp.where(ids < rank, first, 0.0).astype(bf16)
    coeffs[1, at, :] = jnp.where(ids < total - rank, second, 0.0).astype(bf16)


def side_by_side(real, imag):
    flat = (-1, real.shape[-1])
    return jnp.concatenate([real.reshape(flat), imag.reshape(flat)], axis=1)


def plain_product(coeffs, both):
    half, tile = coeffs.shape[1] // 2, both.shape[1] // 2
    product = dot(coeffs, both, 0, 0)
    lead, trail = product[:, :tile], product[:, tile:]
    return jnp.concatenate([lead[:half] - trail[half:], lead[half:] + trail[:half]], axis=0)


def unstage(outs, stage, m, span, size, me):
    for s in range(len(outs)):
        for c in range(span):
            block = stage[(m * len(outs) + (me ^ s)) * span + c, pl.ds(0, size), :]
            outs[s][m, pl.ds(c * size, size), :] = block.astype(bf16)


def adjoint_kernel(devices, parts, ranks_far, u_far, basis_far, *rest):
    outs = rest[:devices]
    ranks, u_ref, basis, turned, stage, sems = rest[devices:]
    freqs, rows, _, cols, _, slots, tile = basis_far.shape
    total = slots + slots // 6
    half = u_ref.shape[2] // 2
    per = devices // parts
    me = lax.axis_index("tile")
    rank_copy = pltpu.make_async_copy(ranks_far, ranks, sems.at[0])
    data_copy = pltpu.make_async_copy(u_far, u_ref, sems.at[1])
    data_copy.start()
    rank_copy.start()
    copies = {}
    for i in range(rows):
        for p in range(parts):
            for f in range(freqs):
                at = pl.ds(p * per, per)
                copies[f, i, p] = pltpu.make_async_copy(
                    basis_far.at[f, i, at], basis.at[f, i, at], sems.at[2 + (f * rows + i) * parts + p]
                )
                copies[f, i, p].start(priority=(p + f) % 2)
    data_copy.wait()
    for f in range(freqs):
        for i in range(rows):
            values = u_ref[f, i * tile : (i + 1) * tile, :]
            wide = values.astype(f32)
            lane = lax.broadcasted_iota(jnp.int32, wide.shape, 1)
            rolled = pltpu.roll(wide, half, 1)
            turned[f, i, :tile, :] = values
            turned[f, i, tile:, :] = jnp.where(lane < half, rolled, -rolled).astype(bf16)
    waited = False
    for m in range(freqs // 2):
        for i in range(rows):
            for p in range(parts):
                pair = []
                at = pl.ds(p * per, per)
                for f in (2 * m, 2 * m + 1):
                    copies[f, i, p].wait()
                    both = side_by_side(basis[f, i, at, :, 0], basis[f, i, at, :, 1])
                    pair.append(dot(both, turned[f, i], 1, 0))
                if not waited:
                    rank_copy.wait()
                    waited = True
                for n in range(per * cols):
                    col = p * per * cols + n
                    rank = ranks[2 * m, me * rows + i, col]
                    cut = slice(n * slots, (n + 1) * slots)
                    pack_rows(stage, m * devices * cols + col, i * total, rank, pair[0][cut], pair[1][cut])
        unstage(outs, stage, m, cols, rows * total, me)


def image_kernel(devices, owners, ranks_near, basis, *rest):
    packed = rest[:devices][::-1]
    outs = rest[-owners - 5 : -5]
    ranks, stage, coeffs, z, sem = rest[-5:]
    freqs, _, rows, cols, _, slots, tile = basis.shape
    total = slots + slots // 6
    half = coeffs.shape[3] // 2
    quarter = half // owners
    size = rows * total
    me, mine = lax.axis_index("tile"), lax.axis_index("freq")
    rank_copy = pltpu.make_async_copy(ranks_near, ranks, sem)
    rank_copy.start()
    for m in range(freqs // 2):
        for s in range(devices):
            for c in range(cols):
                block = packed[s][m, pl.ds(c * size, size), :]
                stage[(m * devices + s) * cols + c, pl.ds(0, size), :] = block.astype(f32)
    rank_copy.wait()
    for m in range(freqs // 2):
        for c in range(cols):
            for s in range(devices):
                for i in range(rows):
                    row = (me ^ s) * rows + i
                    rank = ranks[0, (m * devices * rows + row) * cols + c]
                    slot = (m * devices + s) * cols + c
                    unpack_rows(stage, slot, i * total, rank, total, coeffs.at[c], row * slots)
            for n in range(2):
                f = 2 * m + n
                both = side_by_side(basis[f, :, :, c, 0], basis[f, :, :, c, 1])
                z[f, :, pl.ds(c * tile, tile)] = plain_product(coeffs[c, n], both)
    for r in range(owners):
        low = pl.multiple_of((mine ^ r) * quarter, quarter)
        for f in range(freqs):
            real = z[f, pl.ds(low, quarter), :]
            imag = z[f, pl.ds(half + low, quarter), :]
            outs[r][f] = jnp.concatenate([real, imag], axis=0).astype(bf16)


def prepare_kernel(ranks_far, basis_far, mask, table, choice, same, *rest):
    basis, short, high, low, ranks, full, sems = rest[-7:]
    freqs, devices, rows, cols = basis_far.shape[:4]
    row_tiles, col_tiles = ranks.shape[1:]
    me = lax.axis_index("tile")
    rank_copy = pltpu.make_async_copy(ranks_far, ranks, sems.at[freqs * devices])
    rank_copy.start()
    basis_copies = []
    for f in range(freqs):
        for d in range(devices):
            n = f * devices + d
            basis_copies.append(pltpu.make_async_copy(basis_far.at[f, d], basis.at[f, d], sems.at[n]))
            basis_copies[n].start(priority=n % 2)
    exact = lax.Precision.HIGHEST
    full[...] = dot(mask[...].astype(f32), table[...], 0, 0, exact)
    quarter, side = same.shape
    mine = full[pl.ds(pl.multiple_of(lax.axis_index("freq") * quarter, quarter), quarter), :]
    entries = dot(mine[:, : choice.shape[0]], choice[...], 1, 0, exact)
    for n in range(side // quarter):
        block = entries[:, n * side : (n + 1) * side] * same[...]
        upper = block.astype(bf16)
        high[n * quarter : (n + 1) * quarter, :] = upper
        low[n * quarter : (n + 1) * quarter, :] = (block - upper.astype(f32)).astype(bf16)
    rank_copy.wait()
    at = 0
    for m in range(freqs // 2):
        for row in range(row_tiles):
            for c in range(cols):
                short[0, at] = ranks[2 * m, row, me * cols + c]
                at += 1
    for m in range(freqs // 2):
        for i in range(rows):
            for col in range(col_tiles):
                short[0, at] = ranks[2 * m, me * rows + i, col]
                at += 1
    for copy in basis_copies:
        copy.wait()


def mix_kernel(owners, high, low, *rest):
    arrived = rest[:owners][::-1]
    outs = rest[owners : 2 * owners]
    z, w = rest[2 * owners :]
    freqs, rows, span = arrived[0].shape
    mine = lax.axis_index("freq")
    size = freqs * rows
    for r in range(owners):
        z[pl.ds(pl.multiple_of((mine ^ r) * size, 16), size), :] = arrived[r][...].reshape(size, span)
    w[...] = dot(high[...], z[...], 1, 0) + dot(low[...], z[...], 1, 0)
    for r in range(owners):
        block = w[pl.ds(pl.multiple_of((mine ^ r) * size, 16), size), :]
        outs[r][...] = block.reshape(freqs, rows, span).astype(bf16)


def forward_kernel(devices, owners, ranks_near, basis, *rest):
    arrived = rest[:owners][::-1]
    outs = rest[owners : owners + devices]
    ranks, w, stage, sem = rest[owners + devices :]
    freqs, _, rows, cols, _, slots, tile = basis.shape
    total = slots + slots // 6
    half = w.shape[2] // 2
    quarter = half // owners
    me, mine = lax.axis_index("tile"), lax.axis_index("freq")
    rank_copy = pltpu.make_async_copy(ranks_near, ranks, sem)
    rank_copy.start()
    for r in range(owners):
        low = pl.multiple_of((mine ^ r) * quarter, quarter)
        for f in range(freqs):
            for c in range(cols):
                at = slice(c * tile, (c + 1) * tile)
                real, imag = arrived[r][f, :quarter, at], arrived[r][f, quarter:, at]
                w[f, c, pl.ds(low, quarter), :tile] = real
                w[f, c, pl.ds(half + low, quarter), :tile] = imag
                w[f, c, pl.ds(low, quarter), tile:] = imag
                w[f, c, pl.ds(half + low, quarter), tile:] = -real
    rank_copy.wait()
    for m in range(freqs // 2):
        for c in range(cols):
            pair = []
            for f in (2 * m, 2 * m + 1):
                both = side_by_side(basis[f, :, :, c, 0], basis[f, :, :, c, 1])
                pair.append(dot(both, w[f, c], 1, 1))
            for d in range(devices):
                for i in range(rows):
                    rank = ranks[0, (m * devices * rows + d * rows + i) * cols + c]
                    cut = slice((d * rows + i) * slots, (d * rows + i + 1) * slots)
                    slot = (m * devices + d) * cols + c
                    pack_rows(stage, slot, i * total, rank, pair[0][cut], pair[1][cut])
        unstage(outs, stage, m, cols, rows * total, me)


def result_kernel(devices, ranks_near, basis, *rest):
    packed = rest[:devices][::-1]
    out, ranks, stage, coeffs, sem = rest[devices:]
    freqs, rows, _, cols, _, slots, tile = basis.shape
    total = slots + slots // 6
    size = rows * total
    before = freqs // 2 * devices * rows * cols
    me = lax.axis_index("tile")
    rank_copy = pltpu.make_async_copy(ranks_near, ranks, sem)
    rank_copy.start()
    for m in range(freqs // 2):
        for s in range(devices):
            for c in range(cols):
                block = packed[s][m, pl.ds(c * size, size), :]
                stage[(m * devices + s) * cols + c, pl.ds(0, size), :] = block.astype(f32)
    rank_copy.wait()
    for m in range(freqs // 2):
        for i in range(rows):
            for s in range(devices):
                for c in range(cols):
                    col = (me ^ s) * cols + c
                    rank = ranks[0, before + (m * rows + i) * devices * cols + col]
                    slot = (m * devices + s) * cols + c
                    unpack_rows(stage, slot, i * total, rank, total, coeffs.at[i], col * slots)
            for n in range(2):
                f = 2 * m + n
                both = side_by_side(basis[f, i, :, :, 0], basis[f, i, :, :, 1])
                r = plain_product(coeffs[i, n], both)
                out[f, pl.ds(i * tile, tile), :] = r.T.astype(bf16)


def send(value, axis, s):
    if s == 0:
        return value
    return lax.ppermute(value, axis, [(d, d ^ s) for d in range(lax.axis_size(axis))])


def spread(values, axis):
    return [(whole, send(values[s], axis, s)) for s in reversed(range(len(values)))]


def local(u_data, u_basis, v_basis, ranks, time_mask):
    freqs, row_count, width = u_data.shape
    rows, col_tiles, _, slots, tile = u_basis.shape[1:]
    row_tiles, cols = v_basis.shape[1:3]
    total = slots // 6 + slots
    pairs = freqs // 2
    devices = lax.axis_size("tile")
    owners = lax.axis_size("freq")
    stage_rows = rows * total + 2 * slots
    quarter = width // 2 // owners
    count = owners * freqs
    side = count * 2 * quarter
    by_cols = u_basis.reshape(freqs, rows, devices, cols, 2, slots, tile)
    by_rows = v_basis.reshape(freqs, devices, rows, cols, 2, slots, tile)
    per_device = [((pairs, cols * rows * total, width), bf16)] * devices
    per_owner = [((freqs, 2 * quarter, cols * tile), bf16)] * owners
    work = {"flops": 4 * row_count * slots * width * col_tiles * freqs * 2, "moved": u_basis.size * 2}
    count_short = pairs * (row_tiles * cols + rows * col_tiles)
    ranks_here = pltpu.SMEM((1, count_short), jnp.int32)
    stage = pltpu.VMEM((pairs * devices * cols, stage_rows, width), f32)
    one = pltpu.SemaphoreType.DMA

    table = lag_tables(count, time_mask.shape[0], 128)
    choice, same = lag_choice(count, quarter)
    parts = math.gcd(devices, 4)
    packed = call(
        functools.partial(adjoint_kernel, devices, parts),
        "adjoint",
        [(far, hold(x)) for x in (ranks, u_data, by_cols)],
        per_device,
        [
            pltpu.SMEM(ranks.shape, jnp.int32),
            pltpu.VMEM((freqs, row_count, width), bf16),
            pltpu.VMEM(by_cols.shape, bf16),
            pltpu.VMEM((freqs, rows, 2 * tile, width), bf16),
            stage,
            one((2 + freqs * rows * parts,)),
        ],
        **work,
    )
    near, short, *window = call(
        prepare_kernel,
        "prepare",
        [(far, hold(ranks)), (far, hold(by_rows))]
        + [(whole, jnp.asarray(x)) for x in (time_mask, table, choice, same)]
        + [(anywhere, packed[0])],
        [(by_rows.shape, bf16), ((1, count_short), jnp.int32)] + [((side, side), bf16)] * 2,
        [pltpu.SMEM(ranks.shape, jnp.int32), pltpu.VMEM((width // 2, 128), f32), one((freqs * devices + 1,))],
        specs=[whole, scalars, whole, whole],
        moved=u_basis.size * 2,
    )
    images = call(
        functools.partial(image_kernel, devices, owners),
        "image",
        [(whole, short), (whole, near)] + spread(packed, "tile"),
        per_owner,
        [
            ranks_here,
            stage,
            pltpu.VMEM((cols, 2, row_tiles * slots, width), bf16),
            pltpu.VMEM((freqs, width, cols * tile), f32),
            one,
        ],
        **work,
    )
    mixed = call(
        functools.partial(mix_kernel, owners),
        "mix",
        [(whole, x) for x in window] + spread(images, "freq"),
        per_owner,
        [pltpu.VMEM((side, cols * tile), bf16), pltpu.VMEM((side, cols * tile), f32)],
        flops=4 * side * side * cols * tile,
    )
    packed = call(
        functools.partial(forward_kernel, devices, owners),
        "forward",
        [(whole, short), (whole, near)] + spread(mixed, "freq"),
        per_device,
        [ranks_here, pltpu.VMEM((freqs, cols, width, 2 * tile), bf16), stage, one],
        **work,
    )
    [out] = call(
        functools.partial(result_kernel, devices),
        "result",
        [(whole, short), (whole, by_cols)] + spread(packed, "tile"),
        [((freqs, row_count, width), bf16)],
        [ranks_here, stage, pltpu.VMEM((rows, 2, col_tiles * slots, width), bf16), one],
        **work,
    )
    return out


def solution(mesh):
    placed = (
        P("freq", "tile", None),
        P("freq", "tile", None, None, None, None),
        P("freq", None, "tile", None, None, None),
        P("freq", None, None),
        P(),
    )
    return jax.shard_map(
        local, mesh=mesh, in_specs=placed, out_specs=P("freq", "tile", None), check_vma=False
    )
```

```python
import functools
import math

import jax
import jax.numpy as jnp
import numpy as np
from jax import lax
from jax.experimental import pallas as pl
from jax.experimental.pallas import tpu as pltpu
from jax.sharding import PartitionSpec as P

vmem_limit = 48 * 1024 * 1024
bf16 = jnp.bfloat16
f32 = jnp.float32

whole = pl.BlockSpec(memory_space=pltpu.VMEM)
scalars = pl.BlockSpec(memory_space=pltpu.SMEM)
far = pl.BlockSpec(memory_space=pltpu.HBM)
anywhere = pl.BlockSpec(memory_space=pl.ANY)


def hold(value):
    return pltpu.with_memory_space_constraint(value, pltpu.HBM)


def call(kernel, name, ins, outs, scratch, flops=0, moved=0, specs=None):
    shapes = [jax.ShapeDtypeStruct(shape, kind) for shape, kind in outs]
    return pl.pallas_call(
        kernel,
        in_specs=[spec for spec, _ in ins],
        out_specs=specs or [whole] * len(outs),
        out_shape=shapes,
        scratch_shapes=scratch,
        compiler_params=pltpu.CompilerParams(vmem_limit_bytes=vmem_limit),
        cost_estimate=pl.CostEstimate(flops=flops, bytes_accessed=moved, transcendentals=0),
        name=name,
    )(*[value for _, value in ins])


def dot(lhs, rhs, lhs_dim, rhs_dim, precision=None):
    return lax.dot_general(
        lhs, rhs, (((lhs_dim,), (rhs_dim,)), ((), ())),
        precision=precision, preferred_element_type=f32,
    )


def lag_tables(count, time_count, lanes):
    samples = np.arange(time_count)[:, None]
    lags = np.arange(count)[None, :]
    angle = 2.0 * math.pi / time_count * ((samples * lags) % time_count)
    table = np.zeros((time_count, lanes), np.float32)
    table[:, :count] = np.cos(angle) / time_count
    table[:, count : 2 * count] = np.sin(angle) / time_count
    return table


def lag_choice(count, quarter):
    side = count * 2 * quarter
    choice = np.zeros((2 * count, count, 2, count, 2, quarter), np.float32)
    for f in range(count):
        for g in range(count):
            sign = 1.0 if g >= f else -1.0
            lag = abs(g - f)
            choice[lag, f, 0, g, 0] = 1.0
            choice[lag, f, 1, g, 1] = 1.0
            choice[count + lag, f, 0, g, 1] = -sign
            choice[count + lag, f, 1, g, 0] = sign
    same = np.arange(quarter)[:, None] == np.arange(side)[None, :] % quarter
    return choice.reshape(2 * count, 2 * count * side), same.astype(np.float32)


def pack_rows(stage, slot, row, rank, first, second):
    size = first.shape[0]
    stage[slot, pl.ds(row, size), :] = first
    stage[slot, pl.ds(row + rank, size), :] = second


def unpack_rows(stage, slot, row, rank, total, coeffs, base):
    slots = total - total // 7
    first = stage[slot, pl.ds(row, slots), :]
    second = stage[slot, pl.ds(row + rank, slots), :]
    ids = lax.broadcasted_iota(jnp.int32, first.shape, 0)
    at = pl.ds(pl.multiple_of(base, 16), slots)
    coeffs[0, at, :] = jnp.where(ids < rank, first, 0.0).astype(bf16)
    coeffs[1, at, :] = jnp.where(ids < total - rank, second, 0.0).astype(bf16)


def side_by_side(real, imag):
    flat = (-1, real.shape[-1])
    return jnp.concatenate([real.reshape(flat), imag.reshape(flat)], axis=1)


def plain_product(coeffs, both):
    half, tile = coeffs.shape[1] // 2, both.shape[1] // 2
    product = dot(coeffs, both, 0, 0)
    lead, trail = product[:, :tile], product[:, tile:]
    return jnp.concatenate([lead[:half] - trail[half:], lead[half:] + trail[:half]], axis=0)


def split_blocks(devices):
    part = devices // 4
    return [[(3 * part, part)], [(2 * part, part), (0, 2 * part)]]


def block_base(me, block):
    first, size = block
    return (me ^ first) & ~(size - 1)


def unstage(outs, stage, m, slots, span, size, places):
    for out, place in zip(outs, places):
        for c in range(span):
            rows = stage[(m * slots + place) * span + c, pl.ds(0, size), :]
            out[m, pl.ds(c * size, size), :] = rows.astype(bf16)


def adjoint_kernel(blocks, turn, ranks_far, basis_far, u_far, *rest):
    partners = sum(size for _, size in blocks)
    ranks, u_ref, basis, stage, sems = rest[-5:]
    outs = rest[-5 - partners - turn : -5 - turn]
    turned = rest[-6] if turn else u_far
    freqs, rows, _, cols, _, slots, tile = basis_far.shape
    total = slots + slots // 6
    half = turned.shape[3] // 2
    me = lax.axis_index("tile")
    rank_copy = pltpu.make_async_copy(ranks_far, ranks, sems.at[0])
    if turn:
        data_copy = pltpu.make_async_copy(u_far, u_ref, sems.at[1])
        data_copy.start()
    rank_copy.start()
    copies = [[] for _ in range(rows)]
    at = 0
    for b, block in enumerate(blocks):
        for i in range(rows):
            for f in range(freqs):
                copy = pltpu.make_async_copy(
                    basis_far.at[f, i, pl.ds(block_base(me, block), block[1])],
                    basis.at[f, i, pl.ds(at, block[1])],
                    sems.at[2 + (b * rows + i) * freqs + f],
                )
                copy.start(priority=f % 2)
                copies[i].append(copy)
        at += block[1]
    if turn:
        data_copy.wait()
        for f in range(freqs):
            for i in range(rows):
                values = u_ref[f, i * tile : (i + 1) * tile, :]
                wide = values.astype(f32)
                lane = lax.broadcasted_iota(jnp.int32, wide.shape, 1)
                rolled = pltpu.roll(wide, half, 1)
                turned[f, i, :tile, :] = values
                turned[f, i, tile:, :] = jnp.where(lane < half, rolled, -rolled).astype(bf16)
    rank_copy.wait()
    for i in range(rows):
        for copy in copies[i]:
            copy.wait()
        for m in range(freqs // 2):
            pair = []
            for f in (2 * m, 2 * m + 1):
                both = side_by_side(basis[f, i, :, :, 0], basis[f, i, :, :, 1])
                pair.append(dot(both, turned[f, i], 1, 0))
            at = 0
            for block in blocks:
                for n in range(block[1] * cols):
                    rank = ranks[2 * m, me * rows + i, block_base(me, block) * cols + n]
                    cut = slice((at * cols + n) * slots, (at * cols + n + 1) * slots)
                    slot = (m * partners + at) * cols + n
                    pack_rows(stage, slot, i * total, rank, pair[0][cut], pair[1][cut])
                at += block[1]
    at = 0
    for first, size in blocks:
        places = [at + ((me ^ (first + n)) & (size - 1)) for n in range(size)]
        for m in range(freqs // 2):
            unstage(outs[at : at + size], stage, m, partners, cols, rows * total, places)
        at += size


def image_kernel(blocks, owners, first, last, ranks_near, basis, *rest):
    partners = sum(size for _, size in blocks)
    packed, rest = rest[:partners], rest[partners:]
    ranks, stage, coeffs, z, sem = rest[-5:]
    freqs, _, rows, cols, _, slots, tile = basis.shape
    total = slots + slots // 6
    half = coeffs.shape[3] // 2
    quarter = half // owners
    size = rows * total
    me, mine = lax.axis_index("tile"), lax.axis_index("freq")
    rank_copy = pltpu.make_async_copy(ranks_near, ranks, sem)
    rank_copy.start()
    order = [start + n for start, count in blocks for n in reversed(range(count))]
    for m in range(freqs // 2):
        for n in range(partners):
            for c in range(cols):
                rows_in = packed[n][m, pl.ds(c * size, size), :]
                stage[(m * partners + n) * cols + c, pl.ds(0, size), :] = rows_in.astype(f32)
    rank_copy.wait()
    for m in range(freqs // 2):
        for c in range(cols):
            at = 0
            for start, count in blocks:
                for n in range(at, at + count):
                    partner = me ^ order[n]
                    for i in range(rows):
                        rank = ranks[0, (m * basis.shape[1] * rows + partner * rows + i) * cols + c]
                        slot = (m * partners + n) * cols + c
                        place = ((at + (partner & (count - 1))) * rows + i) * slots
                        unpack_rows(stage, slot, i * total, rank, total, coeffs.at[c], place)
                at += count
            for n in range(2):
                f = 2 * m + n
                part = None if first else rest[0][f, :, pl.ds(c * tile, tile)]
                at = 0
                for block in blocks:
                    here = pl.ds(block_base(me, block), block[1])
                    both = side_by_side(basis[f, here, :, c, 0], basis[f, here, :, c, 1])
                    rows_at = slice(at * rows * slots, (at + block[1]) * rows * slots)
                    term = plain_product(coeffs[c, n, rows_at], both)
                    part = term if part is None else part + term
                    at += block[1]
                if last:
                    z[f, :, pl.ds(c * tile, tile)] = part
                else:
                    rest[-6][f, :, pl.ds(c * tile, tile)] = part
    if last:
        outs = rest[-5 - owners : -5]
        for r in range(owners):
            low = pl.multiple_of((mine ^ r) * quarter, quarter)
            for f in range(freqs):
                real = z[f, pl.ds(low, quarter), :]
                imag = z[f, pl.ds(half + low, quarter), :]
                outs[r][f] = jnp.concatenate([real, imag], axis=0).astype(bf16)


def prepare_kernel(rows, cols, ranks_far, mask, table, choice, same, *rest):
    short, high, low, ranks, full, sem = rest[-6:]
    freqs, row_tiles, col_tiles = ranks.shape
    me = lax.axis_index("tile")
    rank_copy = pltpu.make_async_copy(ranks_far, ranks, sem)
    rank_copy.start()
    exact = lax.Precision.HIGHEST
    full[...] = dot(mask[...].astype(f32), table[...], 0, 0, exact)
    quarter, side = same.shape
    mine = full[pl.ds(pl.multiple_of(lax.axis_index("freq") * quarter, quarter), quarter), :]
    entries = dot(mine[:, : choice.shape[0]], choice[...], 1, 0, exact)
    for n in range(side // quarter):
        block = entries[:, n * side : (n + 1) * side] * same[...]
        upper = block.astype(bf16)
        high[n * quarter : (n + 1) * quarter, :] = upper
        low[n * quarter : (n + 1) * quarter, :] = (block - upper.astype(f32)).astype(bf16)
    rank_copy.wait()
    at = 0
    for m in range(freqs // 2):
        for row in range(row_tiles):
            for c in range(cols):
                short[0, at] = ranks[2 * m, row, me * cols + c]
                at += 1
    for m in range(freqs // 2):
        for i in range(rows):
            for col in range(col_tiles):
                short[0, at] = ranks[2 * m, me * rows + i, col]
                at += 1


def mix_kernel(owners, high, low, *rest):
    arrived = rest[:owners][::-1]
    outs = rest[owners : 2 * owners]
    z, w = rest[2 * owners :]
    freqs, rows, span = arrived[0].shape
    mine = lax.axis_index("freq")
    size = freqs * rows
    for r in range(owners):
        z[pl.ds(pl.multiple_of((mine ^ r) * size, 16), size), :] = arrived[r][...].reshape(size, span)
    w[...] = dot(high[...], z[...], 1, 0) + dot(low[...], z[...], 1, 0)
    for r in range(owners):
        block = w[pl.ds(pl.multiple_of((mine ^ r) * size, 16), size), :]
        outs[r][...] = block.reshape(freqs, rows, span).astype(bf16)


def forward_kernel(devices, owners, ranks_near, basis, *rest):
    arrived = rest[:owners][::-1]
    outs = rest[owners : owners + devices]
    ranks, w, stage, sem = rest[owners + devices :]
    freqs, _, rows, cols, _, slots, tile = basis.shape
    total = slots + slots // 6
    half = w.shape[2] // 2
    quarter = half // owners
    me, mine = lax.axis_index("tile"), lax.axis_index("freq")
    rank_copy = pltpu.make_async_copy(ranks_near, ranks, sem)
    rank_copy.start()
    for r in range(owners):
        low = pl.multiple_of((mine ^ r) * quarter, quarter)
        for f in range(freqs):
            for c in range(cols):
                at = slice(c * tile, (c + 1) * tile)
                real, imag = arrived[r][f, :quarter, at], arrived[r][f, quarter:, at]
                w[f, c, pl.ds(low, quarter), :tile] = real
                w[f, c, pl.ds(half + low, quarter), :tile] = imag
                w[f, c, pl.ds(low, quarter), tile:] = imag
                w[f, c, pl.ds(half + low, quarter), tile:] = -real
    rank_copy.wait()
    for m in range(freqs // 2):
        for c in range(cols):
            pair = []
            for f in (2 * m, 2 * m + 1):
                both = side_by_side(basis[f, :, :, c, 0], basis[f, :, :, c, 1])
                pair.append(dot(both, w[f, c], 1, 1))
            for d in range(devices):
                for i in range(rows):
                    rank = ranks[0, (m * devices * rows + d * rows + i) * cols + c]
                    cut = slice((d * rows + i) * slots, (d * rows + i + 1) * slots)
                    slot = (m * devices + d) * cols + c
                    pack_rows(stage, slot, i * total, rank, pair[0][cut], pair[1][cut])
        unstage(outs, stage, m, devices, cols, rows * total, [me ^ n for n in range(devices)])


def result_kernel(devices, ranks_near, basis, *rest):
    packed = rest[:devices][::-1]
    out, ranks, stage, coeffs, sem = rest[devices:]
    freqs, rows, _, cols, _, slots, tile = basis.shape
    total = slots + slots // 6
    size = rows * total
    before = freqs // 2 * devices * rows * cols
    me = lax.axis_index("tile")
    rank_copy = pltpu.make_async_copy(ranks_near, ranks, sem)
    rank_copy.start()
    for m in range(freqs // 2):
        for s in range(devices):
            for c in range(cols):
                block = packed[s][m, pl.ds(c * size, size), :]
                stage[(m * devices + s) * cols + c, pl.ds(0, size), :] = block.astype(f32)
    rank_copy.wait()
    for m in range(freqs // 2):
        for i in range(rows):
            for s in range(devices):
                for c in range(cols):
                    col = (me ^ s) * cols + c
                    rank = ranks[0, before + (m * rows + i) * devices * cols + col]
                    slot = (m * devices + s) * cols + c
                    unpack_rows(stage, slot, i * total, rank, total, coeffs.at[i], col * slots)
            for n in range(2):
                f = 2 * m + n
                both = side_by_side(basis[f, i, :, :, 0], basis[f, i, :, :, 1])
                r = plain_product(coeffs[i, n], both)
                out[f, pl.ds(i * tile, tile), :] = r.T.astype(bf16)


def send(value, axis, s):
    if s == 0:
        return value
    return lax.ppermute(value, axis, [(d, d ^ s) for d in range(lax.axis_size(axis))])


def spread(values, axis, first=0):
    return [(whole, send(values[s], axis, first + s)) for s in reversed(range(len(values)))]


def local(u_data, u_basis, v_basis, ranks, time_mask):
    freqs, row_count, width = u_data.shape
    rows, col_tiles, _, slots, tile = u_basis.shape[1:]
    row_tiles, cols = v_basis.shape[1:3]
    total = slots // 6 + slots
    pairs = freqs // 2
    devices = lax.axis_size("tile")
    owners = lax.axis_size("freq")
    stage_rows = rows * total + 2 * slots
    quarter = width // 2 // owners
    count = owners * freqs
    side = count * 2 * quarter
    by_cols = u_basis.reshape(freqs, rows, devices, cols, 2, slots, tile)
    by_rows = v_basis.reshape(freqs, devices, rows, cols, 2, slots, tile)
    per_device = [((pairs, cols * rows * total, width), bf16)] * devices
    per_owner = [((freqs, 2 * quarter, cols * tile), bf16)] * owners
    work = {"flops": 4 * row_count * slots * width * col_tiles * freqs * 2, "moved": u_basis.size * 2}
    count_short = pairs * (row_tiles * cols + rows * col_tiles)
    ranks_here = pltpu.SMEM((1, count_short), jnp.int32)
    stage = pltpu.VMEM((pairs * devices * cols, stage_rows, width), f32)
    one = pltpu.SemaphoreType.DMA

    table = lag_tables(count, time_mask.shape[0], 128)
    choice, same = lag_choice(count, quarter)
    def share(partners):
        return {name: value * partners // devices for name, value in work.items()}

    def stage_for(partners):
        return pltpu.VMEM((pairs * partners * cols, stage_rows, width), f32)

    calls = split_blocks(devices)
    data, after, packed = (far, hold(u_data)), [], {}
    for k, blocks in enumerate(calls):
        turn = int(k == 0)
        partners = sum(size for _, size in blocks)
        made = call(
            functools.partial(adjoint_kernel, blocks, turn),
            "adjoint",
            [(far, hold(ranks)), (far, hold(by_cols)), data] + after,
            [((pairs, cols * rows * total, width), bf16)] * partners
            + [((freqs, rows, 2 * tile, width), bf16)] * turn,
            [
                pltpu.SMEM(ranks.shape, jnp.int32),
                pltpu.VMEM((freqs, row_count, width), bf16),
                pltpu.VMEM((freqs, rows, partners, cols, 2, slots, tile), bf16),
                stage_for(partners),
                one((2 + freqs * rows * len(blocks),)),
            ],
            **share(partners),
        )
        if turn:
            data = (whole, made[-1])
        for block in blocks:
            packed[block], made = made[: block[1]], made[block[1] :]
    short, *window = call(
        functools.partial(prepare_kernel, rows, cols),
        "prepare",
        [(far, hold(ranks))]
        + [(whole, jnp.asarray(x)) for x in (time_mask, table, choice, same)]
        + [(anywhere, packed[calls[-1][-1]][0])],
        [((1, count_short), jnp.int32)] + [((side, side), bf16)] * 2,
        [pltpu.SMEM(ranks.shape, jnp.int32), pltpu.VMEM((width // 2, 128), f32), one],
        specs=[scalars, whole, whole],
        flops=6 * quarter * 2 * count * 2 * count * side,
    )
    images = []
    for k, blocks in enumerate(calls):
        first, last = k == 0, k == len(calls) - 1
        partners = sum(size for _, size in blocks)
        images = call(
            functools.partial(image_kernel, blocks, owners, first, last),
            "image",
            [(whole, short), (whole, by_rows)]
            + [x for block in blocks for x in spread(packed[block], "tile", block[0])]
            + [(whole, x) for x in images],
            per_owner if last else [((freqs, width, cols * tile), f32)],
            [
                ranks_here,
                stage_for(partners),
                pltpu.VMEM((cols, 2, partners * rows * slots, width), bf16),
                pltpu.VMEM((freqs, width, cols * tile), f32),
                one,
            ],
            **share(partners),
        )
    mixed = call(
        functools.partial(mix_kernel, owners),
        "mix",
        [(whole, x) for x in window] + spread(images, "freq"),
        per_owner,
        [pltpu.VMEM((side, cols * tile), bf16), pltpu.VMEM((side, cols * tile), f32)],
        flops=4 * side * side * cols * tile,
    )
    packed = call(
        functools.partial(forward_kernel, devices, owners),
        "forward",
        [(whole, short), (whole, by_rows)] + spread(mixed, "freq"),
        per_device,
        [ranks_here, pltpu.VMEM((freqs, cols, width, 2 * tile), bf16), stage, one],
        **work,
    )
    [out] = call(
        functools.partial(result_kernel, devices),
        "result",
        [(whole, short), (whole, by_cols)] + spread(packed, "tile"),
        [((freqs, row_count, width), bf16)],
        [ranks_here, stage, pltpu.VMEM((rows, 2, col_tiles * slots, width), bf16), one],
        **work,
    )
    return out


def solution(mesh):
    placed = (
        P("freq", "tile", None),
        P("freq", "tile", None, None, None, None),
        P("freq", None, "tile", None, None, None),
        P("freq", None, None),
        P(),
    )
    return jax.shard_map(
        local, mesh=mesh, in_specs=placed, out_specs=P("freq", "tile", None), check_vma=False
    )
```

```python
import functools
import math

import jax
import jax.numpy as jnp
import numpy as np
from jax import lax
from jax.experimental import pallas as pl
from jax.experimental.pallas import tpu as pltpu
from jax.sharding import PartitionSpec as P

vmem_limit = 48 * 1024 * 1024
bf16 = jnp.bfloat16
f32 = jnp.float32

whole = pl.BlockSpec(memory_space=pltpu.VMEM)
scalars = pl.BlockSpec(memory_space=pltpu.SMEM)
far = pl.BlockSpec(memory_space=pltpu.HBM)
anywhere = pl.BlockSpec(memory_space=pl.ANY)


def hold(value):
    return pltpu.with_memory_space_constraint(value, pltpu.HBM)


def call(kernel, name, ins, outs, scratch, flops=0, moved=0, specs=None):
    shapes = [jax.ShapeDtypeStruct(shape, kind) for shape, kind in outs]
    return pl.pallas_call(
        kernel,
        in_specs=[spec for spec, _ in ins],
        out_specs=specs or [whole] * len(outs),
        out_shape=shapes,
        scratch_shapes=scratch,
        compiler_params=pltpu.CompilerParams(vmem_limit_bytes=vmem_limit),
        cost_estimate=pl.CostEstimate(flops=flops, bytes_accessed=moved, transcendentals=0),
        name=name,
    )(*[value for _, value in ins])


def dot(lhs, rhs, lhs_dim, rhs_dim, precision=None):
    return lax.dot_general(
        lhs, rhs, (((lhs_dim,), (rhs_dim,)), ((), ())),
        precision=precision, preferred_element_type=f32,
    )


def lag_tables(count, time_count, lanes):
    samples = np.arange(time_count)[:, None]
    lags = np.arange(count)[None, :]
    angle = 2.0 * math.pi / time_count * ((samples * lags) % time_count)
    table = np.zeros((time_count, lanes), np.float32)
    table[:, :count] = np.cos(angle) / time_count
    table[:, count : 2 * count] = np.sin(angle) / time_count
    return table


def lag_choice(count, quarter):
    side = count * 2 * quarter
    choice = np.zeros((2 * count, count, 2, count, 2, quarter), np.float32)
    for f in range(count):
        for g in range(count):
            sign = 1.0 if g >= f else -1.0
            lag = abs(g - f)
            choice[lag, f, 0, g, 0] = 1.0
            choice[lag, f, 1, g, 1] = 1.0
            choice[count + lag, f, 0, g, 1] = -sign
            choice[count + lag, f, 1, g, 0] = sign
    same = np.arange(quarter)[:, None] == np.arange(side)[None, :] % quarter
    return choice.reshape(2 * count, 2 * count * side), same.astype(np.float32)


def pack_rows(stage, slot, row, rank, first, second):
    size = first.shape[0]
    stage[slot, pl.ds(row, size), :] = first
    stage[slot, pl.ds(row + rank, size), :] = second


def unpack_rows(stage, slot, row, rank, total, coeffs, base):
    slots = total - total // 7
    first = stage[slot, pl.ds(row, slots), :]
    second = stage[slot, pl.ds(row + rank, slots), :]
    ids = lax.broadcasted_iota(jnp.int32, first.shape, 0)
    at = pl.ds(pl.multiple_of(base, 16), slots)
    coeffs[0, at, :] = jnp.where(ids < rank, first, 0.0).astype(bf16)
    coeffs[1, at, :] = jnp.where(ids < total - rank, second, 0.0).astype(bf16)


def side_by_side(real, imag):
    flat = (-1, real.shape[-1])
    return jnp.concatenate([real.reshape(flat), imag.reshape(flat)], axis=1)


def turn_over(values):
    side = values.shape[1]
    row = lax.broadcasted_iota(jnp.int32, (side, side), 0)
    unit = (row == lax.broadcasted_iota(jnp.int32, (side, side), 1)).astype(f32).astype(bf16)
    return dot(unit, values, 1, 1).astype(bf16)


def plain_product(coeffs, both):
    half, tile = coeffs.shape[1] // 2, both.shape[1] // 2
    product = dot(turn_over(coeffs), both, 1, 0)
    lead, trail = product[:, :tile], product[:, tile:]
    return jnp.concatenate([lead[:half] - trail[half:], lead[half:] + trail[:half]], axis=0)


def split_blocks(devices):
    half = devices // 2
    return [[(half, half)], [(0, half)]]


def block_base(me, block):
    first, size = block
    return (me ^ first) & ~(size - 1)


def unstage(outs, stage, m, slots, span, size, places):
    for out, place in zip(outs, places):
        for c in range(span):
            rows = stage[(m * slots + place) * span + c, pl.ds(0, size), :]
            out[m, pl.ds(c * size, size), :] = rows.astype(bf16)


def adjoint_kernel(blocks, turn, ranks_far, basis_far, u_far, *rest):
    partners = sum(size for _, size in blocks)
    ranks, u_ref, basis, stage, sems = rest[-5:]
    outs = rest[-5 - partners - turn : -5 - turn]
    turned = rest[-6] if turn else u_far
    freqs, rows, _, cols, _, slots, tile = basis_far.shape
    total = slots + slots // 6
    half = turned.shape[3] // 2
    me = lax.axis_index("tile")
    rank_copy = pltpu.make_async_copy(ranks_far, ranks, sems.at[0])
    if turn:
        data_copy = pltpu.make_async_copy(u_far, u_ref, sems.at[1])
        data_copy.start()
    rank_copy.start()
    copies = [[] for _ in range(rows)]
    at = 0
    for b, block in enumerate(blocks):
        for i in range(rows):
            for f in range(freqs):
                copy = pltpu.make_async_copy(
                    basis_far.at[f, i, pl.ds(block_base(me, block), block[1])],
                    basis.at[f, i, pl.ds(at, block[1])],
                    sems.at[2 + (b * rows + i) * freqs + f],
                )
                copy.start(priority=f % 2)
                copies[i].append(copy)
        at += block[1]
    if turn:
        data_copy.wait()
        for f in range(freqs):
            for i in range(rows):
                values = u_ref[f, i * tile : (i + 1) * tile, :]
                wide = values.astype(f32)
                lane = lax.broadcasted_iota(jnp.int32, wide.shape, 1)
                rolled = pltpu.roll(wide, half, 1)
                turned[f, i, :tile, :] = values
                turned[f, i, tile:, :] = jnp.where(lane < half, rolled, -rolled).astype(bf16)
    rank_copy.wait()
    for i in range(rows):
        for copy in copies[i]:
            copy.wait()
        for m in range(freqs // 2):
            pair = []
            for f in (2 * m, 2 * m + 1):
                both = side_by_side(basis[f, i, :, :, 0], basis[f, i, :, :, 1])
                pair.append(dot(both, turned[f, i], 1, 0))
            at = 0
            for block in blocks:
                for n in range(block[1] * cols):
                    rank = ranks[2 * m, me * rows + i, block_base(me, block) * cols + n]
                    cut = slice((at * cols + n) * slots, (at * cols + n + 1) * slots)
                    slot = (m * partners + at) * cols + n
                    pack_rows(stage, slot, i * total, rank, pair[0][cut], pair[1][cut])
                at += block[1]
    at = 0
    for first, size in blocks:
        places = [at + ((me ^ (first + n)) & (size - 1)) for n in range(size)]
        for m in range(freqs // 2):
            unstage(outs[at : at + size], stage, m, partners, cols, rows * total, places)
        at += size


def image_kernel(devices, owners, ranks_near, basis, *rest):
    packed = rest[:devices][::-1]
    outs = rest[-owners - 5 : -5]
    ranks, stage, coeffs, z, sem = rest[-5:]
    freqs, _, rows, cols, _, slots, tile = basis.shape
    total = slots + slots // 6
    half = coeffs.shape[3] // 2
    quarter = half // owners
    size = rows * total
    me, mine = lax.axis_index("tile"), lax.axis_index("freq")
    rank_copy = pltpu.make_async_copy(ranks_near, ranks, sem)
    rank_copy.start()
    for m in range(freqs // 2):
        for s in range(devices):
            for c in range(cols):
                block = packed[s][m, pl.ds(c * size, size), :]
                stage[(m * devices + s) * cols + c, pl.ds(0, size), :] = block.astype(f32)
    rank_copy.wait()
    for m in range(freqs // 2):
        for c in range(cols):
            for s in range(devices):
                for i in range(rows):
                    row = (me ^ s) * rows + i
                    rank = ranks[0, (m * devices * rows + row) * cols + c]
                    slot = (m * devices + s) * cols + c
                    unpack_rows(stage, slot, i * total, rank, total, coeffs.at[c], row * slots)
            for n in range(2):
                f = 2 * m + n
                both = side_by_side(basis[f, :, :, c, 0], basis[f, :, :, c, 1])
                z[f, :, pl.ds(c * tile, tile)] = plain_product(coeffs[c, n], both)
    for r in range(owners):
        low = pl.multiple_of((mine ^ r) * quarter, quarter)
        for f in range(freqs):
            real = z[f, pl.ds(low, quarter), :]
            imag = z[f, pl.ds(half + low, quarter), :]
            outs[r][f] = jnp.concatenate([real, imag], axis=0).astype(bf16)


def prepare_kernel(rows, cols, ranks_far, mask, table, choice, same, *rest):
    short, high, low, ranks, full, sem = rest[-6:]
    freqs, row_tiles, col_tiles = ranks.shape
    me = lax.axis_index("tile")
    rank_copy = pltpu.make_async_copy(ranks_far, ranks, sem)
    rank_copy.start()
    exact = lax.Precision.HIGHEST
    full[...] = dot(mask[...].astype(f32), table[...], 0, 0, exact)
    quarter, side = same.shape
    mine = full[pl.ds(pl.multiple_of(lax.axis_index("freq") * quarter, quarter), quarter), :]
    entries = dot(mine[:, : choice.shape[0]], choice[...], 1, 0, exact)
    for n in range(side // quarter):
        block = entries[:, n * side : (n + 1) * side] * same[...]
        upper = block.astype(bf16)
        high[n * quarter : (n + 1) * quarter, :] = upper
        low[n * quarter : (n + 1) * quarter, :] = (block - upper.astype(f32)).astype(bf16)
    rank_copy.wait()
    at = 0
    for m in range(freqs // 2):
        for row in range(row_tiles):
            for c in range(cols):
                short[0, at] = ranks[2 * m, row, me * cols + c]
                at += 1
    for m in range(freqs // 2):
        for i in range(rows):
            for col in range(col_tiles):
                short[0, at] = ranks[2 * m, me * rows + i, col]
                at += 1


def mix_kernel(owners, high, low, *rest):
    arrived = rest[:owners][::-1]
    outs = rest[owners : 2 * owners]
    z, w = rest[2 * owners :]
    freqs, rows, span = arrived[0].shape
    mine = lax.axis_index("freq")
    size = freqs * rows
    for r in range(owners):
        z[pl.ds(pl.multiple_of((mine ^ r) * size, 16), size), :] = arrived[r][...].reshape(size, span)
    w[...] = dot(high[...], z[...], 1, 0) + dot(low[...], z[...], 1, 0)
    for r in range(owners):
        block = w[pl.ds(pl.multiple_of((mine ^ r) * size, 16), size), :]
        outs[r][...] = block.reshape(freqs, rows, span).astype(bf16)


def forward_kernel(devices, owners, ranks_near, basis, *rest):
    arrived = rest[:owners][::-1]
    outs = rest[owners : owners + devices]
    ranks, w, stage, sem = rest[owners + devices :]
    freqs, _, rows, cols, _, slots, tile = basis.shape
    total = slots + slots // 6
    half = w.shape[2] // 2
    quarter = half // owners
    me, mine = lax.axis_index("tile"), lax.axis_index("freq")
    rank_copy = pltpu.make_async_copy(ranks_near, ranks, sem)
    rank_copy.start()
    for r in range(owners):
        low = pl.multiple_of((mine ^ r) * quarter, quarter)
        for f in range(freqs):
            for c in range(cols):
                at = slice(c * tile, (c + 1) * tile)
                real, imag = arrived[r][f, :quarter, at], arrived[r][f, quarter:, at]
                w[f, c, pl.ds(low, quarter), :tile] = real
                w[f, c, pl.ds(half + low, quarter), :tile] = imag
                w[f, c, pl.ds(low, quarter), tile:] = imag
                w[f, c, pl.ds(half + low, quarter), tile:] = -real
    rank_copy.wait()
    for m in range(freqs // 2):
        for c in range(cols):
            pair = []
            for f in (2 * m, 2 * m + 1):
                both = side_by_side(basis[f, :, :, c, 0], basis[f, :, :, c, 1])
                pair.append(dot(both, w[f, c], 1, 1))
            for d in range(devices):
                for i in range(rows):
                    rank = ranks[0, (m * devices * rows + d * rows + i) * cols + c]
                    cut = slice((d * rows + i) * slots, (d * rows + i + 1) * slots)
                    slot = (m * devices + d) * cols + c
                    pack_rows(stage, slot, i * total, rank, pair[0][cut], pair[1][cut])
        unstage(outs, stage, m, devices, cols, rows * total, [me ^ n for n in range(devices)])


def result_kernel(devices, ranks_near, basis, *rest):
    packed = rest[:devices][::-1]
    out, ranks, stage, coeffs, sem = rest[devices:]
    freqs, rows, _, cols, _, slots, tile = basis.shape
    total = slots + slots // 6
    size = rows * total
    before = freqs // 2 * devices * rows * cols
    me = lax.axis_index("tile")
    rank_copy = pltpu.make_async_copy(ranks_near, ranks, sem)
    rank_copy.start()
    for m in range(freqs // 2):
        for s in range(devices):
            for c in range(cols):
                block = packed[s][m, pl.ds(c * size, size), :]
                stage[(m * devices + s) * cols + c, pl.ds(0, size), :] = block.astype(f32)
    rank_copy.wait()
    for m in range(freqs // 2):
        for i in range(rows):
            for s in range(devices):
                for c in range(cols):
                    col = (me ^ s) * cols + c
                    rank = ranks[0, before + (m * rows + i) * devices * cols + col]
                    slot = (m * devices + s) * cols + c
                    unpack_rows(stage, slot, i * total, rank, total, coeffs.at[i], col * slots)
            for n in range(2):
                f = 2 * m + n
                both = side_by_side(basis[f, i, :, :, 0], basis[f, i, :, :, 1])
                r = plain_product(coeffs[i, n], both)
                out[f, pl.ds(i * tile, tile), :] = turn_over(r.astype(bf16))


def send(value, axis, s):
    if s == 0:
        return value
    return lax.ppermute(value, axis, [(d, d ^ s) for d in range(lax.axis_size(axis))])


def spread(values, axis, first=0):
    return [(whole, send(values[s], axis, first + s)) for s in reversed(range(len(values)))]


def local(u_data, u_basis, v_basis, ranks, time_mask):
    freqs, row_count, width = u_data.shape
    rows, col_tiles, _, slots, tile = u_basis.shape[1:]
    row_tiles, cols = v_basis.shape[1:3]
    total = slots // 6 + slots
    pairs = freqs // 2
    devices = lax.axis_size("tile")
    owners = lax.axis_size("freq")
    stage_rows = rows * total + 2 * slots
    quarter = width // 2 // owners
    count = owners * freqs
    side = count * 2 * quarter
    by_cols = u_basis.reshape(freqs, rows, devices, cols, 2, slots, tile)
    by_rows = v_basis.reshape(freqs, devices, rows, cols, 2, slots, tile)
    per_device = [((pairs, cols * rows * total, width), bf16)] * devices
    per_owner = [((freqs, 2 * quarter, cols * tile), bf16)] * owners
    work = {"flops": 4 * row_count * slots * width * col_tiles * freqs * 2, "moved": u_basis.size * 2}
    count_short = pairs * (row_tiles * cols + rows * col_tiles)
    ranks_here = pltpu.SMEM((1, count_short), jnp.int32)
    stage = pltpu.VMEM((pairs * devices * cols, stage_rows, width), f32)
    one = pltpu.SemaphoreType.DMA

    table = lag_tables(count, time_mask.shape[0], 128)
    choice, same = lag_choice(count, quarter)
    def share(partners):
        return {name: value * partners // devices for name, value in work.items()}

    def stage_for(partners):
        return pltpu.VMEM((pairs * partners * cols, stage_rows, width), f32)

    calls = split_blocks(devices)
    data, after, packed = (far, hold(u_data)), [], {}
    for k, blocks in enumerate(calls):
        turn = int(k == 0)
        partners = sum(size for _, size in blocks)
        made = call(
            functools.partial(adjoint_kernel, blocks, turn),
            "adjoint",
            [(far, hold(ranks)), (far, hold(by_cols)), data] + after,
            [((pairs, cols * rows * total, width), bf16)] * partners
            + [((freqs, rows, 2 * tile, width), bf16)] * turn,
            [
                pltpu.SMEM(ranks.shape, jnp.int32),
                pltpu.VMEM((freqs, row_count, width), bf16),
                pltpu.VMEM((freqs, rows, partners, cols, 2, slots, tile), bf16),
                stage_for(partners),
                one((2 + freqs * rows * len(blocks),)),
            ],
            **share(partners),
        )
        if turn:
            data = (whole, made[-1])
        for block in blocks:
            packed[block], made = made[: block[1]], made[block[1] :]
    short, *window = call(
        functools.partial(prepare_kernel, rows, cols),
        "prepare",
        [(far, hold(ranks))]
        + [(whole, jnp.asarray(x)) for x in (time_mask, table, choice, same)]
        + [(anywhere, packed[calls[-1][-1]][0])],
        [((1, count_short), jnp.int32)] + [((side, side), bf16)] * 2,
        [pltpu.SMEM(ranks.shape, jnp.int32), pltpu.VMEM((width // 2, 128), f32), one],
        specs=[scalars, whole, whole],
        flops=6 * quarter * 2 * count * 2 * count * side,
    )
    images = call(
        functools.partial(image_kernel, devices, owners),
        "image",
        [(whole, short), (whole, by_rows)]
        + [x for blocks in calls for b in blocks for x in spread(packed[b], "tile", b[0])],
        per_owner,
        [
            ranks_here,
            stage,
            pltpu.VMEM((cols, 2, row_tiles * slots, width), bf16),
            pltpu.VMEM((freqs, width, cols * tile), f32),
            one,
        ],
        **work,
    )
    mixed = call(
        functools.partial(mix_kernel, owners),
        "mix",
        [(whole, x) for x in window] + spread(images, "freq"),
        per_owner,
        [pltpu.VMEM((side, cols * tile), bf16), pltpu.VMEM((side, cols * tile), f32)],
        flops=4 * side * side * cols * tile,
    )
    packed = call(
        functools.partial(forward_kernel, devices, owners),
        "forward",
        [(whole, short), (whole, by_rows)] + spread(mixed, "freq"),
        per_device,
        [ranks_here, pltpu.VMEM((freqs, cols, width, 2 * tile), bf16), stage, one],
        **work,
    )
    [out] = call(
        functools.partial(result_kernel, devices),
        "result",
        [(whole, short), (whole, by_cols)] + spread(packed, "tile"),
        [((freqs, row_count, width), bf16)],
        [ranks_here, stage, pltpu.VMEM((rows, 2, col_tiles * slots, width), bf16), one],
        **work,
    )
    return out


def solution(mesh):
    placed = (
        P("freq", "tile", None),
        P("freq", "tile", None, None, None, None),
        P("freq", None, "tile", None, None, None),
        P("freq", None, None),
        P(),
    )
    return jax.shard_map(
        local, mesh=mesh, in_specs=placed, out_specs=P("freq", "tile", None), check_vma=False
    )
```

```python
import functools
import math

import jax
import jax.numpy as jnp
import numpy as np
from jax import lax
from jax.experimental import pallas as pl
from jax.experimental.pallas import tpu as pltpu
from jax.sharding import PartitionSpec as P

vmem_limit = 48 * 1024 * 1024
bf16 = jnp.bfloat16
f32 = jnp.float32

whole = pl.BlockSpec(memory_space=pltpu.VMEM)
scalars = pl.BlockSpec(memory_space=pltpu.SMEM)
far = pl.BlockSpec(memory_space=pltpu.HBM)
anywhere = pl.BlockSpec(memory_space=pl.ANY)


def hold(value):
    return pltpu.with_memory_space_constraint(value, pltpu.HBM)


def call(kernel, name, ins, outs, scratch, flops=0, moved=0, specs=None):
    shapes = [jax.ShapeDtypeStruct(shape, kind) for shape, kind in outs]
    return pl.pallas_call(
        kernel,
        in_specs=[spec for spec, _ in ins],
        out_specs=specs or [whole] * len(outs),
        out_shape=shapes,
        scratch_shapes=scratch,
        compiler_params=pltpu.CompilerParams(vmem_limit_bytes=vmem_limit),
        cost_estimate=pl.CostEstimate(flops=flops, bytes_accessed=moved, transcendentals=0),
        name=name,
    )(*[value for _, value in ins])


def dot(lhs, rhs, lhs_dim, rhs_dim, precision=None):
    return lax.dot_general(
        lhs, rhs, (((lhs_dim,), (rhs_dim,)), ((), ())),
        precision=precision, preferred_element_type=f32,
    )


def lag_tables(count, time_count, lanes):
    samples = np.arange(time_count)[:, None]
    lags = np.arange(count)[None, :]
    angle = 2.0 * math.pi / time_count * ((samples * lags) % time_count)
    table = np.zeros((time_count, lanes), np.float32)
    table[:, :count] = np.cos(angle) / time_count
    table[:, count : 2 * count] = np.sin(angle) / time_count
    return table


def lag_choice(count, quarter):
    side = count * 2 * quarter
    choice = np.zeros((2 * count, count, 2, count, 2, quarter), np.float32)
    for f in range(count):
        for g in range(count):
            sign = 1.0 if g >= f else -1.0
            lag = abs(g - f)
            choice[lag, f, 0, g, 0] = 1.0
            choice[lag, f, 1, g, 1] = 1.0
            choice[count + lag, f, 0, g, 1] = -sign
            choice[count + lag, f, 1, g, 0] = sign
    same = np.arange(quarter)[:, None] == np.arange(side)[None, :] % quarter
    return choice.reshape(2 * count, 2 * count * side), same.astype(np.float32)


def pack_rows(stage, slot, row, rank, first, second):
    size = first.shape[0]
    stage[slot, pl.ds(row, size), :] = first
    stage[slot, pl.ds(row + rank, size), :] = second


def unpack_rows(stage, slot, row, rank, total, coeffs, base):
    slots = total - total // 7
    first = stage[slot, pl.ds(row, slots), :]
    second = stage[slot, pl.ds(row + rank, slots), :]
    ids = lax.broadcasted_iota(jnp.int32, first.shape, 0)
    at = pl.ds(pl.multiple_of(base, 16), slots)
    coeffs[0, at, :] = jnp.where(ids < rank, first, 0.0).astype(bf16)
    coeffs[1, at, :] = jnp.where(ids < total - rank, second, 0.0).astype(bf16)


def side_by_side(real, imag):
    flat = (-1, real.shape[-1])
    return jnp.concatenate([real.reshape(flat), imag.reshape(flat)], axis=1)


def plain_product(coeffs, both):
    half, tile = coeffs.shape[1] // 2, both.shape[1] // 2
    product = dot(coeffs, both, 0, 0)
    lead, trail = product[:, :tile], product[:, tile:]
    return jnp.concatenate([lead[:half] - trail[half:], lead[half:] + trail[:half]], axis=0)


def parity(value, mask):
    odd = value & 0
    bit = 0
    while mask >> bit:
        if (mask >> bit) & 1:
            odd = odd ^ ((value >> bit) & 1)
        bit += 1
    return odd


def exchange_slots(devices):
    half = devices // 2
    spare, mixed = list(range(half, devices)), []
    alone = []
    for near in reversed(range(2, half)):
        found = [
            (far, mask)
            for far in spare
            for mask in range(3, devices, 2)
            if not parity(near, mask) and not parity(far, mask)
        ]
        if found and len(spare) > 2:
            far, mask = found[0]
            spare.remove(far)
            mixed += [(far, near, mask), (near, far, mask)]
        else:
            alone.append((near, near, 1))
    first = [(far, far, 1) for far in reversed(spare)]
    return first, mixed + alone + [(1, 1, 1)] * (devices > 1) + [(0, 0, 1)]


def partner(me, slot):
    even, odd, mask = slot
    if even == odd:
        return me ^ even
    return me ^ (even ^ (parity(me, mask) * (even ^ odd)))


def unstage(outs, slots_out, stage, m, devices, span, size, me):
    for out, slot in zip(outs, slots_out):
        for c in range(span):
            rows = stage[(m * devices + partner(me, slot)) * span + c, pl.ds(0, size), :]
            out[m, pl.ds(c * size, size), :] = rows.astype(bf16)


def adjoint_kernel(slots_out, turn, ranks_far, basis_far, u_far, *rest):
    shifts = sorted({n for slot in slots_out for n in slot[:2]})
    ranks, u_ref, basis, stage, sems = rest[-5:]
    outs = rest[-5 - len(slots_out) - turn : -5 - turn]
    turned = rest[-6] if turn else u_far
    freqs, rows, devices, cols, _, slots, tile = basis_far.shape
    total = slots + slots // 6
    half = turned.shape[3] // 2
    me = lax.axis_index("tile")
    rank_copy = pltpu.make_async_copy(ranks_far, ranks, sems.at[0])
    if turn:
        data_copy = pltpu.make_async_copy(u_far, u_ref, sems.at[1])
        data_copy.start()
    rank_copy.start()
    copies = [[] for _ in range(rows)]
    for i in range(rows):
        for f in range(freqs):
            for n, shift in enumerate(shifts):
                copy = pltpu.make_async_copy(
                    basis_far.at[f, i, me ^ shift],
                    basis.at[f, i, n],
                    sems.at[2 + (i * freqs + f) * len(shifts) + n],
                )
                copy.start(priority=n % 2)
                copies[i].append(copy)
    if turn:
        data_copy.wait()
        for f in range(freqs):
            for i in range(rows):
                values = u_ref[f, i * tile : (i + 1) * tile, :]
                wide = values.astype(f32)
                lane = lax.broadcasted_iota(jnp.int32, wide.shape, 1)
                rolled = pltpu.roll(wide, half, 1)
                turned[f, i, :tile, :] = values
                turned[f, i, tile:, :] = jnp.where(lane < half, rolled, -rolled).astype(bf16)
    rank_copy.wait()
    for i in range(rows):
        for copy in copies[i]:
            copy.wait()
        for m in range(freqs // 2):
            pair = []
            for f in (2 * m, 2 * m + 1):
                both = side_by_side(basis[f, i, :, :, 0], basis[f, i, :, :, 1])
                pair.append(dot(both, turned[f, i], 1, 0))
            for n, shift in enumerate(shifts):
                for c in range(cols):
                    rank = ranks[2 * m, me * rows + i, (me ^ shift) * cols + c]
                    cut = slice((n * cols + c) * slots, (n * cols + c + 1) * slots)
                    slot = (m * devices + (me ^ shift)) * cols + c
                    pack_rows(stage, slot, i * total, rank, pair[0][cut], pair[1][cut])
    for m in range(freqs // 2):
        unstage(outs, slots_out, stage, m, devices, cols, rows * total, me)


def image_kernel(slots_in, owners, ranks_near, basis, *rest):
    devices = len(slots_in)
    packed = rest[:devices]
    outs = rest[-owners - 5 : -5]
    ranks, stage, coeffs, z, sem = rest[-5:]
    freqs, _, rows, cols, _, slots, tile = basis.shape
    total = slots + slots // 6
    half = coeffs.shape[3] // 2
    quarter = half // owners
    size = rows * total
    me, mine = lax.axis_index("tile"), lax.axis_index("freq")
    rank_copy = pltpu.make_async_copy(ranks_near, ranks, sem)
    rank_copy.start()
    for m in range(freqs // 2):
        for s in range(devices):
            for c in range(cols):
                block = packed[s][m, pl.ds(c * size, size), :]
                stage[(m * devices + s) * cols + c, pl.ds(0, size), :] = block.astype(f32)
    rank_copy.wait()
    for m in range(freqs // 2):
        for c in range(cols):
            for s in range(devices):
                for i in range(rows):
                    row = partner(me, slots_in[s]) * rows + i
                    rank = ranks[0, (m * devices * rows + row) * cols + c]
                    slot = (m * devices + s) * cols + c
                    unpack_rows(stage, slot, i * total, rank, total, coeffs.at[c], row * slots)
            for n in range(2):
                f = 2 * m + n
                both = side_by_side(basis[f, :, :, c, 0], basis[f, :, :, c, 1])
                z[f, :, pl.ds(c * tile, tile)] = plain_product(coeffs[c, n], both)
    for r in range(owners):
        low = pl.multiple_of((mine ^ r) * quarter, quarter)
        for f in range(freqs):
            real = z[f, pl.ds(low, quarter), :]
            imag = z[f, pl.ds(half + low, quarter), :]
            outs[r][f] = jnp.concatenate([real, imag], axis=0).astype(bf16)


def prepare_kernel(rows, cols, ranks_far, mask, table, choice, same, *rest):
    short, high, low, ranks, full, sem = rest[-6:]
    freqs, row_tiles, col_tiles = ranks.shape
    me = lax.axis_index("tile")
    rank_copy = pltpu.make_async_copy(ranks_far, ranks, sem)
    rank_copy.start()
    exact = lax.Precision.HIGHEST
    full[...] = dot(mask[...].astype(f32), table[...], 0, 0, exact)
    quarter, side = same.shape
    mine = full[pl.ds(pl.multiple_of(lax.axis_index("freq") * quarter, quarter), quarter), :]
    entries = dot(mine[:, : choice.shape[0]], choice[...], 1, 0, exact)
    for n in range(side // quarter):
        block = entries[:, n * side : (n + 1) * side] * same[...]
        upper = block.astype(bf16)
        high[n * quarter : (n + 1) * quarter, :] = upper
        low[n * quarter : (n + 1) * quarter, :] = (block - upper.astype(f32)).astype(bf16)
    rank_copy.wait()
    at = 0
    for m in range(freqs // 2):
        for row in range(row_tiles):
            for c in range(cols):
                short[0, at] = ranks[2 * m, row, me * cols + c]
                at += 1
    for m in range(freqs // 2):
        for i in range(rows):
            for col in range(col_tiles):
                short[0, at] = ranks[2 * m, me * rows + i, col]
                at += 1


def mix_kernel(owners, high, low, *rest):
    arrived = rest[:owners][::-1]
    outs = rest[owners : 2 * owners]
    z, w = rest[2 * owners :]
    freqs, rows, span = arrived[0].shape
    mine = lax.axis_index("freq")
    size = freqs * rows
    for r in range(owners):
        z[pl.ds(pl.multiple_of((mine ^ r) * size, 16), size), :] = arrived[r][...].reshape(size, span)
    w[...] = dot(high[...], z[...], 1, 0) + dot(low[...], z[...], 1, 0)
    for r in range(owners):
        block = w[pl.ds(pl.multiple_of((mine ^ r) * size, 16), size), :]
        outs[r][...] = block.reshape(freqs, rows, span).astype(bf16)


def forward_kernel(slots_out, owners, ranks_near, basis, *rest):
    devices = len(slots_out)
    arrived = rest[:owners][::-1]
    outs = rest[owners : owners + devices]
    ranks, w, stage, sem = rest[owners + devices :]
    freqs, _, rows, cols, _, slots, tile = basis.shape
    total = slots + slots // 6
    half = w.shape[2] // 2
    quarter = half // owners
    me, mine = lax.axis_index("tile"), lax.axis_index("freq")
    rank_copy = pltpu.make_async_copy(ranks_near, ranks, sem)
    rank_copy.start()
    for r in range(owners):
        low = pl.multiple_of((mine ^ r) * quarter, quarter)
        for f in range(freqs):
            for c in range(cols):
                at = slice(c * tile, (c + 1) * tile)
                real, imag = arrived[r][f, :quarter, at], arrived[r][f, quarter:, at]
                w[f, c, pl.ds(low, quarter), :tile] = real
                w[f, c, pl.ds(half + low, quarter), :tile] = imag
                w[f, c, pl.ds(low, quarter), tile:] = imag
                w[f, c, pl.ds(half + low, quarter), tile:] = -real
    rank_copy.wait()
    for m in range(freqs // 2):
        for c in range(cols):
            pair = []
            for f in (2 * m, 2 * m + 1):
                both = side_by_side(basis[f, :, :, c, 0], basis[f, :, :, c, 1])
                pair.append(dot(both, w[f, c], 1, 1))
            for d in range(devices):
                for i in range(rows):
                    rank = ranks[0, (m * devices * rows + d * rows + i) * cols + c]
                    cut = slice((d * rows + i) * slots, (d * rows + i + 1) * slots)
                    slot = (m * devices + d) * cols + c
                    pack_rows(stage, slot, i * total, rank, pair[0][cut], pair[1][cut])
        unstage(outs, slots_out, stage, m, devices, cols, rows * total, me)


def result_kernel(slots_in, ranks_near, basis, *rest):
    devices = len(slots_in)
    packed = rest[:devices]
    out, ranks, stage, coeffs, sem = rest[devices:]
    freqs, rows, _, cols, _, slots, tile = basis.shape
    total = slots + slots // 6
    size = rows * total
    before = freqs // 2 * devices * rows * cols
    me = lax.axis_index("tile")
    rank_copy = pltpu.make_async_copy(ranks_near, ranks, sem)
    rank_copy.start()
    for m in range(freqs // 2):
        for s in range(devices):
            for c in range(cols):
                block = packed[s][m, pl.ds(c * size, size), :]
                stage[(m * devices + s) * cols + c, pl.ds(0, size), :] = block.astype(f32)
    rank_copy.wait()
    for m in range(freqs // 2):
        for i in range(rows):
            for s in range(devices):
                for c in range(cols):
                    col = partner(me, slots_in[s]) * cols + c
                    rank = ranks[0, before + (m * rows + i) * devices * cols + col]
                    slot = (m * devices + s) * cols + c
                    unpack_rows(stage, slot, i * total, rank, total, coeffs.at[i], col * slots)
            for n in range(2):
                f = 2 * m + n
                both = side_by_side(basis[f, i, :, :, 0], basis[f, i, :, :, 1])
                r = plain_product(coeffs[i, n], both)
                out[f, pl.ds(i * tile, tile), :] = r.T.astype(bf16)


def send(value, axis, slot):
    if slot[:2] == (0, 0):
        return value
    return lax.ppermute(value, axis, [(d, partner(d, slot)) for d in range(lax.axis_size(axis))])


def spread(values, axis, slots):
    return [(whole, send(value, axis, slot)) for value, slot in zip(values, slots)]


def to_owners(values):
    return spread(values[::-1], "freq", [(n, n, 1) for n in reversed(range(len(values)))])


def local(u_data, u_basis, v_basis, ranks, time_mask):
    freqs, row_count, width = u_data.shape
    rows, col_tiles, _, slots, tile = u_basis.shape[1:]
    row_tiles, cols = v_basis.shape[1:3]
    total = slots // 6 + slots
    pairs = freqs // 2
    devices = lax.axis_size("tile")
    owners = lax.axis_size("freq")
    stage_rows = rows * total + 2 * slots
    quarter = width // 2 // owners
    count = owners * freqs
    side = count * 2 * quarter
    by_cols = u_basis.reshape(freqs, rows, devices, cols, 2, slots, tile)
    by_rows = v_basis.reshape(freqs, devices, rows, cols, 2, slots, tile)
    per_device = [((pairs, cols * rows * total, width), bf16)] * devices
    per_owner = [((freqs, 2 * quarter, cols * tile), bf16)] * owners
    work = {"flops": 4 * row_count * slots * width * col_tiles * freqs * 2, "moved": u_basis.size * 2}
    count_short = pairs * (row_tiles * cols + rows * col_tiles)
    ranks_here = pltpu.SMEM((1, count_short), jnp.int32)
    stage = pltpu.VMEM((pairs * devices * cols, stage_rows, width), f32)
    one = pltpu.SemaphoreType.DMA

    table = lag_tables(count, time_mask.shape[0], 128)
    choice, same = lag_choice(count, quarter)
    def share(partners):
        return {name: value * partners // devices for name, value in work.items()}

    early, late = exchange_slots(devices)
    slots_all = early + late
    data, packed = (far, hold(u_data)), []
    for turn, part in ((1, early), (0, late)):
        partners = len(part)
        made = call(
            functools.partial(adjoint_kernel, part, turn),
            "adjoint",
            [(far, hold(ranks)), (far, hold(by_cols)), data],
            [((pairs, cols * rows * total, width), bf16)] * partners
            + [((freqs, rows, 2 * tile, width), bf16)] * turn,
            [
                pltpu.SMEM(ranks.shape, jnp.int32),
                pltpu.VMEM((freqs, row_count, width), bf16),
                pltpu.VMEM((freqs, rows, partners, cols, 2, slots, tile), bf16),
                stage,
                one((2 + freqs * rows * partners,)),
            ],
            **share(partners),
        )
        if turn:
            data = (whole, made[-1])
        packed += made[:partners]
    short, *window = call(
        functools.partial(prepare_kernel, rows, cols),
        "prepare",
        [(far, hold(ranks))]
        + [(whole, jnp.asarray(x)) for x in (time_mask, table, choice, same)]
        + [(anywhere, packed[-1])],
        [((1, count_short), jnp.int32)] + [((side, side), bf16)] * 2,
        [pltpu.SMEM(ranks.shape, jnp.int32), pltpu.VMEM((width // 2, 128), f32), one],
        specs=[scalars, whole, whole],
        flops=6 * quarter * 2 * count * 2 * count * side,
    )
    images = call(
        functools.partial(image_kernel, slots_all, owners),
        "image",
        [(whole, short), (whole, by_rows)] + spread(packed, "tile", slots_all),
        per_owner,
        [
            ranks_here,
            stage,
            pltpu.VMEM((cols, 2, row_tiles * slots, width), bf16),
            pltpu.VMEM((freqs, width, cols * tile), f32),
            one,
        ],
        **work,
    )
    mixed = call(
        functools.partial(mix_kernel, owners),
        "mix",
        [(whole, x) for x in window] + to_owners(images),
        per_owner,
        [pltpu.VMEM((side, cols * tile), bf16), pltpu.VMEM((side, cols * tile), f32)],
        flops=4 * side * side * cols * tile,
    )
    packed = call(
        functools.partial(forward_kernel, slots_all, owners),
        "forward",
        [(whole, short), (whole, by_rows)] + to_owners(mixed),
        per_device,
        [ranks_here, pltpu.VMEM((freqs, cols, width, 2 * tile), bf16), stage, one],
        **work,
    )
    [out] = call(
        functools.partial(result_kernel, slots_all),
        "result",
        [(whole, short), (whole, by_cols)] + spread(packed, "tile", slots_all),
        [((freqs, row_count, width), bf16)],
        [ranks_here, stage, pltpu.VMEM((rows, 2, col_tiles * slots, width), bf16), one],
        **work,
    )
    return out


def solution(mesh):
    placed = (
        P("freq", "tile", None),
        P("freq", "tile", None, None, None, None),
        P("freq", None, "tile", None, None, None),
        P("freq", None, None),
        P(),
    )
    return jax.shard_map(
        local, mesh=mesh, in_specs=placed, out_specs=P("freq", "tile", None), check_vma=False
    )
```

```python
import functools
import math

import jax
import jax.numpy as jnp
import numpy as np
from jax import lax
from jax.experimental import pallas as pl
from jax.experimental.pallas import tpu as pltpu
from jax.sharding import PartitionSpec as P

vmem_limit = 48 * 1024 * 1024
bf16 = jnp.bfloat16
f32 = jnp.float32

whole = pl.BlockSpec(memory_space=pltpu.VMEM)
scalars = pl.BlockSpec(memory_space=pltpu.SMEM)
far = pl.BlockSpec(memory_space=pltpu.HBM)
anywhere = pl.BlockSpec(memory_space=pl.ANY)


def hold(value):
    return pltpu.with_memory_space_constraint(value, pltpu.HBM)


def call(kernel, name, ins, outs, scratch, flops=0, moved=0, specs=None):
    shapes = [jax.ShapeDtypeStruct(shape, kind) for shape, kind in outs]
    return pl.pallas_call(
        kernel,
        in_specs=[spec for spec, _ in ins],
        out_specs=specs or [whole] * len(outs),
        out_shape=shapes,
        scratch_shapes=scratch,
        compiler_params=pltpu.CompilerParams(vmem_limit_bytes=vmem_limit),
        cost_estimate=pl.CostEstimate(flops=flops, bytes_accessed=moved, transcendentals=0),
        name=name,
    )(*[value for _, value in ins])


def dot(lhs, rhs, lhs_dim, rhs_dim, precision=None):
    return lax.dot_general(
        lhs, rhs, (((lhs_dim,), (rhs_dim,)), ((), ())),
        precision=precision, preferred_element_type=f32,
    )


def lag_tables(count, time_count, lanes):
    samples = np.arange(time_count)[:, None]
    lags = np.arange(count)[None, :]
    angle = 2.0 * math.pi / time_count * ((samples * lags) % time_count)
    table = np.zeros((time_count, lanes), np.float32)
    table[:, :count] = np.cos(angle) / time_count
    table[:, count : 2 * count] = np.sin(angle) / time_count
    return table


def lag_choice(count, quarter):
    side = count * 2 * quarter
    choice = np.zeros((2 * count, count, 2, count, 2, quarter), np.float32)
    for f in range(count):
        for g in range(count):
            sign = 1.0 if g >= f else -1.0
            lag = abs(g - f)
            choice[lag, f, 0, g, 0] = 1.0
            choice[lag, f, 1, g, 1] = 1.0
            choice[count + lag, f, 0, g, 1] = -sign
            choice[count + lag, f, 1, g, 0] = sign
    same = np.arange(quarter)[:, None] == np.arange(side)[None, :] % quarter
    return choice.reshape(2 * count, 2 * count * side), same.astype(np.float32)


def pack_rows(stage, slot, row, rank, first, second):
    size = first.shape[0]
    stage[slot, pl.ds(row, size), :] = first
    stage[slot, pl.ds(row + rank, size), :] = second


def unpack_rows(stage, slot, row, rank, total, coeffs, base):
    slots = total - total // 7
    first = stage[slot, pl.ds(row, slots), :]
    second = stage[slot, pl.ds(row + rank, slots), :]
    ids = lax.broadcasted_iota(jnp.int32, first.shape, 0)
    at = pl.ds(pl.multiple_of(base, 16), slots)
    coeffs[0, at, :] = jnp.where(ids < rank, first, 0.0).astype(bf16)
    coeffs[1, at, :] = jnp.where(ids < total - rank, second, 0.0).astype(bf16)


def side_by_side(real, imag):
    flat = (-1, real.shape[-1])
    return jnp.concatenate([real.reshape(flat), imag.reshape(flat)], axis=1)


def plain_product(coeffs, both):
    half, tile = coeffs.shape[1] // 2, both.shape[1] // 2
    product = dot(coeffs, both, 0, 0)
    lead, trail = product[:, :tile], product[:, tile:]
    return jnp.concatenate([lead[:half] - trail[half:], lead[half:] + trail[:half]], axis=0)


def parity(value, mask):
    odd = value & 0
    bit = 0
    while mask >> bit:
        if (mask >> bit) & 1:
            odd = odd ^ ((value >> bit) & 1)
        bit += 1
    return odd


def exchange_slots(devices):
    half = devices // 2
    spare, mixed = list(range(half, devices)), []
    alone = []
    for near in reversed(range(2, half)):
        found = [
            (far, mask)
            for far in spare
            for mask in range(3, devices, 2)
            if not parity(near, mask) and not parity(far, mask)
        ]
        if found and len(spare) > 2:
            far, mask = found[0]
            spare.remove(far)
            mixed += [(far, near, mask), (near, far, mask)]
        else:
            alone.append((near, near, 1))
    first = [(far, far, 1) for far in reversed(spare)]
    return first, mixed + alone + [(1, 1, 1)] * (devices > 1) + [(0, 0, 1)]


def partner(me, slot):
    even, odd, mask = slot
    if even == odd:
        return me ^ even
    return me ^ (even ^ (parity(me, mask) * (even ^ odd)))


def owner_slots(owners):
    mixed = [(1, 2), (2, 1)] if owners > 2 else [(n, n) for n in range(1, owners)]
    return [(n, n) for n in reversed(range(3, owners))] + mixed + [(0, 0)]


def owner(mine, me, slot):
    even, odd = slot
    return mine ^ even if even == odd else mine ^ (even ^ ((me & 1) * (even ^ odd)))


def unstage(outs, slots_out, stage, m, devices, span, size, me):
    for out, slot in zip(outs, slots_out):
        for c in range(span):
            rows = stage[(m * devices + partner(me, slot)) * span + c, pl.ds(0, size), :]
            out[m, pl.ds(c * size, size), :] = rows.astype(bf16)


def adjoint_kernel(slots_out, turn, ranks_far, basis_far, u_far, *rest):
    shifts = sorted({n for slot in slots_out for n in slot[:2]})
    ranks, u_ref, basis, stage, sems = rest[-5:]
    outs = rest[-5 - len(slots_out) - turn : -5 - turn]
    turned = rest[-6] if turn else u_far
    freqs, rows, devices, cols, _, slots, tile = basis_far.shape
    total = slots + slots // 6
    half = turned.shape[3] // 2
    me = lax.axis_index("tile")
    rank_copy = pltpu.make_async_copy(ranks_far, ranks, sems.at[0])
    if turn:
        data_copy = pltpu.make_async_copy(u_far, u_ref, sems.at[1])
        data_copy.start()
    rank_copy.start()
    copies = [[] for _ in range(rows)]
    for i in range(rows):
        for f in range(freqs):
            for n, shift in enumerate(shifts):
                copy = pltpu.make_async_copy(
                    basis_far.at[f, i, me ^ shift],
                    basis.at[f, i, n],
                    sems.at[2 + (i * freqs + f) * len(shifts) + n],
                )
                copy.start(priority=n % 2)
                copies[i].append(copy)
    if turn:
        data_copy.wait()
        for f in range(freqs):
            for i in range(rows):
                values = u_ref[f, i * tile : (i + 1) * tile, :]
                wide = values.astype(f32)
                lane = lax.broadcasted_iota(jnp.int32, wide.shape, 1)
                rolled = pltpu.roll(wide, half, 1)
                turned[f, i, :tile, :] = values
                turned[f, i, tile:, :] = jnp.where(lane < half, rolled, -rolled).astype(bf16)
    rank_copy.wait()
    for i in range(rows):
        for copy in copies[i]:
            copy.wait()
        for m in range(freqs // 2):
            pair = []
            for f in (2 * m, 2 * m + 1):
                both = side_by_side(basis[f, i, :, :, 0], basis[f, i, :, :, 1])
                pair.append(dot(both, turned[f, i], 1, 0))
            for n, shift in enumerate(shifts):
                for c in range(cols):
                    rank = ranks[2 * m, me * rows + i, (me ^ shift) * cols + c]
                    cut = slice((n * cols + c) * slots, (n * cols + c + 1) * slots)
                    slot = (m * devices + (me ^ shift)) * cols + c
                    pack_rows(stage, slot, i * total, rank, pair[0][cut], pair[1][cut])
    for m in range(freqs // 2):
        unstage(outs, slots_out, stage, m, devices, cols, rows * total, me)


def image_kernel(slots_in, owners, ranks_near, basis, *rest):
    devices = len(slots_in)
    packed = rest[:devices]
    outs = rest[-owners - 5 : -5]
    ranks, stage, coeffs, z, sem = rest[-5:]
    freqs, _, rows, cols, _, slots, tile = basis.shape
    total = slots + slots // 6
    half = coeffs.shape[3] // 2
    quarter = half // owners
    size = rows * total
    me, mine = lax.axis_index("tile"), lax.axis_index("freq")
    rank_copy = pltpu.make_async_copy(ranks_near, ranks, sem)
    rank_copy.start()
    for m in range(freqs // 2):
        for s in range(devices):
            for c in range(cols):
                block = packed[s][m, pl.ds(c * size, size), :]
                stage[(m * devices + s) * cols + c, pl.ds(0, size), :] = block.astype(f32)
    rank_copy.wait()
    for m in range(freqs // 2):
        for c in range(cols):
            for s in range(devices):
                for i in range(rows):
                    row = partner(me, slots_in[s]) * rows + i
                    rank = ranks[0, (m * devices * rows + row) * cols + c]
                    slot = (m * devices + s) * cols + c
                    unpack_rows(stage, slot, i * total, rank, total, coeffs.at[c], row * slots)
            for n in range(2):
                f = 2 * m + n
                both = side_by_side(basis[f, :, :, c, 0], basis[f, :, :, c, 1])
                z[f, :, pl.ds(c * tile, tile)] = plain_product(coeffs[c, n], both)
    for r, slot in enumerate(owner_slots(owners)):
        low = pl.multiple_of(owner(mine, me, slot) * quarter, quarter)
        for f in range(freqs):
            real = z[f, pl.ds(low, quarter), :]
            imag = z[f, pl.ds(half + low, quarter), :]
            outs[r][f] = jnp.concatenate([real, imag], axis=0).astype(bf16)


def prepare_kernel(rows, cols, ranks_far, mask, table, choice, same, *rest):
    short, high, low, ranks, full, sem = rest[-6:]
    freqs, row_tiles, col_tiles = ranks.shape
    me = lax.axis_index("tile")
    rank_copy = pltpu.make_async_copy(ranks_far, ranks, sem)
    rank_copy.start()
    exact = lax.Precision.HIGHEST
    full[...] = dot(mask[...].astype(f32), table[...], 0, 0, exact)
    quarter, side = same.shape
    mine = full[pl.ds(pl.multiple_of(lax.axis_index("freq") * quarter, quarter), quarter), :]
    entries = dot(mine[:, : choice.shape[0]], choice[...], 1, 0, exact)
    for n in range(side // quarter):
        block = entries[:, n * side : (n + 1) * side] * same[...]
        upper = block.astype(bf16)
        high[n * quarter : (n + 1) * quarter, :] = upper
        low[n * quarter : (n + 1) * quarter, :] = (block - upper.astype(f32)).astype(bf16)
    rank_copy.wait()
    at = 0
    for m in range(freqs // 2):
        for row in range(row_tiles):
            for c in range(cols):
                short[0, at] = ranks[2 * m, row, me * cols + c]
                at += 1
    for m in range(freqs // 2):
        for i in range(rows):
            for col in range(col_tiles):
                short[0, at] = ranks[2 * m, me * rows + i, col]
                at += 1


def mix_kernel(owners, high, low, *rest):
    arrived = rest[:owners]
    outs = rest[owners : 2 * owners]
    z, w = rest[2 * owners :]
    freqs, rows, span = arrived[0].shape
    me, mine = lax.axis_index("tile"), lax.axis_index("freq")
    size = freqs * rows
    places = [pl.multiple_of(owner(mine, me, slot) * size, 16) for slot in owner_slots(owners)]
    for r in range(owners):
        z[pl.ds(places[r], size), :] = arrived[r][...].reshape(size, span)
    w[...] = dot(high[...], z[...], 1, 0) + dot(low[...], z[...], 1, 0)
    for r in range(owners):
        block = w[pl.ds(places[r], size), :]
        outs[r][...] = block.reshape(freqs, rows, span).astype(bf16)


def forward_kernel(slots_out, owners, ranks_near, basis, *rest):
    devices = len(slots_out)
    arrived = rest[:owners]
    outs = rest[owners : owners + devices]
    ranks, w, stage, sem = rest[owners + devices :]
    freqs, _, rows, cols, _, slots, tile = basis.shape
    total = slots + slots // 6
    half = w.shape[2] // 2
    quarter = half // owners
    me, mine = lax.axis_index("tile"), lax.axis_index("freq")
    rank_copy = pltpu.make_async_copy(ranks_near, ranks, sem)
    rank_copy.start()
    for r, slot in enumerate(owner_slots(owners)):
        low = pl.multiple_of(owner(mine, me, slot) * quarter, quarter)
        for f in range(freqs):
            for c in range(cols):
                at = slice(c * tile, (c + 1) * tile)
                real, imag = arrived[r][f, :quarter, at], arrived[r][f, quarter:, at]
                w[f, c, pl.ds(low, quarter), :tile] = real
                w[f, c, pl.ds(half + low, quarter), :tile] = imag
                w[f, c, pl.ds(low, quarter), tile:] = imag
                w[f, c, pl.ds(half + low, quarter), tile:] = -real
    rank_copy.wait()
    for m in range(freqs // 2):
        for c in range(cols):
            pair = []
            for f in (2 * m, 2 * m + 1):
                both = side_by_side(basis[f, :, :, c, 0], basis[f, :, :, c, 1])
                pair.append(dot(both, w[f, c], 1, 1))
            for d in range(devices):
                for i in range(rows):
                    rank = ranks[0, (m * devices * rows + d * rows + i) * cols + c]
                    cut = slice((d * rows + i) * slots, (d * rows + i + 1) * slots)
                    slot = (m * devices + d) * cols + c
                    pack_rows(stage, slot, i * total, rank, pair[0][cut], pair[1][cut])
        unstage(outs, slots_out, stage, m, devices, cols, rows * total, me)


def result_kernel(slots_in, ranks_near, basis, *rest):
    devices = len(slots_in)
    packed = rest[:devices]
    out, ranks, stage, coeffs, sem = rest[devices:]
    freqs, rows, _, cols, _, slots, tile = basis.shape
    total = slots + slots // 6
    size = rows * total
    before = freqs // 2 * devices * rows * cols
    me = lax.axis_index("tile")
    rank_copy = pltpu.make_async_copy(ranks_near, ranks, sem)
    rank_copy.start()
    for m in range(freqs // 2):
        for s in range(devices):
            for c in range(cols):
                block = packed[s][m, pl.ds(c * size, size), :]
                stage[(m * devices + s) * cols + c, pl.ds(0, size), :] = block.astype(f32)
    rank_copy.wait()
    for m in range(freqs // 2):
        for i in range(rows):
            for s in range(devices):
                for c in range(cols):
                    col = partner(me, slots_in[s]) * cols + c
                    rank = ranks[0, before + (m * rows + i) * devices * cols + col]
                    slot = (m * devices + s) * cols + c
                    unpack_rows(stage, slot, i * total, rank, total, coeffs.at[i], col * slots)
            for n in range(2):
                f = 2 * m + n
                both = side_by_side(basis[f, i, :, :, 0], basis[f, i, :, :, 1])
                r = plain_product(coeffs[i, n], both)
                out[f, pl.ds(i * tile, tile), :] = r.T.astype(bf16)


def send(value, axis, slot):
    if slot[:2] == (0, 0):
        return value
    return lax.ppermute(value, axis, [(d, partner(d, slot)) for d in range(lax.axis_size(axis))])


def spread(values, axis, slots):
    return [(whole, send(value, axis, slot)) for value, slot in zip(values, slots)]


def to_owners(values):
    owners, devices = lax.axis_size("freq"), lax.axis_size("tile")
    landed = []
    for value, slot in zip(values, owner_slots(owners)):
        if slot != (0, 0):
            pairs = [
                (mine * devices + me, owner(mine, me, slot) * devices + me)
                for mine in range(owners)
                for me in range(devices)
            ]
            value = lax.ppermute(value, ("freq", "tile"), pairs)
        landed.append((whole, value))
    return landed


def local(u_data, u_basis, v_basis, ranks, time_mask):
    freqs, row_count, width = u_data.shape
    rows, col_tiles, _, slots, tile = u_basis.shape[1:]
    row_tiles, cols = v_basis.shape[1:3]
    total = slots // 6 + slots
    pairs = freqs // 2
    devices = lax.axis_size("tile")
    owners = lax.axis_size("freq")
    stage_rows = rows * total + 2 * slots
    quarter = width // 2 // owners
    count = owners * freqs
    side = count * 2 * quarter
    by_cols = u_basis.reshape(freqs, rows, devices, cols, 2, slots, tile)
    by_rows = v_basis.reshape(freqs, devices, rows, cols, 2, slots, tile)
    per_device = [((pairs, cols * rows * total, width), bf16)] * devices
    per_owner = [((freqs, 2 * quarter, cols * tile), bf16)] * owners
    work = {"flops": 4 * row_count * slots * width * col_tiles * freqs * 2, "moved": u_basis.size * 2}
    count_short = pairs * (row_tiles * cols + rows * col_tiles)
    ranks_here = pltpu.SMEM((1, count_short), jnp.int32)
    stage = pltpu.VMEM((pairs * devices * cols, stage_rows, width), f32)
    one = pltpu.SemaphoreType.DMA

    table = lag_tables(count, time_mask.shape[0], 128)
    choice, same = lag_choice(count, quarter)
    def share(partners):
        return {name: value * partners // devices for name, value in work.items()}

    early, late = exchange_slots(devices)
    slots_all = early + late
    data, packed = (far, hold(u_data)), []
    for turn, part in ((1, early), (0, late)):
        partners = len(part)
        made = call(
            functools.partial(adjoint_kernel, part, turn),
            "adjoint",
            [(far, hold(ranks)), (far, hold(by_cols)), data],
            [((pairs, cols * rows * total, width), bf16)] * partners
            + [((freqs, rows, 2 * tile, width), bf16)] * turn,
            [
                pltpu.SMEM(ranks.shape, jnp.int32),
                pltpu.VMEM((freqs, row_count, width), bf16),
                pltpu.VMEM((freqs, rows, partners, cols, 2, slots, tile), bf16),
                stage,
                one((2 + freqs * rows * partners,)),
            ],
            **share(partners),
        )
        if turn:
            data = (whole, made[-1])
        packed += made[:partners]
    short, *window = call(
        functools.partial(prepare_kernel, rows, cols),
        "prepare",
        [(far, hold(ranks))]
        + [(whole, jnp.asarray(x)) for x in (time_mask, table, choice, same)]
        + [(anywhere, packed[-1])],
        [((1, count_short), jnp.int32)] + [((side, side), bf16)] * 2,
        [pltpu.SMEM(ranks.shape, jnp.int32), pltpu.VMEM((width // 2, 128), f32), one],
        specs=[scalars, whole, whole],
        flops=6 * quarter * 2 * count * 2 * count * side,
    )
    images = call(
        functools.partial(image_kernel, slots_all, owners),
        "image",
        [(whole, short), (whole, by_rows)] + spread(packed, "tile", slots_all),
        per_owner,
        [
            ranks_here,
            stage,
            pltpu.VMEM((cols, 2, row_tiles * slots, width), bf16),
            pltpu.VMEM((freqs, width, cols * tile), f32),
            one,
        ],
        **work,
    )
    mixed = call(
        functools.partial(mix_kernel, owners),
        "mix",
        [(whole, x) for x in window] + to_owners(images),
        per_owner,
        [pltpu.VMEM((side, cols * tile), bf16), pltpu.VMEM((side, cols * tile), f32)],
        flops=4 * side * side * cols * tile,
    )
    packed = call(
        functools.partial(forward_kernel, slots_all, owners),
        "forward",
        [(whole, short), (whole, by_rows)] + to_owners(mixed),
        per_device,
        [ranks_here, pltpu.VMEM((freqs, cols, width, 2 * tile), bf16), stage, one],
        **work,
    )
    [out] = call(
        functools.partial(result_kernel, slots_all),
        "result",
        [(whole, short), (whole, by_cols)] + spread(packed, "tile", slots_all),
        [((freqs, row_count, width), bf16)],
        [ranks_here, stage, pltpu.VMEM((rows, 2, col_tiles * slots, width), bf16), one],
        **work,
    )
    return out


def solution(mesh):
    placed = (
        P("freq", "tile", None),
        P("freq", "tile", None, None, None, None),
        P("freq", None, "tile", None, None, None),
        P("freq", None, None),
        P(),
    )
    return jax.shard_map(
        local, mesh=mesh, in_specs=placed, out_specs=P("freq", "tile", None), check_vma=False
    )
```

```python
import functools
import math

import jax
import jax.numpy as jnp
import numpy as np
from jax import lax
from jax.experimental import pallas as pl
from jax.experimental.pallas import tpu as pltpu
from jax.sharding import PartitionSpec as P

vmem_limit = 48 * 1024 * 1024
bf16 = jnp.bfloat16
f32 = jnp.float32

whole = pl.BlockSpec(memory_space=pltpu.VMEM)
scalars = pl.BlockSpec(memory_space=pltpu.SMEM)
far = pl.BlockSpec(memory_space=pltpu.HBM)
anywhere = pl.BlockSpec(memory_space=pl.ANY)


def hold(value):
    return pltpu.with_memory_space_constraint(value, pltpu.HBM)


def call(kernel, name, ins, outs, scratch, flops=0, moved=0, specs=None):
    shapes = [jax.ShapeDtypeStruct(shape, kind) for shape, kind in outs]
    return pl.pallas_call(
        kernel,
        in_specs=[spec for spec, _ in ins],
        out_specs=specs or [whole] * len(outs),
        out_shape=shapes,
        scratch_shapes=scratch,
        compiler_params=pltpu.CompilerParams(vmem_limit_bytes=vmem_limit),
        cost_estimate=pl.CostEstimate(flops=flops, bytes_accessed=moved, transcendentals=0),
        name=name,
    )(*[value for _, value in ins])


def dot(lhs, rhs, lhs_dim, rhs_dim, precision=None):
    return lax.dot_general(
        lhs, rhs, (((lhs_dim,), (rhs_dim,)), ((), ())),
        precision=precision, preferred_element_type=f32,
    )


def lag_tables(count, time_count, lanes):
    samples = np.arange(time_count)[:, None]
    lags = np.arange(count)[None, :]
    angle = 2.0 * math.pi / time_count * ((samples * lags) % time_count)
    table = np.zeros((time_count, lanes), np.float32)
    table[:, :count] = np.cos(angle) / time_count
    table[:, count : 2 * count] = np.sin(angle) / time_count
    return table


def lag_choice(count, quarter):
    side = count * 2 * quarter
    choice = np.zeros((2 * count, count, 2, count, 2, quarter), np.float32)
    for f in range(count):
        for g in range(count):
            sign = 1.0 if g >= f else -1.0
            lag = abs(g - f)
            choice[lag, f, 0, g, 0] = 1.0
            choice[lag, f, 1, g, 1] = 1.0
            choice[count + lag, f, 0, g, 1] = -sign
            choice[count + lag, f, 1, g, 0] = sign
    same = np.arange(quarter)[:, None] == np.arange(side)[None, :] % quarter
    return choice.reshape(2 * count, 2 * count * side), same.astype(np.float32)


def pack_rows(stage, slot, row, rank, first, second):
    size = first.shape[0]
    stage[slot, pl.ds(row, size), :] = first
    stage[slot, pl.ds(row + rank, size), :] = second


def unpack_rows(stage, slot, row, rank, total, coeffs, base):
    slots = total - total // 7
    first = stage[slot, pl.ds(row, slots), :]
    second = stage[slot, pl.ds(row + rank, slots), :]
    ids = lax.broadcasted_iota(jnp.int32, first.shape, 0)
    at = pl.ds(pl.multiple_of(base, 16), slots)
    coeffs[0, at, :] = jnp.where(ids < rank, first, 0.0).astype(bf16)
    coeffs[1, at, :] = jnp.where(ids < total - rank, second, 0.0).astype(bf16)


def side_by_side(real, imag):
    flat = (-1, real.shape[-1])
    return jnp.concatenate([real.reshape(flat), imag.reshape(flat)], axis=1)


def plain_product(coeffs, both):
    half, tile = coeffs.shape[1] // 2, both.shape[1] // 2
    product = dot(coeffs, both, 0, 0)
    lead, trail = product[:, :tile], product[:, tile:]
    return jnp.concatenate([lead[:half] - trail[half:], lead[half:] + trail[:half]], axis=0)


def parity(value, mask):
    odd = value & 0
    bit = 0
    while mask >> bit:
        if (mask >> bit) & 1:
            odd = odd ^ ((value >> bit) & 1)
        bit += 1
    return odd


def exchange_slots(devices):
    half = devices // 2
    spare, mixed = list(range(half, devices)), []
    alone = []
    for near in reversed(range(2, half)):
        found = [
            (far, mask)
            for far in spare
            for mask in range(3, devices, 2)
            if not parity(near, mask) and not parity(far, mask)
        ]
        if found and len(spare) > 2:
            far, mask = found[0]
            spare.remove(far)
            mixed += [(far, near, mask), (near, far, mask)]
        else:
            alone.append((near, near, 1))
    first = [(far, far, 1) for far in reversed(spare)]
    return first, mixed + alone + [(1, 1, 1)] * (devices > 1) + [(0, 0, 1)]


def partner(me, slot):
    even, odd, mask = slot
    if even == odd:
        return me ^ even
    return me ^ (even ^ (parity(me, mask) * (even ^ odd)))


def owner_slots(owners):
    mixed = [(1, 2), (2, 1)] if owners > 2 else [(n, n) for n in range(1, owners)]
    return [(n, n) for n in reversed(range(3, owners))] + mixed + [(0, 0)]


def owner(mine, me, slot):
    even, odd = slot
    return mine ^ even if even == odd else mine ^ (even ^ ((me & 1) * (even ^ odd)))


def unstage(outs, slots_out, stage, m, devices, span, size, me):
    for out, slot in zip(outs, slots_out):
        for c in range(span):
            rows = stage[(m * devices + partner(me, slot)) * span + c, pl.ds(0, size), :]
            out[m, pl.ds(c * size, size), :] = rows.astype(bf16)


def adjoint_part(slots_out, first_rank, ranks, turned, basis, outs, stage, waits):
    shifts = sorted({n for slot in slots_out for n in slot[:2]})
    freqs, rows, devices, cols, _, slots, tile = basis.shape
    total = slots + slots // 6
    me = lax.axis_index("tile")
    for i in range(rows):
        for copy in waits[i]:
            copy.wait()
        for m in range(freqs // 2):
            pair = []
            for f in (2 * m, 2 * m + 1):
                real = jnp.concatenate([basis[f, i, me ^ n, :, 0] for n in shifts], axis=0)
                imag = jnp.concatenate([basis[f, i, me ^ n, :, 1] for n in shifts], axis=0)
                pair.append(dot(side_by_side(real, imag), turned[f, i], 1, 0))
            for n, shift in enumerate(shifts):
                for c in range(cols):
                    col = (me ^ shift) * cols + c
                    rank = ranks[0, first_rank + (m * rows + i) * devices * cols + col]
                    cut = slice((n * cols + c) * slots, (n * cols + c + 1) * slots)
                    pack_rows(stage, m * devices * cols + col, i * total, rank, pair[0][cut], pair[1][cut])
    for m in range(freqs // 2):
        unstage(outs, slots_out, stage, m, devices, cols, rows * total, me)


def adjoint_kernel(slots_out, cols, ranks_far, u_far, basis_far, *rest):
    outs = rest[: len(slots_out)]
    turned, basis, short_out, ranks, short, u_ref, stage, sems = rest[len(slots_out) :]
    freqs, rows, devices, _, _, slots, tile = basis.shape
    row_tiles, col_tiles = ranks.shape[1:]
    half = turned.shape[3] // 2
    me = lax.axis_index("tile")
    shifts = sorted({n for slot in slots_out for n in slot[:2]})
    rank_copy = pltpu.make_async_copy(ranks_far, ranks, sems.at[0])
    data_copy = pltpu.make_async_copy(u_far, u_ref, sems.at[1])
    data_copy.start()
    rank_copy.start()
    early, late, at = [[] for _ in range(rows)], [], 3
    for group in (shifts, [n for n in range(devices) if n not in shifts]):
        for i in range(rows):
            for f in range(freqs):
                for n in group:
                    copy = pltpu.make_async_copy(
                        basis_far.at[f, i, me ^ n], basis.at[f, i, me ^ n], sems.at[at]
                    )
                    at += 1
                    copy.start(priority=n % 2)
                    (early[i] if group is shifts else late).append(copy)
    rank_copy.wait()
    first_rank = freqs // 2 * row_tiles * cols
    for m in range(freqs // 2):
        for row in range(row_tiles):
            for c in range(cols):
                short[0, (m * row_tiles + row) * cols + c] = ranks[2 * m, row, me * cols + c]
        for i in range(rows):
            for col in range(col_tiles):
                short[0, first_rank + (m * rows + i) * col_tiles + col] = ranks[2 * m, me * rows + i, col]
    short_copy = pltpu.make_async_copy(short, short_out, sems.at[2])
    short_copy.start()
    data_copy.wait()
    for f in range(freqs):
        for i in range(rows):
            values = u_ref[f, i * tile : (i + 1) * tile, :]
            wide = values.astype(f32)
            lane = lax.broadcasted_iota(jnp.int32, wide.shape, 1)
            rolled = pltpu.roll(wide, half, 1)
            turned[f, i, :tile, :] = values
            turned[f, i, tile:, :] = jnp.where(lane < half, rolled, -rolled).astype(bf16)
    adjoint_part(slots_out, first_rank, short, turned, basis, outs, stage, early)
    short_copy.wait()
    for copy in late:
        copy.wait()


def adjoint_rest_kernel(slots_out, first_rank, short, turned, basis, *rest):
    outs = rest[: len(slots_out)]
    ranks, stage, sem = rest[len(slots_out) :]
    rank_copy = pltpu.make_async_copy(short, ranks, sem)
    rank_copy.start()
    waits = [[rank_copy]] + [[]] * (basis.shape[1] - 1)
    adjoint_part(slots_out, first_rank, ranks, turned, basis, outs, stage, waits)


def image_kernel(slots_in, owners, ranks_near, basis, *rest):
    devices = len(slots_in)
    packed = rest[:devices]
    outs = rest[-owners - 5 : -5]
    ranks, stage, coeffs, z, sem = rest[-5:]
    freqs, _, rows, cols, _, slots, tile = basis.shape
    total = slots + slots // 6
    half = coeffs.shape[3] // 2
    quarter = half // owners
    size = rows * total
    me, mine = lax.axis_index("tile"), lax.axis_index("freq")
    rank_copy = pltpu.make_async_copy(ranks_near, ranks, sem)
    rank_copy.start()
    for m in range(freqs // 2):
        for s in range(devices):
            for c in range(cols):
                block = packed[s][m, pl.ds(c * size, size), :]
                stage[(m * devices + s) * cols + c, pl.ds(0, size), :] = block.astype(f32)
    rank_copy.wait()
    for m in range(freqs // 2):
        for c in range(cols):
            for s in range(devices):
                for i in range(rows):
                    row = partner(me, slots_in[s]) * rows + i
                    rank = ranks[0, (m * devices * rows + row) * cols + c]
                    slot = (m * devices + s) * cols + c
                    unpack_rows(stage, slot, i * total, rank, total, coeffs.at[c], row * slots)
            for n in range(2):
                f = 2 * m + n
                both = side_by_side(basis[f, :, :, c, 0], basis[f, :, :, c, 1])
                z[f, :, pl.ds(c * tile, tile)] = plain_product(coeffs[c, n], both)
    for r, slot in enumerate(owner_slots(owners)):
        low = pl.multiple_of(owner(mine, me, slot) * quarter, quarter)
        for f in range(freqs):
            real = z[f, pl.ds(low, quarter), :]
            imag = z[f, pl.ds(half + low, quarter), :]
            outs[r][f] = jnp.concatenate([real, imag], axis=0).astype(bf16)


def prepare_kernel(basis_far, mask, table, choice, same, *rest):
    basis, high, low, full, sem = rest[-5:]
    basis_copy = pltpu.make_async_copy(basis_far, basis, sem)
    basis_copy.start()
    exact = lax.Precision.HIGHEST
    full[...] = dot(mask[...].astype(f32), table[...], 0, 0, exact)
    quarter, side = same.shape
    mine = full[pl.ds(pl.multiple_of(lax.axis_index("freq") * quarter, quarter), quarter), :]
    entries = dot(mine[:, : choice.shape[0]], choice[...], 1, 0, exact)
    for n in range(side // quarter):
        block = entries[:, n * side : (n + 1) * side] * same[...]
        upper = block.astype(bf16)
        high[n * quarter : (n + 1) * quarter, :] = upper
        low[n * quarter : (n + 1) * quarter, :] = (block - upper.astype(f32)).astype(bf16)
    basis_copy.wait()


def mix_kernel(owners, high, low, *rest):
    arrived = rest[:owners]
    outs = rest[owners : 2 * owners]
    z, w = rest[2 * owners :]
    freqs, rows, span = arrived[0].shape
    me, mine = lax.axis_index("tile"), lax.axis_index("freq")
    size = freqs * rows
    places = [pl.multiple_of(owner(mine, me, slot) * size, 16) for slot in owner_slots(owners)]
    for r in range(owners):
        z[pl.ds(places[r], size), :] = arrived[r][...].reshape(size, span)
    w[...] = dot(high[...], z[...], 1, 0) + dot(low[...], z[...], 1, 0)
    for r in range(owners):
        block = w[pl.ds(places[r], size), :]
        outs[r][...] = block.reshape(freqs, rows, span).astype(bf16)


def forward_kernel(slots_out, owners, ranks_near, basis, *rest):
    devices = len(slots_out)
    arrived = rest[:owners]
    outs = rest[owners : owners + devices]
    ranks, w, stage, sem = rest[owners + devices :]
    freqs, _, rows, cols, _, slots, tile = basis.shape
    total = slots + slots // 6
    half = w.shape[2] // 2
    quarter = half // owners
    me, mine = lax.axis_index("tile"), lax.axis_index("freq")
    rank_copy = pltpu.make_async_copy(ranks_near, ranks, sem)
    rank_copy.start()
    for r, slot in enumerate(owner_slots(owners)):
        low = pl.multiple_of(owner(mine, me, slot) * quarter, quarter)
        for f in range(freqs):
            for c in range(cols):
                at = slice(c * tile, (c + 1) * tile)
                real, imag = arrived[r][f, :quarter, at], arrived[r][f, quarter:, at]
                w[f, c, pl.ds(low, quarter), :tile] = real
                w[f, c, pl.ds(half + low, quarter), :tile] = imag
                w[f, c, pl.ds(low, quarter), tile:] = imag
                w[f, c, pl.ds(half + low, quarter), tile:] = -real
    rank_copy.wait()
    for m in range(freqs // 2):
        for c in range(cols):
            pair = []
            for f in (2 * m, 2 * m + 1):
                both = side_by_side(basis[f, :, :, c, 0], basis[f, :, :, c, 1])
                pair.append(dot(both, w[f, c], 1, 1))
            for d in range(devices):
                for i in range(rows):
                    rank = ranks[0, (m * devices * rows + d * rows + i) * cols + c]
                    cut = slice((d * rows + i) * slots, (d * rows + i + 1) * slots)
                    slot = (m * devices + d) * cols + c
                    pack_rows(stage, slot, i * total, rank, pair[0][cut], pair[1][cut])
        unstage(outs, slots_out, stage, m, devices, cols, rows * total, me)


def result_kernel(slots_in, ranks_near, basis, *rest):
    devices = len(slots_in)
    packed = rest[:devices]
    out, ranks, stage, coeffs, sem = rest[devices:]
    freqs, rows, _, cols, _, slots, tile = basis.shape
    total = slots + slots // 6
    size = rows * total
    before = freqs // 2 * devices * rows * cols
    me = lax.axis_index("tile")
    rank_copy = pltpu.make_async_copy(ranks_near, ranks, sem)
    rank_copy.start()
    for m in range(freqs // 2):
        for s in range(devices):
            for c in range(cols):
                block = packed[s][m, pl.ds(c * size, size), :]
                stage[(m * devices + s) * cols + c, pl.ds(0, size), :] = block.astype(f32)
    rank_copy.wait()
    for m in range(freqs // 2):
        for i in range(rows):
            for s in range(devices):
                for c in range(cols):
                    col = partner(me, slots_in[s]) * cols + c
                    rank = ranks[0, before + (m * rows + i) * devices * cols + col]
                    slot = (m * devices + s) * cols + c
                    unpack_rows(stage, slot, i * total, rank, total, coeffs.at[i], col * slots)
            for n in range(2):
                f = 2 * m + n
                both = side_by_side(basis[f, i, :, :, 0], basis[f, i, :, :, 1])
                r = plain_product(coeffs[i, n], both)
                out[f, pl.ds(i * tile, tile), :] = r.T.astype(bf16)


def send(value, axis, slot):
    if slot[:2] == (0, 0):
        return value
    return lax.ppermute(value, axis, [(d, partner(d, slot)) for d in range(lax.axis_size(axis))])


def spread(values, axis, slots):
    return [(whole, send(value, axis, slot)) for value, slot in zip(values, slots)]


def to_owners(values):
    owners, devices = lax.axis_size("freq"), lax.axis_size("tile")
    landed = []
    for value, slot in zip(values, owner_slots(owners)):
        if slot != (0, 0):
            pairs = [
                (mine * devices + me, owner(mine, me, slot) * devices + me)
                for mine in range(owners)
                for me in range(devices)
            ]
            value = lax.ppermute(value, ("freq", "tile"), pairs)
        landed.append((whole, value))
    return landed


def local(u_data, u_basis, v_basis, ranks, time_mask):
    freqs, row_count, width = u_data.shape
    rows, col_tiles, _, slots, tile = u_basis.shape[1:]
    row_tiles, cols = v_basis.shape[1:3]
    total = slots // 6 + slots
    pairs = freqs // 2
    devices = lax.axis_size("tile")
    owners = lax.axis_size("freq")
    stage_rows = rows * total + 2 * slots
    quarter = width // 2 // owners
    count = owners * freqs
    side = count * 2 * quarter
    by_cols = u_basis.reshape(freqs, rows, devices, cols, 2, slots, tile)
    by_rows = v_basis.reshape(freqs, devices, rows, cols, 2, slots, tile)
    packed_kind = ((pairs, cols * rows * total, width), bf16)
    per_device = [packed_kind] * devices
    per_owner = [((freqs, 2 * quarter, cols * tile), bf16)] * owners
    work = {"flops": 4 * row_count * slots * width * col_tiles * freqs * 2, "moved": u_basis.size * 2}
    count_short = pairs * (row_tiles * cols + rows * col_tiles)
    ranks_here = pltpu.SMEM((1, count_short), jnp.int32)
    stage = pltpu.VMEM((pairs * devices * cols, stage_rows, width), f32)
    one = pltpu.SemaphoreType.DMA

    table = lag_tables(count, time_mask.shape[0], 128)
    choice, same = lag_choice(count, quarter)
    def share(partners):
        return {name: value * partners // devices for name, value in work.items()}

    early, late = exchange_slots(devices)
    slots_all = early + late
    *packed, data, basis, short = call(
        functools.partial(adjoint_kernel, early, cols),
        "adjoint",
        [(far, hold(x)) for x in (ranks, u_data, by_cols)],
        [packed_kind] * len(early)
        + [((freqs, rows, 2 * tile, width), bf16), (by_cols.shape, bf16), ((1, count_short), jnp.int32)],
        [
            pltpu.SMEM(ranks.shape, jnp.int32),
            ranks_here,
            pltpu.VMEM((freqs, row_count, width), bf16),
            stage,
            one((3 + freqs * rows * devices,)),
        ],
        **share(len(early)),
    )
    packed += call(
        functools.partial(adjoint_rest_kernel, late, pairs * row_tiles * cols),
        "adjoint",
        [(whole, short), (whole, data), (whole, basis)],
        [packed_kind] * len(late),
        [ranks_here, stage, one],
        **share(len(late)),
    )
    near, *window = call(
        prepare_kernel,
        "prepare",
        [(far, hold(by_rows))]
        + [(whole, jnp.asarray(x)) for x in (time_mask, table, choice, same)]
        + [(anywhere, packed[-1])],
        [(by_rows.shape, bf16)] + [((side, side), bf16)] * 2,
        [pltpu.VMEM((width // 2, 128), f32), one],
        flops=6 * quarter * 2 * count * 2 * count * side,
        moved=u_basis.size * 2,
    )
    images = call(
        functools.partial(image_kernel, slots_all, owners),
        "image",
        [(whole, short), (whole, near)] + spread(packed, "tile", slots_all),
        per_owner,
        [
            ranks_here,
            stage,
            pltpu.VMEM((cols, 2, row_tiles * slots, width), bf16),
            pltpu.VMEM((freqs, width, cols * tile), f32),
            one,
        ],
        **work,
    )
    mixed = call(
        functools.partial(mix_kernel, owners),
        "mix",
        [(whole, x) for x in window] + to_owners(images),
        per_owner,
        [pltpu.VMEM((side, cols * tile), bf16), pltpu.VMEM((side, cols * tile), f32)],
        flops=4 * side * side * cols * tile,
    )
    packed = call(
        functools.partial(forward_kernel, slots_all, owners),
        "forward",
        [(whole, short), (whole, near)] + to_owners(mixed),
        per_device,
        [ranks_here, pltpu.VMEM((freqs, cols, width, 2 * tile), bf16), stage, one],
        **work,
    )
    [out] = call(
        functools.partial(result_kernel, slots_all),
        "result",
        [(whole, short), (whole, basis)] + spread(packed, "tile", slots_all),
        [((freqs, row_count, width), bf16)],
        [ranks_here, stage, pltpu.VMEM((rows, 2, col_tiles * slots, width), bf16), one],
        **work,
    )
    return out


def solution(mesh):
    placed = (
        P("freq", "tile", None),
        P("freq", "tile", None, None, None, None),
        P("freq", None, "tile", None, None, None),
        P("freq", None, None),
        P(),
    )
    return jax.shard_map(
        local, mesh=mesh, in_specs=placed, out_specs=P("freq", "tile", None), check_vma=False
    )
```

```python
import functools
import math

import jax
import jax.numpy as jnp
import numpy as np
from jax import lax
from jax.experimental import pallas as pl
from jax.experimental.pallas import tpu as pltpu
from jax.sharding import PartitionSpec as P

vmem_limit = 48 * 1024 * 1024
bf16 = jnp.bfloat16
f32 = jnp.float32

whole = pl.BlockSpec(memory_space=pltpu.VMEM)
scalars = pl.BlockSpec(memory_space=pltpu.SMEM)
far = pl.BlockSpec(memory_space=pltpu.HBM)
anywhere = pl.BlockSpec(memory_space=pl.ANY)


def hold(value):
    return pltpu.with_memory_space_constraint(value, pltpu.HBM)


def call(kernel, name, ins, outs, scratch, flops=0, moved=0, specs=None):
    shapes = [jax.ShapeDtypeStruct(shape, kind) for shape, kind in outs]
    return pl.pallas_call(
        kernel,
        in_specs=[spec for spec, _ in ins],
        out_specs=specs or [whole] * len(outs),
        out_shape=shapes,
        scratch_shapes=scratch,
        compiler_params=pltpu.CompilerParams(vmem_limit_bytes=vmem_limit),
        cost_estimate=pl.CostEstimate(flops=flops, bytes_accessed=moved, transcendentals=0),
        name=name,
    )(*[value for _, value in ins])


def dot(lhs, rhs, lhs_dim, rhs_dim, precision=None):
    return lax.dot_general(
        lhs, rhs, (((lhs_dim,), (rhs_dim,)), ((), ())),
        precision=precision, preferred_element_type=f32,
    )


def lag_tables(count, time_count, lanes):
    samples = np.arange(time_count)[:, None]
    lags = np.arange(count)[None, :]
    angle = 2.0 * math.pi / time_count * ((samples * lags) % time_count)
    table = np.zeros((time_count, lanes), np.float32)
    table[:, :count] = np.cos(angle) / time_count
    table[:, count : 2 * count] = np.sin(angle) / time_count
    return table


def lag_choice(count, quarter):
    side = count * 2 * quarter
    choice = np.zeros((2 * count, count, 2, count, 2, quarter), np.float32)
    for f in range(count):
        for g in range(count):
            sign = 1.0 if g >= f else -1.0
            lag = abs(g - f)
            choice[lag, f, 0, g, 0] = 1.0
            choice[lag, f, 1, g, 1] = 1.0
            choice[count + lag, f, 0, g, 1] = -sign
            choice[count + lag, f, 1, g, 0] = sign
    same = np.arange(quarter)[:, None] == np.arange(side)[None, :] % quarter
    return choice.reshape(2 * count, 2 * count * side), same.astype(np.float32)


def pack_rows(stage, slot, row, rank, first, second):
    size = first.shape[0]
    stage[slot, pl.ds(row, size), :] = first
    stage[slot, pl.ds(row + rank, size), :] = second


def unpack_rows(stage, slot, row, rank, total, coeffs, base):
    slots = total - total // 7
    first = stage[slot, pl.ds(row, slots), :]
    second = stage[slot, pl.ds(row + rank, slots), :]
    ids = lax.broadcasted_iota(jnp.int32, first.shape, 0)
    at = pl.ds(pl.multiple_of(base, 16), slots)
    coeffs[0, at, :] = jnp.where(ids < rank, first, 0.0).astype(bf16)
    coeffs[1, at, :] = jnp.where(ids < total - rank, second, 0.0).astype(bf16)


def side_by_side(real, imag):
    flat = (-1, real.shape[-1])
    return jnp.concatenate([real.reshape(flat), imag.reshape(flat)], axis=1)


def plain_product(coeffs, both):
    half, tile = coeffs.shape[1] // 2, both.shape[1] // 2
    product = dot(coeffs, both, 0, 0)
    lead, trail = product[:, :tile], product[:, tile:]
    return jnp.concatenate([lead[:half] - trail[half:], lead[half:] + trail[:half]], axis=0)


def parity(value, mask):
    odd = value & 0
    bit = 0
    while mask >> bit:
        if (mask >> bit) & 1:
            odd = odd ^ ((value >> bit) & 1)
        bit += 1
    return odd


def exchange_slots(devices):
    half = devices // 2
    spare, mixed = list(range(half, devices)), []
    alone = []
    for near in reversed(range(2, half)):
        found = [
            (far, mask)
            for far in spare
            for mask in range(3, devices, 2)
            if not parity(near, mask) and not parity(far, mask)
        ]
        if found and len(spare) > 2:
            far, mask = found[0]
            spare.remove(far)
            mixed += [(far, near, mask), (near, far, mask)]
        else:
            alone.append((near, near, 1))
    first = [(far, far, 1) for far in reversed(spare)]
    return first, mixed + alone + [(1, 1, 1)] * (devices > 1) + [(0, 0, 1)]


def partner(me, slot):
    even, odd, mask = slot
    if even == odd:
        return me ^ even
    return me ^ (even ^ (parity(me, mask) * (even ^ odd)))


def owner_slots(owners):
    mixed = [(1, 2), (2, 1)] if owners > 2 else [(n, n) for n in range(1, owners)]
    return [(n, n) for n in reversed(range(3, owners))] + mixed + [(0, 0)]


def owner(mine, me, slot):
    even, odd = slot
    return mine ^ even if even == odd else mine ^ (even ^ ((me & 1) * (even ^ odd)))


def unstage(outs, slots_out, stage, m, devices, span, size, me):
    for out, slot in zip(outs, slots_out):
        for c in range(span):
            rows = stage[(m * devices + partner(me, slot)) * span + c, pl.ds(0, size), :]
            out[m, pl.ds(c * size, size), :] = rows.astype(bf16)


def adjoint_part(slots_out, first_rank, ranks, turned, basis, outs, stage, waits):
    shifts = sorted({n for slot in slots_out for n in slot[:2]})
    freqs, rows, devices, cols, _, slots, tile = basis.shape
    total = slots + slots // 6
    me = lax.axis_index("tile")
    for i in range(rows):
        for copy in waits[i]:
            copy.wait()
        for m in range(freqs // 2):
            pair = []
            for f in (2 * m, 2 * m + 1):
                real = jnp.concatenate([basis[f, i, me ^ n, :, 0] for n in shifts], axis=0)
                imag = jnp.concatenate([basis[f, i, me ^ n, :, 1] for n in shifts], axis=0)
                pair.append(dot(side_by_side(real, imag), turned[f, i], 1, 0))
            for n, shift in enumerate(shifts):
                for c in range(cols):
                    col = (me ^ shift) * cols + c
                    rank = ranks[0, first_rank + (m * rows + i) * devices * cols + col]
                    cut = slice((n * cols + c) * slots, (n * cols + c + 1) * slots)
                    pack_rows(stage, m * devices * cols + col, i * total, rank, pair[0][cut], pair[1][cut])
    for m in range(freqs // 2):
        unstage(outs, slots_out, stage, m, devices, cols, rows * total, me)


def adjoint_kernel(slots_out, cols, ranks_far, u_far, basis_far, *rest):
    outs = rest[: len(slots_out)]
    turned, basis, short_out, ranks, short, u_ref, stage, sems = rest[len(slots_out) :]
    freqs, rows, devices, _, _, slots, tile = basis.shape
    row_tiles, col_tiles = ranks.shape[1:]
    half = turned.shape[3] // 2
    me = lax.axis_index("tile")
    shifts = sorted({n for slot in slots_out for n in slot[:2]})
    rank_copy = pltpu.make_async_copy(ranks_far, ranks, sems.at[0])
    data_copy = pltpu.make_async_copy(u_far, u_ref, sems.at[1])
    data_copy.start()
    rank_copy.start()
    early, late, at = [[] for _ in range(rows)], [], 3
    for group in (shifts, [n for n in range(devices) if n not in shifts]):
        for i in range(rows):
            for f in range(freqs):
                for n in group:
                    copy = pltpu.make_async_copy(
                        basis_far.at[f, i, me ^ n], basis.at[f, i, me ^ n], sems.at[at]
                    )
                    at += 1
                    copy.start(priority=n % 2)
                    (early[i] if group is shifts else late).append(copy)
    rank_copy.wait()
    first_rank = freqs // 2 * row_tiles * cols
    for m in range(freqs // 2):
        for row in range(row_tiles):
            for c in range(cols):
                short[0, (m * row_tiles + row) * cols + c] = ranks[2 * m, row, me * cols + c]
        for i in range(rows):
            for col in range(col_tiles):
                short[0, first_rank + (m * rows + i) * col_tiles + col] = ranks[2 * m, me * rows + i, col]
    short_copy = pltpu.make_async_copy(short, short_out, sems.at[2])
    short_copy.start()
    data_copy.wait()
    for f in range(freqs):
        for i in range(rows):
            values = u_ref[f, i * tile : (i + 1) * tile, :]
            wide = values.astype(f32)
            lane = lax.broadcasted_iota(jnp.int32, wide.shape, 1)
            rolled = pltpu.roll(wide, half, 1)
            turned[f, i, :tile, :] = values
            turned[f, i, tile:, :] = jnp.where(lane < half, rolled, -rolled).astype(bf16)
    adjoint_part(slots_out, first_rank, short, turned, basis, outs, stage, early)
    short_copy.wait()
    for copy in late:
        copy.wait()


def adjoint_rest_kernel(slots_out, first_rank, short, turned, basis, *rest):
    outs = rest[: len(slots_out)]
    ranks, stage, sem = rest[len(slots_out) :]
    rank_copy = pltpu.make_async_copy(short, ranks, sem)
    rank_copy.start()
    waits = [[rank_copy]] + [[]] * (basis.shape[1] - 1)
    adjoint_part(slots_out, first_rank, ranks, turned, basis, outs, stage, waits)


def gathered(slots_in):
    shifts = sorted({n for slot in slots_in for n in slot[:2]})

    def place(me, slot):
        even, odd, mask = slot
        first, second = shifts.index(even), shifts.index(odd)
        return first if even == odd else first + parity(me, mask) * (second - first)

    return shifts, place


def image_kernel(slots_in, owners, ranks_near, basis, *rest):
    devices = len(slots_in)
    packed = rest[:devices]
    outs = rest[-owners - 5 : -5]
    ranks, stage, coeffs, z, sem = rest[-5:]
    freqs, _, rows, cols, _, slots, tile = basis.shape
    total = slots + slots // 6
    half = coeffs.shape[3] // 2
    quarter = half // owners
    size = rows * total
    me, mine = lax.axis_index("tile"), lax.axis_index("freq")
    rank_copy = pltpu.make_async_copy(ranks_near, ranks, sem)
    rank_copy.start()
    for m in range(freqs // 2):
        for s in range(devices):
            for c in range(cols):
                block = packed[s][m, pl.ds(c * size, size), :]
                stage[(m * devices + s) * cols + c, pl.ds(0, size), :] = block.astype(f32)
    rank_copy.wait()
    for m in range(freqs // 2):
        for c in range(cols):
            for s in range(devices):
                for i in range(rows):
                    row = partner(me, slots_in[s]) * rows + i
                    rank = ranks[0, (m * devices * rows + row) * cols + c]
                    slot = (m * devices + s) * cols + c
                    unpack_rows(stage, slot, i * total, rank, total, coeffs.at[c], row * slots)
            for n in range(2):
                f = 2 * m + n
                both = side_by_side(basis[f, :, :, c, 0], basis[f, :, :, c, 1])
                z[f, :, pl.ds(c * tile, tile)] = plain_product(coeffs[c, n], both)
    for r, slot in enumerate(owner_slots(owners)):
        low = pl.multiple_of(owner(mine, me, slot) * quarter, quarter)
        for f in range(freqs):
            real = z[f, pl.ds(low, quarter), :]
            imag = z[f, pl.ds(half + low, quarter), :]
            outs[r][f] = jnp.concatenate([real, imag], axis=0).astype(bf16)


def prepare_kernel(basis_far, mask, table, choice, same, *rest):
    basis, high, low, full, sem = rest[-5:]
    basis_copy = pltpu.make_async_copy(basis_far, basis, sem)
    basis_copy.start()
    exact = lax.Precision.HIGHEST
    full[...] = dot(mask[...].astype(f32), table[...], 0, 0, exact)
    quarter, side = same.shape
    mine = full[pl.ds(pl.multiple_of(lax.axis_index("freq") * quarter, quarter), quarter), :]
    entries = dot(mine[:, : choice.shape[0]], choice[...], 1, 0, exact)
    for n in range(side // quarter):
        block = entries[:, n * side : (n + 1) * side] * same[...]
        upper = block.astype(bf16)
        high[n * quarter : (n + 1) * quarter, :] = upper
        low[n * quarter : (n + 1) * quarter, :] = (block - upper.astype(f32)).astype(bf16)
    basis_copy.wait()


def mix_kernel(owners, high, low, *rest):
    arrived = rest[:owners]
    outs = rest[owners : 2 * owners]
    z, w = rest[2 * owners :]
    freqs, rows, span = arrived[0].shape
    me, mine = lax.axis_index("tile"), lax.axis_index("freq")
    size = freqs * rows
    places = [pl.multiple_of(owner(mine, me, slot) * size, 16) for slot in owner_slots(owners)]
    for r in range(owners):
        z[pl.ds(places[r], size), :] = arrived[r][...].reshape(size, span)
    w[...] = dot(high[...], z[...], 1, 0) + dot(low[...], z[...], 1, 0)
    for r in range(owners):
        block = w[pl.ds(places[r], size), :]
        outs[r][...] = block.reshape(freqs, rows, span).astype(bf16)


def forward_kernel(slots_out, owners, ranks_near, basis, *rest):
    devices = len(slots_out)
    arrived = rest[:owners]
    outs = rest[owners : owners + devices]
    ranks, w, stage, sem = rest[owners + devices :]
    freqs, _, rows, cols, _, slots, tile = basis.shape
    total = slots + slots // 6
    half = w.shape[2] // 2
    quarter = half // owners
    me, mine = lax.axis_index("tile"), lax.axis_index("freq")
    rank_copy = pltpu.make_async_copy(ranks_near, ranks, sem)
    rank_copy.start()
    for r, slot in enumerate(owner_slots(owners)):
        low = pl.multiple_of(owner(mine, me, slot) * quarter, quarter)
        for f in range(freqs):
            for c in range(cols):
                at = slice(c * tile, (c + 1) * tile)
                real, imag = arrived[r][f, :quarter, at], arrived[r][f, quarter:, at]
                w[f, c, pl.ds(low, quarter), :tile] = real
                w[f, c, pl.ds(half + low, quarter), :tile] = imag
                w[f, c, pl.ds(low, quarter), tile:] = imag
                w[f, c, pl.ds(half + low, quarter), tile:] = -real
    rank_copy.wait()
    for m in range(freqs // 2):
        for c in range(cols):
            pair = []
            for f in (2 * m, 2 * m + 1):
                both = side_by_side(basis[f, :, :, c, 0], basis[f, :, :, c, 1])
                pair.append(dot(both, w[f, c], 1, 1))
            for d in range(devices):
                for i in range(rows):
                    rank = ranks[0, (m * devices * rows + d * rows + i) * cols + c]
                    cut = slice((d * rows + i) * slots, (d * rows + i + 1) * slots)
                    slot = (m * devices + d) * cols + c
                    pack_rows(stage, slot, i * total, rank, pair[0][cut], pair[1][cut])
        unstage(outs, slots_out, stage, m, devices, cols, rows * total, me)


def result_kernel(slots_in, last, ranks_near, basis, *rest):
    count = len(slots_in)
    shifts, place = gathered(slots_in)
    packed, rest = rest[:count], rest[count:]
    out, ranks, stage, coeffs, sem = rest[-5:]
    freqs, rows, devices, cols, _, slots, tile = basis.shape
    total = slots + slots // 6
    size = rows * total
    first_rank = freqs // 2 * devices * rows * cols
    me = lax.axis_index("tile")
    rank_copy = pltpu.make_async_copy(ranks_near, ranks, sem)
    rank_copy.start()
    for m in range(freqs // 2):
        for n in range(count):
            for c in range(cols):
                block = packed[n][m, pl.ds(c * size, size), :]
                stage[(m * count + n) * cols + c, pl.ds(0, size), :] = block.astype(f32)
    rank_copy.wait()
    for m in range(freqs // 2):
        for i in range(rows):
            for n, slot in enumerate(slots_in):
                for c in range(cols):
                    col = partner(me, slot) * cols + c
                    rank = ranks[0, first_rank + (m * rows + i) * devices * cols + col]
                    base = (place(me, slot) * cols + c) * slots
                    unpack_rows(stage, (m * count + n) * cols + c, i * total, rank, total, coeffs.at[i], base)
            for n in range(2):
                f = 2 * m + n
                real = jnp.concatenate([basis[f, i, me ^ shift, :, 0] for shift in shifts], axis=0)
                imag = jnp.concatenate([basis[f, i, me ^ shift, :, 1] for shift in shifts], axis=0)
                part = plain_product(coeffs[i, n], side_by_side(real, imag))
                if last:
                    out[f, pl.ds(i * tile, tile), :] = (part + rest[0][f, i]).T.astype(bf16)
                else:
                    out[f, i] = part


def send(value, axis, slot):
    if slot[:2] == (0, 0):
        return value
    return lax.ppermute(value, axis, [(d, partner(d, slot)) for d in range(lax.axis_size(axis))])


def spread(values, axis, slots):
    return [(whole, send(value, axis, slot)) for value, slot in zip(values, slots)]


def to_owners(values):
    owners, devices = lax.axis_size("freq"), lax.axis_size("tile")
    landed = []
    for value, slot in zip(values, owner_slots(owners)):
        if slot != (0, 0):
            pairs = [
                (mine * devices + me, owner(mine, me, slot) * devices + me)
                for mine in range(owners)
                for me in range(devices)
            ]
            value = lax.ppermute(value, ("freq", "tile"), pairs)
        landed.append((whole, value))
    return landed


def local(u_data, u_basis, v_basis, ranks, time_mask):
    freqs, row_count, width = u_data.shape
    rows, col_tiles, _, slots, tile = u_basis.shape[1:]
    row_tiles, cols = v_basis.shape[1:3]
    total = slots // 6 + slots
    pairs = freqs // 2
    devices = lax.axis_size("tile")
    owners = lax.axis_size("freq")
    stage_rows = rows * total + 2 * slots
    quarter = width // 2 // owners
    count = owners * freqs
    side = count * 2 * quarter
    by_cols = u_basis.reshape(freqs, rows, devices, cols, 2, slots, tile)
    by_rows = v_basis.reshape(freqs, devices, rows, cols, 2, slots, tile)
    packed_kind = ((pairs, cols * rows * total, width), bf16)
    per_device = [packed_kind] * devices
    per_owner = [((freqs, 2 * quarter, cols * tile), bf16)] * owners
    work = {"flops": 4 * row_count * slots * width * col_tiles * freqs * 2, "moved": u_basis.size * 2}
    count_short = pairs * (row_tiles * cols + rows * col_tiles)
    ranks_here = pltpu.SMEM((1, count_short), jnp.int32)
    stage = pltpu.VMEM((pairs * devices * cols, stage_rows, width), f32)
    one = pltpu.SemaphoreType.DMA

    table = lag_tables(count, time_mask.shape[0], 128)
    choice, same = lag_choice(count, quarter)
    def share(partners):
        return {name: value * partners // devices for name, value in work.items()}

    early, late = exchange_slots(devices)
    slots_all = early + late
    *packed, data, basis, short = call(
        functools.partial(adjoint_kernel, early, cols),
        "adjoint",
        [(far, hold(x)) for x in (ranks, u_data, by_cols)],
        [packed_kind] * len(early)
        + [((freqs, rows, 2 * tile, width), bf16), (by_cols.shape, bf16), ((1, count_short), jnp.int32)],
        [
            pltpu.SMEM(ranks.shape, jnp.int32),
            ranks_here,
            pltpu.VMEM((freqs, row_count, width), bf16),
            stage,
            one((3 + freqs * rows * devices,)),
        ],
        **share(len(early)),
    )
    packed += call(
        functools.partial(adjoint_rest_kernel, late, pairs * row_tiles * cols),
        "adjoint",
        [(whole, short), (whole, data), (whole, basis)],
        [packed_kind] * len(late),
        [ranks_here, stage, one],
        **share(len(late)),
    )
    near, *window = call(
        prepare_kernel,
        "prepare",
        [(far, hold(by_rows))]
        + [(whole, jnp.asarray(x)) for x in (time_mask, table, choice, same)]
        + [(anywhere, packed[-1])],
        [(by_rows.shape, bf16)] + [((side, side), bf16)] * 2,
        [pltpu.VMEM((width // 2, 128), f32), one],
        flops=6 * quarter * 2 * count * 2 * count * side,
        moved=u_basis.size * 2,
    )
    cut = len(early) + len([slot for slot in late if slot[0] != slot[1]]) // 4 * 2
    own = len(slots_all) - 1
    groups = [list(range(cut)) + [own], list(range(cut, own))]

    def landed(packed):
        arrived = spread(packed, "tile", slots_all)
        return [[arrived[n] for n in group] for group in groups]

    def stage_for(partners):
        return pltpu.VMEM((pairs * partners * cols, stage_rows, width), f32)

    images = call(
        functools.partial(image_kernel, slots_all, owners),
        "image",
        [(whole, short), (whole, near)] + spread(packed, "tile", slots_all),
        per_owner,
        [
            ranks_here,
            stage,
            pltpu.VMEM((cols, 2, row_tiles * slots, width), bf16),
            pltpu.VMEM((freqs, width, cols * tile), f32),
            one,
        ],
        **work,
    )
    mixed = call(
        functools.partial(mix_kernel, owners),
        "mix",
        [(whole, x) for x in window] + to_owners(images),
        per_owner,
        [pltpu.VMEM((side, cols * tile), bf16), pltpu.VMEM((side, cols * tile), f32)],
        flops=4 * side * side * cols * tile,
    )
    packed = call(
        functools.partial(forward_kernel, slots_all, owners),
        "forward",
        [(whole, short), (whole, near)] + to_owners(mixed),
        per_device,
        [ranks_here, pltpu.VMEM((freqs, cols, width, 2 * tile), bf16), stage, one],
        **work,
    )
    out = []
    for group, arrived in zip(groups, landed(packed)):
        last = group is groups[-1]
        out = call(
            functools.partial(result_kernel, [slots_all[n] for n in group], last),
            "result",
            [(whole, short), (whole, basis)] + arrived + [(whole, x) for x in out],
            [((freqs, row_count, width), bf16) if last else ((freqs, rows, width, tile), f32)],
            [
                ranks_here,
                stage_for(len(group)),
                pltpu.VMEM((rows, 2, len(group) * cols * slots, width), bf16),
                one,
            ],
            **share(len(group)),
        )
    return out[0]


def solution(mesh):
    placed = (
        P("freq", "tile", None),
        P("freq", "tile", None, None, None, None),
        P("freq", None, "tile", None, None, None),
        P("freq", None, None),
        P(),
    )
    return jax.shard_map(
        local, mesh=mesh, in_specs=placed, out_specs=P("freq", "tile", None), check_vma=False
    )
```

```python
import functools
import math

import jax
import jax.numpy as jnp
import numpy as np
from jax import lax
from jax.experimental import pallas as pl
from jax.experimental.pallas import tpu as pltpu
from jax.sharding import PartitionSpec as P

vmem_limit = 48 * 1024 * 1024
bf16 = jnp.bfloat16
f32 = jnp.float32

whole = pl.BlockSpec(memory_space=pltpu.VMEM)
scalars = pl.BlockSpec(memory_space=pltpu.SMEM)
far = pl.BlockSpec(memory_space=pltpu.HBM)
anywhere = pl.BlockSpec(memory_space=pl.ANY)


def hold(value):
    return pltpu.with_memory_space_constraint(value, pltpu.HBM)


def call(kernel, name, ins, outs, scratch, flops=0, moved=0, specs=None):
    shapes = [jax.ShapeDtypeStruct(shape, kind) for shape, kind in outs]
    return pl.pallas_call(
        kernel,
        in_specs=[spec for spec, _ in ins],
        out_specs=specs or [whole] * len(outs),
        out_shape=shapes,
        scratch_shapes=scratch,
        compiler_params=pltpu.CompilerParams(vmem_limit_bytes=vmem_limit),
        cost_estimate=pl.CostEstimate(flops=flops, bytes_accessed=moved, transcendentals=0),
        name=name,
    )(*[value for _, value in ins])


def dot(lhs, rhs, lhs_dim, rhs_dim, precision=None):
    return lax.dot_general(
        lhs, rhs, (((lhs_dim,), (rhs_dim,)), ((), ())),
        precision=precision, preferred_element_type=f32,
    )


def lag_tables(count, time_count, lanes):
    samples = np.arange(time_count)[:, None]
    lags = np.arange(count)[None, :]
    angle = 2.0 * math.pi / time_count * ((samples * lags) % time_count)
    table = np.zeros((time_count, lanes), np.float32)
    table[:, :count] = np.cos(angle) / time_count
    table[:, count : 2 * count] = np.sin(angle) / time_count
    return table


def lag_choice(count, quarter):
    side = count * 2 * quarter
    choice = np.zeros((2 * count, count, 2, count, 2, quarter), np.float32)
    for f in range(count):
        for g in range(count):
            sign = 1.0 if g >= f else -1.0
            lag = abs(g - f)
            choice[lag, f, 0, g, 0] = 1.0
            choice[lag, f, 1, g, 1] = 1.0
            choice[count + lag, f, 0, g, 1] = -sign
            choice[count + lag, f, 1, g, 0] = sign
    same = np.arange(quarter)[:, None] == np.arange(side)[None, :] % quarter
    return choice.reshape(2 * count, 2 * count * side), same.astype(np.float32)


def pack_rows(stage, slot, row, rank, first, second):
    size = first.shape[0]
    stage[slot, pl.ds(row, size), :] = first
    stage[slot, pl.ds(row + rank, size), :] = second


def unpack_rows(stage, slot, row, rank, total, coeffs, base):
    slots = total - total // 7
    first = stage[slot, pl.ds(row, slots), :]
    second = stage[slot, pl.ds(row + rank, slots), :]
    ids = lax.broadcasted_iota(jnp.int32, first.shape, 0)
    at = pl.ds(pl.multiple_of(base, 16), slots)
    coeffs[0, at, :] = jnp.where(ids < rank, first, 0.0).astype(bf16)
    coeffs[1, at, :] = jnp.where(ids < total - rank, second, 0.0).astype(bf16)


def side_by_side(real, imag):
    flat = (-1, real.shape[-1])
    return jnp.concatenate([real.reshape(flat), imag.reshape(flat)], axis=1)


def plain_product(coeffs, both):
    half, tile = coeffs.shape[1] // 2, both.shape[1] // 2
    product = dot(coeffs, both, 0, 0)
    lead, trail = product[:, :tile], product[:, tile:]
    return jnp.concatenate([lead[:half] - trail[half:], lead[half:] + trail[:half]], axis=0)


def parity(value, mask):
    odd = value & 0
    bit = 0
    while mask >> bit:
        if (mask >> bit) & 1:
            odd = odd ^ ((value >> bit) & 1)
        bit += 1
    return odd


def exchange_slots(devices):
    half = devices // 2
    spare, mixed = list(range(half, devices)), []
    alone = []
    for near in reversed(range(2, half)):
        found = [
            (far, mask)
            for far in spare
            for mask in range(3, devices, 2)
            if not parity(near, mask) and not parity(far, mask)
        ]
        if found and len(spare) > 3:
            far, mask = found[0]
            spare.remove(far)
            mixed += [(far, near, mask), (near, far, mask)]
        else:
            alone.append((near, near, 1))
    first = [(far, far, 1) for far in reversed(spare)]
    return first, mixed + alone + [(1, 1, 1)] * (devices > 1) + [(0, 0, 1)]


def partner(me, slot):
    even, odd, mask = slot
    if even == odd:
        return me ^ even
    return me ^ (even ^ (parity(me, mask) * (even ^ odd)))


def owner_slots(owners):
    mixed = [(1, 2), (2, 1)] if owners > 2 else [(n, n) for n in range(1, owners)]
    return [(n, n) for n in reversed(range(3, owners))] + mixed + [(0, 0)]


def owner(mine, me, slot):
    even, odd = slot
    return mine ^ even if even == odd else mine ^ (even ^ ((me & 1) * (even ^ odd)))


def unstage(outs, slots_out, stage, m, devices, span, size, me):
    for out, slot in zip(outs, slots_out):
        for c in range(span):
            rows = stage[(m * devices + partner(me, slot)) * span + c, pl.ds(0, size), :]
            out[m, pl.ds(c * size, size), :] = rows.astype(bf16)


def adjoint_part(slots_out, first_rank, ranks, turned, basis, outs, stage, waits):
    shifts = sorted({n for slot in slots_out for n in slot[:2]})
    freqs, rows, devices, cols, _, slots, tile = basis.shape
    total = slots + slots // 6
    me = lax.axis_index("tile")
    for i in range(rows):
        for copy in waits[i]:
            copy.wait()
        for m in range(freqs // 2):
            pair = []
            for f in (2 * m, 2 * m + 1):
                real = jnp.concatenate([basis[f, i, me ^ n, :, 0] for n in shifts], axis=0)
                imag = jnp.concatenate([basis[f, i, me ^ n, :, 1] for n in shifts], axis=0)
                pair.append(dot(side_by_side(real, imag), turned[f, i], 1, 0))
            for n, shift in enumerate(shifts):
                for c in range(cols):
                    col = (me ^ shift) * cols + c
                    rank = ranks[0, first_rank + (m * rows + i) * devices * cols + col]
                    cut = slice((n * cols + c) * slots, (n * cols + c + 1) * slots)
                    pack_rows(stage, m * devices * cols + col, i * total, rank, pair[0][cut], pair[1][cut])
    for m in range(freqs // 2):
        unstage(outs, slots_out, stage, m, devices, cols, rows * total, me)


def adjoint_kernel(slots_out, cols, ranks_far, u_far, basis_far, *rest):
    outs = rest[: len(slots_out)]
    turned, basis, short_out, ranks, short, u_ref, stage, sems = rest[len(slots_out) :]
    freqs, rows, devices, _, _, slots, tile = basis.shape
    row_tiles, col_tiles = ranks.shape[1:]
    half = turned.shape[3] // 2
    me = lax.axis_index("tile")
    shifts = sorted({n for slot in slots_out for n in slot[:2]})
    rank_copy = pltpu.make_async_copy(ranks_far, ranks, sems.at[0])
    data_copy = pltpu.make_async_copy(u_far, u_ref, sems.at[1])
    data_copy.start()
    rank_copy.start()
    early, late, at = [[] for _ in range(rows)], [], 3
    for group in (shifts, [n for n in range(devices) if n not in shifts]):
        for i in range(rows):
            for f in range(freqs):
                for n in group:
                    copy = pltpu.make_async_copy(
                        basis_far.at[f, i, me ^ n], basis.at[f, i, me ^ n], sems.at[at]
                    )
                    at += 1
                    copy.start(priority=n % 2)
                    (early[i] if group is shifts else late).append(copy)
    rank_copy.wait()
    first_rank = freqs // 2 * row_tiles * cols
    for m in range(freqs // 2):
        for row in range(row_tiles):
            for c in range(cols):
                short[0, (m * row_tiles + row) * cols + c] = ranks[2 * m, row, me * cols + c]
        for i in range(rows):
            for col in range(col_tiles):
                short[0, first_rank + (m * rows + i) * col_tiles + col] = ranks[2 * m, me * rows + i, col]
    short_copy = pltpu.make_async_copy(short, short_out, sems.at[2])
    short_copy.start()
    data_copy.wait()
    for f in range(freqs):
        for i in range(rows):
            values = u_ref[f, i * tile : (i + 1) * tile, :]
            wide = values.astype(f32)
            lane = lax.broadcasted_iota(jnp.int32, wide.shape, 1)
            rolled = pltpu.roll(wide, half, 1)
            turned[f, i, :tile, :] = values
            turned[f, i, tile:, :] = jnp.where(lane < half, rolled, -rolled).astype(bf16)
    adjoint_part(slots_out, first_rank, short, turned, basis, outs, stage, early)
    short_copy.wait()
    for copy in late:
        copy.wait()


def adjoint_rest_kernel(slots_out, first_rank, short, turned, basis, *rest):
    outs = rest[: len(slots_out)]
    ranks, stage, sem = rest[len(slots_out) :]
    rank_copy = pltpu.make_async_copy(short, ranks, sem)
    rank_copy.start()
    waits = [[rank_copy]] + [[]] * (basis.shape[1] - 1)
    adjoint_part(slots_out, first_rank, ranks, turned, basis, outs, stage, waits)


def gathered(slots_in):
    shifts = sorted({n for slot in slots_in for n in slot[:2]})

    def place(me, slot):
        even, odd, mask = slot
        first, second = shifts.index(even), shifts.index(odd)
        return first if even == odd else first + parity(me, mask) * (second - first)

    return shifts, place


def image_kernel(slots_in, owners, ranks_near, basis, *rest):
    devices = len(slots_in)
    packed = rest[:devices]
    outs = rest[-owners - 5 : -5]
    ranks, stage, coeffs, z, sem = rest[-5:]
    freqs, _, rows, cols, _, slots, tile = basis.shape
    total = slots + slots // 6
    half = coeffs.shape[3] // 2
    quarter = half // owners
    size = rows * total
    me, mine = lax.axis_index("tile"), lax.axis_index("freq")
    rank_copy = pltpu.make_async_copy(ranks_near, ranks, sem)
    rank_copy.start()
    for m in range(freqs // 2):
        for s in range(devices):
            for c in range(cols):
                block = packed[s][m, pl.ds(c * size, size), :]
                stage[(m * devices + s) * cols + c, pl.ds(0, size), :] = block.astype(f32)
    rank_copy.wait()
    for m in range(freqs // 2):
        for c in range(cols):
            for s in range(devices):
                for i in range(rows):
                    row = partner(me, slots_in[s]) * rows + i
                    rank = ranks[0, (m * devices * rows + row) * cols + c]
                    slot = (m * devices + s) * cols + c
                    unpack_rows(stage, slot, i * total, rank, total, coeffs.at[c], row * slots)
            for n in range(2):
                f = 2 * m + n
                both = side_by_side(basis[f, :, :, c, 0], basis[f, :, :, c, 1])
                z[f, :, pl.ds(c * tile, tile)] = plain_product(coeffs[c, n], both)
    for r, slot in enumerate(owner_slots(owners)):
        low = pl.multiple_of(owner(mine, me, slot) * quarter, quarter)
        for f in range(freqs):
            real = z[f, pl.ds(low, quarter), :]
            imag = z[f, pl.ds(half + low, quarter), :]
            outs[r][f] = jnp.concatenate([real, imag], axis=0).astype(bf16)


def prepare_kernel(basis_far, mask, table, choice, same, *rest):
    basis, high, low, full, sem = rest[-5:]
    basis_copy = pltpu.make_async_copy(basis_far, basis, sem)
    basis_copy.start()
    exact = lax.Precision.HIGHEST
    full[...] = dot(mask[...].astype(f32), table[...], 0, 0, exact)
    quarter, side = same.shape
    mine = full[pl.ds(pl.multiple_of(lax.axis_index("freq") * quarter, quarter), quarter), :]
    entries = dot(mine[:, : choice.shape[0]], choice[...], 1, 0, exact)
    for n in range(side // quarter):
        block = entries[:, n * side : (n + 1) * side] * same[...]
        upper = block.astype(bf16)
        high[n * quarter : (n + 1) * quarter, :] = upper
        low[n * quarter : (n + 1) * quarter, :] = (block - upper.astype(f32)).astype(bf16)
    basis_copy.wait()


def mix_kernel(owners, high, low, *rest):
    arrived = rest[:owners]
    outs = rest[owners : 2 * owners]
    z, w = rest[2 * owners :]
    freqs, rows, span = arrived[0].shape
    me, mine = lax.axis_index("tile"), lax.axis_index("freq")
    size = freqs * rows
    places = [pl.multiple_of(owner(mine, me, slot) * size, 16) for slot in owner_slots(owners)]
    for r in range(owners):
        z[pl.ds(places[r], size), :] = arrived[r][...].reshape(size, span)
    w[...] = dot(high[...], z[...], 1, 0) + dot(low[...], z[...], 1, 0)
    for r in range(owners):
        block = w[pl.ds(places[r], size), :]
        outs[r][...] = block.reshape(freqs, rows, span).astype(bf16)


def forward_kernel(slots_out, owners, ranks_near, basis, *rest):
    devices = len(slots_out)
    arrived = rest[:owners]
    outs = rest[owners : owners + devices]
    ranks, w, stage, sem = rest[owners + devices :]
    freqs, _, rows, cols, _, slots, tile = basis.shape
    total = slots + slots // 6
    half = w.shape[2] // 2
    quarter = half // owners
    me, mine = lax.axis_index("tile"), lax.axis_index("freq")
    rank_copy = pltpu.make_async_copy(ranks_near, ranks, sem)
    rank_copy.start()
    for r, slot in enumerate(owner_slots(owners)):
        low = pl.multiple_of(owner(mine, me, slot) * quarter, quarter)
        for f in range(freqs):
            for c in range(cols):
                at = slice(c * tile, (c + 1) * tile)
                real, imag = arrived[r][f, :quarter, at], arrived[r][f, quarter:, at]
                w[f, c, pl.ds(low, quarter), :tile] = real
                w[f, c, pl.ds(half + low, quarter), :tile] = imag
                w[f, c, pl.ds(low, quarter), tile:] = imag
                w[f, c, pl.ds(half + low, quarter), tile:] = -real
    rank_copy.wait()
    for m in range(freqs // 2):
        for c in range(cols):
            pair = []
            for f in (2 * m, 2 * m + 1):
                both = side_by_side(basis[f, :, :, c, 0], basis[f, :, :, c, 1])
                pair.append(dot(both, w[f, c], 1, 1))
            for d in range(devices):
                for i in range(rows):
                    rank = ranks[0, (m * devices * rows + d * rows + i) * cols + c]
                    cut = slice((d * rows + i) * slots, (d * rows + i + 1) * slots)
                    slot = (m * devices + d) * cols + c
                    pack_rows(stage, slot, i * total, rank, pair[0][cut], pair[1][cut])
        unstage(outs, slots_out, stage, m, devices, cols, rows * total, me)


def result_kernel(slots_in, last, ranks_near, basis, *rest):
    count = len(slots_in)
    shifts, place = gathered(slots_in)
    packed, rest = rest[:count], rest[count:]
    out, ranks, stage, coeffs, sem = rest[-5:]
    freqs, rows, devices, cols, _, slots, tile = basis.shape
    total = slots + slots // 6
    size = rows * total
    first_rank = freqs // 2 * devices * rows * cols
    me = lax.axis_index("tile")
    rank_copy = pltpu.make_async_copy(ranks_near, ranks, sem)
    rank_copy.start()
    for m in range(freqs // 2):
        for n in range(count):
            for c in range(cols):
                block = packed[n][m, pl.ds(c * size, size), :]
                stage[(m * count + n) * cols + c, pl.ds(0, size), :] = block.astype(f32)
    rank_copy.wait()
    for m in range(freqs // 2):
        for i in range(rows):
            for n, slot in enumerate(slots_in):
                for c in range(cols):
                    col = partner(me, slot) * cols + c
                    rank = ranks[0, first_rank + (m * rows + i) * devices * cols + col]
                    base = (place(me, slot) * cols + c) * slots
                    unpack_rows(stage, (m * count + n) * cols + c, i * total, rank, total, coeffs.at[i], base)
            for n in range(2):
                f = 2 * m + n
                real = jnp.concatenate([basis[f, i, me ^ shift, :, 0] for shift in shifts], axis=0)
                imag = jnp.concatenate([basis[f, i, me ^ shift, :, 1] for shift in shifts], axis=0)
                part = plain_product(coeffs[i, n], side_by_side(real, imag))
                if last:
                    out[f, pl.ds(i * tile, tile), :] = (part + rest[0][f, i]).T.astype(bf16)
                else:
                    out[f, i] = part


def send(value, axis, slot):
    if slot[:2] == (0, 0):
        return value
    return lax.ppermute(value, axis, [(d, partner(d, slot)) for d in range(lax.axis_size(axis))])


def spread(values, axis, slots):
    return [(whole, send(value, axis, slot)) for value, slot in zip(values, slots)]


def to_owners(values):
    owners, devices = lax.axis_size("freq"), lax.axis_size("tile")
    landed = []
    for value, slot in zip(values, owner_slots(owners)):
        if slot != (0, 0):
            pairs = [
                (mine * devices + me, owner(mine, me, slot) * devices + me)
                for mine in range(owners)
                for me in range(devices)
            ]
            value = lax.ppermute(value, ("freq", "tile"), pairs)
        landed.append((whole, value))
    return landed


def local(u_data, u_basis, v_basis, ranks, time_mask):
    freqs, row_count, width = u_data.shape
    rows, col_tiles, _, slots, tile = u_basis.shape[1:]
    row_tiles, cols = v_basis.shape[1:3]
    total = slots // 6 + slots
    pairs = freqs // 2
    devices = lax.axis_size("tile")
    owners = lax.axis_size("freq")
    stage_rows = rows * total + 2 * slots
    quarter = width // 2 // owners
    count = owners * freqs
    side = count * 2 * quarter
    by_cols = u_basis.reshape(freqs, rows, devices, cols, 2, slots, tile)
    by_rows = v_basis.reshape(freqs, devices, rows, cols, 2, slots, tile)
    packed_kind = ((pairs, cols * rows * total, width), bf16)
    per_device = [packed_kind] * devices
    per_owner = [((freqs, 2 * quarter, cols * tile), bf16)] * owners
    work = {"flops": 4 * row_count * slots * width * col_tiles * freqs * 2, "moved": u_basis.size * 2}
    count_short = pairs * (row_tiles * cols + rows * col_tiles)
    ranks_here = pltpu.SMEM((1, count_short), jnp.int32)
    stage = pltpu.VMEM((pairs * devices * cols, stage_rows, width), f32)
    one = pltpu.SemaphoreType.DMA

    table = lag_tables(count, time_mask.shape[0], 128)
    choice, same = lag_choice(count, quarter)
    def share(partners):
        return {name: value * partners // devices for name, value in work.items()}

    early, late = exchange_slots(devices)
    slots_all = early + late
    *packed, data, basis, short = call(
        functools.partial(adjoint_kernel, early, cols),
        "adjoint",
        [(far, hold(x)) for x in (ranks, u_data, by_cols)],
        [packed_kind] * len(early)
        + [((freqs, rows, 2 * tile, width), bf16), (by_cols.shape, bf16), ((1, count_short), jnp.int32)],
        [
            pltpu.SMEM(ranks.shape, jnp.int32),
            ranks_here,
            pltpu.VMEM((freqs, row_count, width), bf16),
            stage,
            one((3 + freqs * rows * devices,)),
        ],
        **share(len(early)),
    )
    packed += call(
        functools.partial(adjoint_rest_kernel, late, pairs * row_tiles * cols),
        "adjoint",
        [(whole, short), (whole, data), (whole, basis)],
        [packed_kind] * len(late),
        [ranks_here, stage, one],
        **share(len(late)),
    )
    near, *window = call(
        prepare_kernel,
        "prepare",
        [(far, hold(by_rows))]
        + [(whole, jnp.asarray(x)) for x in (time_mask, table, choice, same)]
        + [(anywhere, packed[-1])],
        [(by_rows.shape, bf16)] + [((side, side), bf16)] * 2,
        [pltpu.VMEM((width // 2, 128), f32), one],
        flops=6 * quarter * 2 * count * 2 * count * side,
        moved=u_basis.size * 2,
    )
    cut = len(early) + len([slot for slot in late if slot[0] != slot[1]]) // 4 * 2
    own = len(slots_all) - 1
    groups = [list(range(cut)) + [own], list(range(cut, own))]

    def landed(packed):
        arrived = spread(packed, "tile", slots_all)
        return [[arrived[n] for n in group] for group in groups]

    def stage_for(partners):
        return pltpu.VMEM((pairs * partners * cols, stage_rows, width), f32)

    images = call(
        functools.partial(image_kernel, slots_all, owners),
        "image",
        [(whole, short), (whole, near)] + spread(packed, "tile", slots_all),
        per_owner,
        [
            ranks_here,
            stage,
            pltpu.VMEM((cols, 2, row_tiles * slots, width), bf16),
            pltpu.VMEM((freqs, width, cols * tile), f32),
            one,
        ],
        **work,
    )
    mixed = call(
        functools.partial(mix_kernel, owners),
        "mix",
        [(whole, x) for x in window] + to_owners(images),
        per_owner,
        [pltpu.VMEM((side, cols * tile), bf16), pltpu.VMEM((side, cols * tile), f32)],
        flops=4 * side * side * cols * tile,
    )
    packed = call(
        functools.partial(forward_kernel, slots_all, owners),
        "forward",
        [(whole, short), (whole, near)] + to_owners(mixed),
        per_device,
        [ranks_here, pltpu.VMEM((freqs, cols, width, 2 * tile), bf16), stage, one],
        **work,
    )
    out = []
    for group, arrived in zip(groups, landed(packed)):
        last = group is groups[-1]
        out = call(
            functools.partial(result_kernel, [slots_all[n] for n in group], last),
            "result",
            [(whole, short), (whole, basis)] + arrived + [(whole, x) for x in out],
            [((freqs, row_count, width), bf16) if last else ((freqs, rows, width, tile), f32)],
            [
                ranks_here,
                stage_for(len(group)),
                pltpu.VMEM((rows, 2, len(group) * cols * slots, width), bf16),
                one,
            ],
            **share(len(group)),
        )
    return out[0]


def solution(mesh):
    placed = (
        P("freq", "tile", None),
        P("freq", "tile", None, None, None, None),
        P("freq", None, "tile", None, None, None),
        P("freq", None, None),
        P(),
    )
    return jax.shard_map(
        local, mesh=mesh, in_specs=placed, out_specs=P("freq", "tile", None), check_vma=False
    )
```

```python
import functools
import math

import jax
import jax.numpy as jnp
import numpy as np
from jax import lax
from jax.experimental import pallas as pl
from jax.experimental.pallas import tpu as pltpu
from jax.sharding import PartitionSpec as P

vmem_limit = 48 * 1024 * 1024
bf16 = jnp.bfloat16
f32 = jnp.float32

whole = pl.BlockSpec(memory_space=pltpu.VMEM)
scalars = pl.BlockSpec(memory_space=pltpu.SMEM)
far = pl.BlockSpec(memory_space=pltpu.HBM)
anywhere = pl.BlockSpec(memory_space=pl.ANY)


def hold(value):
    return pltpu.with_memory_space_constraint(value, pltpu.HBM)


def call(kernel, name, ins, outs, scratch, flops=0, moved=0, specs=None):
    shapes = [jax.ShapeDtypeStruct(shape, kind) for shape, kind in outs]
    return pl.pallas_call(
        kernel,
        in_specs=[spec for spec, _ in ins],
        out_specs=specs or [whole] * len(outs),
        out_shape=shapes,
        scratch_shapes=scratch,
        compiler_params=pltpu.CompilerParams(vmem_limit_bytes=vmem_limit),
        cost_estimate=pl.CostEstimate(flops=flops, bytes_accessed=moved, transcendentals=0),
        name=name,
    )(*[value for _, value in ins])


def dot(lhs, rhs, lhs_dim, rhs_dim, precision=None):
    return lax.dot_general(
        lhs, rhs, (((lhs_dim,), (rhs_dim,)), ((), ())),
        precision=precision, preferred_element_type=f32,
    )


def lag_tables(count, time_count, lanes):
    samples = np.arange(time_count)[:, None]
    lags = np.arange(count)[None, :]
    angle = 2.0 * math.pi / time_count * ((samples * lags) % time_count)
    table = np.zeros((time_count, lanes), np.float32)
    table[:, :count] = np.cos(angle) / time_count
    table[:, count : 2 * count] = np.sin(angle) / time_count
    return table


def lag_choice(count, quarter):
    side = count * 2 * quarter
    choice = np.zeros((2 * count, count, 2, count, 2, quarter), np.float32)
    for f in range(count):
        for g in range(count):
            sign = 1.0 if g >= f else -1.0
            lag = abs(g - f)
            choice[lag, f, 0, g, 0] = 1.0
            choice[lag, f, 1, g, 1] = 1.0
            choice[count + lag, f, 0, g, 1] = -sign
            choice[count + lag, f, 1, g, 0] = sign
    same = np.arange(quarter)[:, None] == np.arange(side)[None, :] % quarter
    return choice.reshape(2 * count, 2 * count * side), same.astype(np.float32)


def pack_rows(stage, slot, row, rank, first, second):
    size = first.shape[0]
    stage[slot, pl.ds(row, size), :] = first
    stage[slot, pl.ds(row + rank, size), :] = second


def unpack_rows(stage, slot, row, rank, total, coeffs, base):
    slots = total - total // 7
    first = stage[slot, pl.ds(row, slots), :]
    second = stage[slot, pl.ds(row + rank, slots), :]
    ids = lax.broadcasted_iota(jnp.int32, first.shape, 0)
    at = pl.ds(pl.multiple_of(base, 16), slots)
    coeffs[0, at, :] = jnp.where(ids < rank, first, 0.0).astype(bf16)
    coeffs[1, at, :] = jnp.where(ids < total - rank, second, 0.0).astype(bf16)


def side_by_side(real, imag):
    flat = (-1, real.shape[-1])
    return jnp.concatenate([real.reshape(flat), imag.reshape(flat)], axis=1)


def plain_product(coeffs, both):
    half, tile = coeffs.shape[1] // 2, both.shape[1] // 2
    product = dot(coeffs, both, 0, 0)
    lead, trail = product[:, :tile], product[:, tile:]
    return jnp.concatenate([lead[:half] - trail[half:], lead[half:] + trail[:half]], axis=0)


def parity(value, mask):
    odd = value & 0
    bit = 0
    while mask >> bit:
        if (mask >> bit) & 1:
            odd = odd ^ ((value >> bit) & 1)
        bit += 1
    return odd


def exchange_slots(devices):
    half = devices // 2
    spare, mixed = list(range(half, devices)), []
    alone = []
    for near in reversed(range(1, half)):
        found = [
            (far, mask)
            for far in spare
            for mask in range(1, devices)
            if not parity(near, mask) and not parity(far, mask)
        ]
        if found and len(spare) > 1:
            far, mask = found[0]
            spare.remove(far)
            mixed += [(far, near, mask), (near, far, mask)]
        else:
            alone.append((near, near, 1))
    first = [(far, far, 1) for far in reversed(spare)]
    return first, mixed + alone + [(0, 0, 1)]


def partner(me, slot):
    even, odd, mask = slot
    if even == odd:
        return me ^ even
    return me ^ (even ^ (parity(me, mask) * (even ^ odd)))


def owner_slots(owners):
    mixed = [(1, 2), (2, 1)] if owners > 2 else [(n, n) for n in range(1, owners)]
    return [(n, n) for n in reversed(range(3, owners))] + mixed + [(0, 0)]


def owner(mine, me, slot):
    even, odd = slot
    return mine ^ even if even == odd else mine ^ (even ^ ((me & 1) * (even ^ odd)))


def unstage(outs, slots_out, stage, m, devices, span, size, me):
    for out, slot in zip(outs, slots_out):
        for c in range(span):
            rows = stage[(m * devices + partner(me, slot)) * span + c, pl.ds(0, size), :]
            out[m, pl.ds(c * size, size), :] = rows.astype(bf16)


def adjoint_part(slots_out, first_rank, ranks, turned, basis, outs, stage, waits):
    shifts = sorted({n for slot in slots_out for n in slot[:2]})
    freqs, rows, devices, cols, _, slots, tile = basis.shape
    total = slots + slots // 6
    me = lax.axis_index("tile")
    for i in range(rows):
        for copy in waits[i]:
            copy.wait()
        for m in range(freqs // 2):
            pair = []
            for f in (2 * m, 2 * m + 1):
                real = jnp.concatenate([basis[f, i, me ^ n, :, 0] for n in shifts], axis=0)
                imag = jnp.concatenate([basis[f, i, me ^ n, :, 1] for n in shifts], axis=0)
                pair.append(dot(side_by_side(real, imag), turned[f, i], 1, 0))
            for n, shift in enumerate(shifts):
                for c in range(cols):
                    col = (me ^ shift) * cols + c
                    rank = ranks[0, first_rank + (m * rows + i) * devices * cols + col]
                    cut = slice((n * cols + c) * slots, (n * cols + c + 1) * slots)
                    pack_rows(stage, m * devices * cols + col, i * total, rank, pair[0][cut], pair[1][cut])
    for m in range(freqs // 2):
        unstage(outs, slots_out, stage, m, devices, cols, rows * total, me)


def adjoint_kernel(slots_out, cols, ranks_far, u_far, basis_far, *rest):
    outs = rest[: len(slots_out)]
    turned, basis, short_out, ranks, short, u_ref, stage, sems = rest[len(slots_out) :]
    freqs, rows, devices, _, _, slots, tile = basis.shape
    row_tiles, col_tiles = ranks.shape[1:]
    half = turned.shape[3] // 2
    me = lax.axis_index("tile")
    shifts = sorted({n for slot in slots_out for n in slot[:2]})
    rank_copy = pltpu.make_async_copy(ranks_far, ranks, sems.at[0])
    data_copy = pltpu.make_async_copy(u_far, u_ref, sems.at[1])
    data_copy.start()
    rank_copy.start()
    early, late, at = [[] for _ in range(rows)], [], 3
    for group in (shifts, [n for n in range(devices) if n not in shifts]):
        for i in range(rows):
            for f in range(freqs):
                for n in group:
                    copy = pltpu.make_async_copy(
                        basis_far.at[f, i, me ^ n], basis.at[f, i, me ^ n], sems.at[at]
                    )
                    at += 1
                    copy.start(priority=n % 2)
                    (early[i] if group is shifts else late).append(copy)
    rank_copy.wait()
    first_rank = freqs // 2 * row_tiles * cols
    for m in range(freqs // 2):
        for row in range(row_tiles):
            for c in range(cols):
                short[0, (m * row_tiles + row) * cols + c] = ranks[2 * m, row, me * cols + c]
        for i in range(rows):
            for col in range(col_tiles):
                short[0, first_rank + (m * rows + i) * col_tiles + col] = ranks[2 * m, me * rows + i, col]
    short_copy = pltpu.make_async_copy(short, short_out, sems.at[2])
    short_copy.start()
    data_copy.wait()
    for f in range(freqs):
        for i in range(rows):
            values = u_ref[f, i * tile : (i + 1) * tile, :]
            wide = values.astype(f32)
            lane = lax.broadcasted_iota(jnp.int32, wide.shape, 1)
            rolled = pltpu.roll(wide, half, 1)
            turned[f, i, :tile, :] = values
            turned[f, i, tile:, :] = jnp.where(lane < half, rolled, -rolled).astype(bf16)
    adjoint_part(slots_out, first_rank, short, turned, basis, outs, stage, early)
    short_copy.wait()
    for copy in late:
        copy.wait()


def adjoint_rest_kernel(slots_out, first_rank, short, turned, basis, *rest):
    outs = rest[: len(slots_out)]
    ranks, stage, sem = rest[len(slots_out) :]
    rank_copy = pltpu.make_async_copy(short, ranks, sem)
    rank_copy.start()
    waits = [[rank_copy]] + [[]] * (basis.shape[1] - 1)
    adjoint_part(slots_out, first_rank, ranks, turned, basis, outs, stage, waits)


def gathered(slots_in):
    shifts = sorted({n for slot in slots_in for n in slot[:2]})

    def place(me, slot):
        even, odd, mask = slot
        first, second = shifts.index(even), shifts.index(odd)
        return first if even == odd else first + parity(me, mask) * (second - first)

    return shifts, place


def image_kernel(slots_in, owners, ranks_near, basis, *rest):
    devices = len(slots_in)
    packed = rest[:devices]
    outs = rest[-owners - 5 : -5]
    ranks, stage, coeffs, z, sem = rest[-5:]
    freqs, _, rows, cols, _, slots, tile = basis.shape
    total = slots + slots // 6
    half = coeffs.shape[3] // 2
    quarter = half // owners
    size = rows * total
    me, mine = lax.axis_index("tile"), lax.axis_index("freq")
    rank_copy = pltpu.make_async_copy(ranks_near, ranks, sem)
    rank_copy.start()
    for m in range(freqs // 2):
        for s in range(devices):
            for c in range(cols):
                block = packed[s][m, pl.ds(c * size, size), :]
                stage[(m * devices + s) * cols + c, pl.ds(0, size), :] = block.astype(f32)
    rank_copy.wait()
    for m in range(freqs // 2):
        for c in range(cols):
            for s in range(devices):
                for i in range(rows):
                    row = partner(me, slots_in[s]) * rows + i
                    rank = ranks[0, (m * devices * rows + row) * cols + c]
                    slot = (m * devices + s) * cols + c
                    unpack_rows(stage, slot, i * total, rank, total, coeffs.at[c], row * slots)
            for n in range(2):
                f = 2 * m + n
                both = side_by_side(basis[f, :, :, c, 0], basis[f, :, :, c, 1])
                z[f, :, pl.ds(c * tile, tile)] = plain_product(coeffs[c, n], both)
    for r, slot in enumerate(owner_slots(owners)):
        low = pl.multiple_of(owner(mine, me, slot) * quarter, quarter)
        for f in range(freqs):
            real = z[f, pl.ds(low, quarter), :]
            imag = z[f, pl.ds(half + low, quarter), :]
            outs[r][f] = jnp.concatenate([real, imag], axis=0).astype(bf16)


def prepare_kernel(basis_far, mask, table, choice, same, *rest):
    basis, high, low, full, sem = rest[-5:]
    basis_copy = pltpu.make_async_copy(basis_far, basis, sem)
    basis_copy.start()
    exact = lax.Precision.HIGHEST
    full[...] = dot(mask[...].astype(f32), table[...], 0, 0, exact)
    quarter, side = same.shape
    mine = full[pl.ds(pl.multiple_of(lax.axis_index("freq") * quarter, quarter), quarter), :]
    entries = dot(mine[:, : choice.shape[0]], choice[...], 1, 0, exact)
    for n in range(side // quarter):
        block = entries[:, n * side : (n + 1) * side] * same[...]
        upper = block.astype(bf16)
        high[n * quarter : (n + 1) * quarter, :] = upper
        low[n * quarter : (n + 1) * quarter, :] = (block - upper.astype(f32)).astype(bf16)
    basis_copy.wait()


def mix_kernel(owners, high, low, *rest):
    arrived = rest[:owners]
    outs = rest[owners : 2 * owners]
    z, w = rest[2 * owners :]
    freqs, rows, span = arrived[0].shape
    me, mine = lax.axis_index("tile"), lax.axis_index("freq")
    size = freqs * rows
    places = [pl.multiple_of(owner(mine, me, slot) * size, 16) for slot in owner_slots(owners)]
    for r in range(owners):
        z[pl.ds(places[r], size), :] = arrived[r][...].reshape(size, span)
    w[...] = dot(high[...], z[...], 1, 0) + dot(low[...], z[...], 1, 0)
    for r in range(owners):
        block = w[pl.ds(places[r], size), :]
        outs[r][...] = block.reshape(freqs, rows, span).astype(bf16)


def forward_kernel(slots_out, owners, ranks_near, basis, *rest):
    devices = len(slots_out)
    arrived = rest[:owners]
    outs = rest[owners : owners + devices]
    ranks, w, stage, sem = rest[owners + devices :]
    freqs, _, rows, cols, _, slots, tile = basis.shape
    total = slots + slots // 6
    half = w.shape[2] // 2
    quarter = half // owners
    me, mine = lax.axis_index("tile"), lax.axis_index("freq")
    rank_copy = pltpu.make_async_copy(ranks_near, ranks, sem)
    rank_copy.start()
    for r, slot in enumerate(owner_slots(owners)):
        low = pl.multiple_of(owner(mine, me, slot) * quarter, quarter)
        for f in range(freqs):
            for c in range(cols):
                at = slice(c * tile, (c + 1) * tile)
                real, imag = arrived[r][f, :quarter, at], arrived[r][f, quarter:, at]
                w[f, c, pl.ds(low, quarter), :tile] = real
                w[f, c, pl.ds(half + low, quarter), :tile] = imag
                w[f, c, pl.ds(low, quarter), tile:] = imag
                w[f, c, pl.ds(half + low, quarter), tile:] = -real
    rank_copy.wait()
    for m in range(freqs // 2):
        for c in range(cols):
            pair = []
            for f in (2 * m, 2 * m + 1):
                both = side_by_side(basis[f, :, :, c, 0], basis[f, :, :, c, 1])
                pair.append(dot(both, w[f, c], 1, 1))
            for d in range(devices):
                for i in range(rows):
                    rank = ranks[0, (m * devices * rows + d * rows + i) * cols + c]
                    cut = slice((d * rows + i) * slots, (d * rows + i + 1) * slots)
                    slot = (m * devices + d) * cols + c
                    pack_rows(stage, slot, i * total, rank, pair[0][cut], pair[1][cut])
        unstage(outs, slots_out, stage, m, devices, cols, rows * total, me)


def result_kernel(slots_in, last, ranks_near, basis, *rest):
    count = len(slots_in)
    shifts, place = gathered(slots_in)
    packed, rest = rest[:count], rest[count:]
    out, ranks, stage, coeffs, sem = rest[-5:]
    freqs, rows, devices, cols, _, slots, tile = basis.shape
    total = slots + slots // 6
    size = rows * total
    first_rank = freqs // 2 * devices * rows * cols
    me = lax.axis_index("tile")
    rank_copy = pltpu.make_async_copy(ranks_near, ranks, sem)
    rank_copy.start()
    for m in range(freqs // 2):
        for n in range(count):
            for c in range(cols):
                block = packed[n][m, pl.ds(c * size, size), :]
                stage[(m * count + n) * cols + c, pl.ds(0, size), :] = block.astype(f32)
    rank_copy.wait()
    for m in range(freqs // 2):
        for i in range(rows):
            for n, slot in enumerate(slots_in):
                for c in range(cols):
                    col = partner(me, slot) * cols + c
                    rank = ranks[0, first_rank + (m * rows + i) * devices * cols + col]
                    base = (place(me, slot) * cols + c) * slots
                    unpack_rows(stage, (m * count + n) * cols + c, i * total, rank, total, coeffs.at[i], base)
            for n in range(2):
                f = 2 * m + n
                real = jnp.concatenate([basis[f, i, me ^ shift, :, 0] for shift in shifts], axis=0)
                imag = jnp.concatenate([basis[f, i, me ^ shift, :, 1] for shift in shifts], axis=0)
                part = plain_product(coeffs[i, n], side_by_side(real, imag))
                if last:
                    out[f, pl.ds(i * tile, tile), :] = (part + rest[0][f, i]).T.astype(bf16)
                else:
                    out[f, i] = part


def send(value, axis, slot):
    if slot[:2] == (0, 0):
        return value
    return lax.ppermute(value, axis, [(d, partner(d, slot)) for d in range(lax.axis_size(axis))])


def spread(values, axis, slots):
    return [(whole, send(value, axis, slot)) for value, slot in zip(values, slots)]


def to_owners(values):
    owners, devices = lax.axis_size("freq"), lax.axis_size("tile")
    landed = []
    for value, slot in zip(values, owner_slots(owners)):
        if slot != (0, 0):
            pairs = [
                (mine * devices + me, owner(mine, me, slot) * devices + me)
                for mine in range(owners)
                for me in range(devices)
            ]
            value = lax.ppermute(value, ("freq", "tile"), pairs)
        landed.append((whole, value))
    return landed


def local(u_data, u_basis, v_basis, ranks, time_mask):
    freqs, row_count, width = u_data.shape
    rows, col_tiles, _, slots, tile = u_basis.shape[1:]
    row_tiles, cols = v_basis.shape[1:3]
    total = slots // 6 + slots
    pairs = freqs // 2
    devices = lax.axis_size("tile")
    owners = lax.axis_size("freq")
    stage_rows = rows * total + 2 * slots
    quarter = width // 2 // owners
    count = owners * freqs
    side = count * 2 * quarter
    by_cols = u_basis.reshape(freqs, rows, devices, cols, 2, slots, tile)
    by_rows = v_basis.reshape(freqs, devices, rows, cols, 2, slots, tile)
    packed_kind = ((pairs, cols * rows * total, width), bf16)
    per_device = [packed_kind] * devices
    per_owner = [((freqs, 2 * quarter, cols * tile), bf16)] * owners
    work = {"flops": 4 * row_count * slots * width * col_tiles * freqs * 2, "moved": u_basis.size * 2}
    count_short = pairs * (row_tiles * cols + rows * col_tiles)
    ranks_here = pltpu.SMEM((1, count_short), jnp.int32)
    stage = pltpu.VMEM((pairs * devices * cols, stage_rows, width), f32)
    one = pltpu.SemaphoreType.DMA

    table = lag_tables(count, time_mask.shape[0], 128)
    choice, same = lag_choice(count, quarter)
    def share(partners):
        return {name: value * partners // devices for name, value in work.items()}

    early, late = exchange_slots(devices)
    slots_all = early + late
    *packed, data, basis, short = call(
        functools.partial(adjoint_kernel, early, cols),
        "adjoint",
        [(far, hold(x)) for x in (ranks, u_data, by_cols)],
        [packed_kind] * len(early)
        + [((freqs, rows, 2 * tile, width), bf16), (by_cols.shape, bf16), ((1, count_short), jnp.int32)],
        [
            pltpu.SMEM(ranks.shape, jnp.int32),
            ranks_here,
            pltpu.VMEM((freqs, row_count, width), bf16),
            stage,
            one((3 + freqs * rows * devices,)),
        ],
        **share(len(early)),
    )
    packed += call(
        functools.partial(adjoint_rest_kernel, late, pairs * row_tiles * cols),
        "adjoint",
        [(whole, short), (whole, data), (whole, basis)],
        [packed_kind] * len(late),
        [ranks_here, stage, one],
        **share(len(late)),
    )
    near, *window = call(
        prepare_kernel,
        "prepare",
        [(far, hold(by_rows))]
        + [(whole, jnp.asarray(x)) for x in (time_mask, table, choice, same)]
        + [(anywhere, packed[-1])],
        [(by_rows.shape, bf16)] + [((side, side), bf16)] * 2,
        [pltpu.VMEM((width // 2, 128), f32), one],
        flops=6 * quarter * 2 * count * 2 * count * side,
        moved=u_basis.size * 2,
    )
    cut = len(early) + len([slot for slot in late if slot[0] != slot[1]]) // 4 * 2
    own = len(slots_all) - 1
    groups = [list(range(cut)) + [own], list(range(cut, own))]

    def landed(packed):
        arrived = spread(packed, "tile", slots_all)
        return [[arrived[n] for n in group] for group in groups]

    def stage_for(partners):
        return pltpu.VMEM((pairs * partners * cols, stage_rows, width), f32)

    images = call(
        functools.partial(image_kernel, slots_all, owners),
        "image",
        [(whole, short), (whole, near)] + spread(packed, "tile", slots_all),
        per_owner,
        [
            ranks_here,
            stage,
            pltpu.VMEM((cols, 2, row_tiles * slots, width), bf16),
            pltpu.VMEM((freqs, width, cols * tile), f32),
            one,
        ],
        **work,
    )
    mixed = call(
        functools.partial(mix_kernel, owners),
        "mix",
        [(whole, x) for x in window] + to_owners(images),
        per_owner,
        [pltpu.VMEM((side, cols * tile), bf16), pltpu.VMEM((side, cols * tile), f32)],
        flops=4 * side * side * cols * tile,
    )
    packed = call(
        functools.partial(forward_kernel, slots_all, owners),
        "forward",
        [(whole, short), (whole, near)] + to_owners(mixed),
        per_device,
        [ranks_here, pltpu.VMEM((freqs, cols, width, 2 * tile), bf16), stage, one],
        **work,
    )
    out = []
    for group, arrived in zip(groups, landed(packed)):
        last = group is groups[-1]
        out = call(
            functools.partial(result_kernel, [slots_all[n] for n in group], last),
            "result",
            [(whole, short), (whole, basis)] + arrived + [(whole, x) for x in out],
            [((freqs, row_count, width), bf16) if last else ((freqs, rows, width, tile), f32)],
            [
                ranks_here,
                stage_for(len(group)),
                pltpu.VMEM((rows, 2, len(group) * cols * slots, width), bf16),
                one,
            ],
            **share(len(group)),
        )
    return out[0]


def solution(mesh):
    placed = (
        P("freq", "tile", None),
        P("freq", "tile", None, None, None, None),
        P("freq", None, "tile", None, None, None),
        P("freq", None, None),
        P(),
    )
    return jax.shard_map(
        local, mesh=mesh, in_specs=placed, out_specs=P("freq", "tile", None), check_vma=False
    )
```

```python
import functools
import math

import jax
import jax.numpy as jnp
import numpy as np
from jax import lax
from jax.experimental import pallas as pl
from jax.experimental.pallas import tpu as pltpu
from jax.sharding import PartitionSpec as P

vmem_limit = 48 * 1024 * 1024
bf16 = jnp.bfloat16
f32 = jnp.float32

whole = pl.BlockSpec(memory_space=pltpu.VMEM)
scalars = pl.BlockSpec(memory_space=pltpu.SMEM)
far = pl.BlockSpec(memory_space=pltpu.HBM)
anywhere = pl.BlockSpec(memory_space=pl.ANY)


def hold(value):
    return pltpu.with_memory_space_constraint(value, pltpu.HBM)


def call(kernel, name, ins, outs, scratch, flops=0, moved=0, specs=None):
    shapes = [jax.ShapeDtypeStruct(shape, kind) for shape, kind in outs]
    return pl.pallas_call(
        kernel,
        in_specs=[spec for spec, _ in ins],
        out_specs=specs or [whole] * len(outs),
        out_shape=shapes,
        scratch_shapes=scratch,
        compiler_params=pltpu.CompilerParams(vmem_limit_bytes=vmem_limit),
        cost_estimate=pl.CostEstimate(flops=flops, bytes_accessed=moved, transcendentals=0),
        name=name,
    )(*[value for _, value in ins])


def dot(lhs, rhs, lhs_dim, rhs_dim, precision=None):
    return lax.dot_general(
        lhs, rhs, (((lhs_dim,), (rhs_dim,)), ((), ())),
        precision=precision, preferred_element_type=f32,
    )


def lag_tables(count, time_count, lanes):
    samples = np.arange(time_count)[:, None]
    lags = np.arange(count)[None, :]
    angle = 2.0 * math.pi / time_count * ((samples * lags) % time_count)
    table = np.zeros((time_count, lanes), np.float32)
    table[:, :count] = np.cos(angle) / time_count
    table[:, count : 2 * count] = np.sin(angle) / time_count
    return table


def lag_choice(count, quarter):
    side = count * 2 * quarter
    choice = np.zeros((2 * count, count, 2, count, 2, quarter), np.float32)
    for f in range(count):
        for g in range(count):
            sign = 1.0 if g >= f else -1.0
            lag = abs(g - f)
            choice[lag, f, 0, g, 0] = 1.0
            choice[lag, f, 1, g, 1] = 1.0
            choice[count + lag, f, 0, g, 1] = -sign
            choice[count + lag, f, 1, g, 0] = sign
    same = np.arange(quarter)[:, None] == np.arange(side)[None, :] % quarter
    return choice.reshape(2 * count, 2 * count * side), same.astype(np.float32)


def pack_rows(stage, slot, row, rank, first, second):
    size = first.shape[0]
    stage[slot, pl.ds(row, size), :] = first
    stage[slot, pl.ds(row + rank, size), :] = second


def unpack_rows(stage, slot, row, rank, total, coeffs, base):
    slots = total - total // 7
    first = stage[slot, pl.ds(row, slots), :]
    second = stage[slot, pl.ds(row + rank, slots), :]
    ids = lax.broadcasted_iota(jnp.int32, first.shape, 0)
    at = pl.ds(pl.multiple_of(base, 16), slots)
    coeffs[0, at, :] = jnp.where(ids < rank, first, 0.0).astype(bf16)
    coeffs[1, at, :] = jnp.where(ids < total - rank, second, 0.0).astype(bf16)


def side_by_side(real, imag):
    flat = (-1, real.shape[-1])
    return jnp.concatenate([real.reshape(flat), imag.reshape(flat)], axis=1)


def plain_product(coeffs, both):
    half, tile = coeffs.shape[1] // 2, both.shape[1] // 2
    product = dot(coeffs, both, 0, 0)
    lead, trail = product[:, :tile], product[:, tile:]
    return jnp.concatenate([lead[:half] - trail[half:], lead[half:] + trail[:half]], axis=0)


def parity(value, mask):
    odd = value & 0
    bit = 0
    while mask >> bit:
        if (mask >> bit) & 1:
            odd = odd ^ ((value >> bit) & 1)
        bit += 1
    return odd


def exchange_slots(devices):
    half = devices // 2
    spare, mixed = list(range(half, devices)), []
    alone = []
    for near in range(2, half):
        found = [
            (far, mask)
            for far in spare
            for mask in range(3, devices, 2)
            if not parity(near, mask) and not parity(far, mask)
        ]
        if found and len(spare) > 2:
            far, mask = found[0]
            spare.remove(far)
            mixed += [(far, near, mask), (near, far, mask)]
        else:
            alone.append((near, near, 1))
    first = [(far, far, 1) for far in reversed(spare)]
    return first, mixed + alone + [(1, 1, 1)] * (devices > 1) + [(0, 0, 1)]


def partner(me, slot):
    even, odd, mask = slot
    if even == odd:
        return me ^ even
    return me ^ (even ^ (parity(me, mask) * (even ^ odd)))


def owner_slots(owners):
    mixed = [(1, 2), (2, 1)] if owners > 2 else [(n, n) for n in range(1, owners)]
    return [(n, n) for n in reversed(range(3, owners))] + mixed + [(0, 0)]


def owner(mine, me, slot):
    even, odd = slot
    return mine ^ even if even == odd else mine ^ (even ^ ((me & 1) * (even ^ odd)))


def unstage(outs, slots_out, stage, m, devices, span, size, me):
    for out, slot in zip(outs, slots_out):
        for c in range(span):
            rows = stage[(m * devices + partner(me, slot)) * span + c, pl.ds(0, size), :]
            out[m, pl.ds(c * size, size), :] = rows.astype(bf16)


def adjoint_part(slots_out, first_rank, ranks, turned, basis, outs, stage, waits):
    shifts = sorted({n for slot in slots_out for n in slot[:2]})
    freqs, rows, devices, cols, _, slots, tile = basis.shape
    total = slots + slots // 6
    me = lax.axis_index("tile")
    for i in range(rows):
        for copy in waits[i]:
            copy.wait()
        for m in range(freqs // 2):
            pair = []
            for f in (2 * m, 2 * m + 1):
                real = jnp.concatenate([basis[f, i, me ^ n, :, 0] for n in shifts], axis=0)
                imag = jnp.concatenate([basis[f, i, me ^ n, :, 1] for n in shifts], axis=0)
                pair.append(dot(side_by_side(real, imag), turned[f, i], 1, 0))
            for n, shift in enumerate(shifts):
                for c in range(cols):
                    col = (me ^ shift) * cols + c
                    rank = ranks[0, first_rank + (m * rows + i) * devices * cols + col]
                    cut = slice((n * cols + c) * slots, (n * cols + c + 1) * slots)
                    pack_rows(stage, m * devices * cols + col, i * total, rank, pair[0][cut], pair[1][cut])
    for m in range(freqs // 2):
        unstage(outs, slots_out, stage, m, devices, cols, rows * total, me)


def adjoint_kernel(slots_out, cols, ranks_far, u_far, basis_far, *rest):
    outs = rest[: len(slots_out)]
    turned, basis, short_out, ranks, short, u_ref, stage, sems = rest[len(slots_out) :]
    freqs, rows, devices, _, _, slots, tile = basis.shape
    row_tiles, col_tiles = ranks.shape[1:]
    half = turned.shape[3] // 2
    me = lax.axis_index("tile")
    shifts = sorted({n for slot in slots_out for n in slot[:2]})
    rank_copy = pltpu.make_async_copy(ranks_far, ranks, sems.at[0])
    data_copy = pltpu.make_async_copy(u_far, u_ref, sems.at[1])
    data_copy.start()
    rank_copy.start()
    early, late, at = [[] for _ in range(rows)], [], 3
    for group in (shifts, [n for n in range(devices) if n not in shifts]):
        for i in range(rows):
            for f in range(freqs):
                for n in group:
                    copy = pltpu.make_async_copy(
                        basis_far.at[f, i, me ^ n], basis.at[f, i, me ^ n], sems.at[at]
                    )
                    at += 1
                    copy.start(priority=n % 2)
                    (early[i] if group is shifts else late).append(copy)
    rank_copy.wait()
    first_rank = freqs // 2 * row_tiles * cols
    for m in range(freqs // 2):
        for row in range(row_tiles):
            for c in range(cols):
                short[0, (m * row_tiles + row) * cols + c] = ranks[2 * m, row, me * cols + c]
        for i in range(rows):
            for col in range(col_tiles):
                short[0, first_rank + (m * rows + i) * col_tiles + col] = ranks[2 * m, me * rows + i, col]
    short_copy = pltpu.make_async_copy(short, short_out, sems.at[2])
    short_copy.start()
    data_copy.wait()
    for f in range(freqs):
        for i in range(rows):
            values = u_ref[f, i * tile : (i + 1) * tile, :]
            wide = values.astype(f32)
            lane = lax.broadcasted_iota(jnp.int32, wide.shape, 1)
            rolled = pltpu.roll(wide, half, 1)
            turned[f, i, :tile, :] = values
            turned[f, i, tile:, :] = jnp.where(lane < half, rolled, -rolled).astype(bf16)
    adjoint_part(slots_out, first_rank, short, turned, basis, outs, stage, early)
    short_copy.wait()
    for copy in late:
        copy.wait()


def adjoint_rest_kernel(slots_out, first_rank, short, turned, basis, *rest):
    outs = rest[: len(slots_out)]
    ranks, stage, sem = rest[len(slots_out) :]
    rank_copy = pltpu.make_async_copy(short, ranks, sem)
    rank_copy.start()
    waits = [[rank_copy]] + [[]] * (basis.shape[1] - 1)
    adjoint_part(slots_out, first_rank, ranks, turned, basis, outs, stage, waits)


def gathered(slots_in):
    shifts = sorted({n for slot in slots_in for n in slot[:2]})

    def place(me, slot):
        even, odd, mask = slot
        first, second = shifts.index(even), shifts.index(odd)
        return first if even == odd else first + parity(me, mask) * (second - first)

    return shifts, place


def image_kernel(slots_in, owners, ranks_near, basis, *rest):
    devices = len(slots_in)
    packed = rest[:devices]
    outs = rest[-owners - 5 : -5]
    ranks, stage, coeffs, z, sem = rest[-5:]
    freqs, _, rows, cols, _, slots, tile = basis.shape
    total = slots + slots // 6
    half = coeffs.shape[3] // 2
    quarter = half // owners
    size = rows * total
    me, mine = lax.axis_index("tile"), lax.axis_index("freq")
    rank_copy = pltpu.make_async_copy(ranks_near, ranks, sem)
    rank_copy.start()
    for m in range(freqs // 2):
        for s in range(devices):
            for c in range(cols):
                block = packed[s][m, pl.ds(c * size, size), :]
                stage[(m * devices + s) * cols + c, pl.ds(0, size), :] = block.astype(f32)
    rank_copy.wait()
    for m in range(freqs // 2):
        for c in range(cols):
            for s in range(devices):
                for i in range(rows):
                    row = partner(me, slots_in[s]) * rows + i
                    rank = ranks[0, (m * devices * rows + row) * cols + c]
                    slot = (m * devices + s) * cols + c
                    unpack_rows(stage, slot, i * total, rank, total, coeffs.at[c], row * slots)
            for n in range(2):
                f = 2 * m + n
                both = side_by_side(basis[f, :, :, c, 0], basis[f, :, :, c, 1])
                z[f, :, pl.ds(c * tile, tile)] = plain_product(coeffs[c, n], both)
    for r, slot in enumerate(owner_slots(owners)):
        low = pl.multiple_of(owner(mine, me, slot) * quarter, quarter)
        for f in range(freqs):
            real = z[f, pl.ds(low, quarter), :]
            imag = z[f, pl.ds(half + low, quarter), :]
            outs[r][f] = jnp.concatenate([real, imag], axis=0).astype(bf16)


def prepare_kernel(basis_far, mask, table, choice, same, *rest):
    basis, high, low, full, sem = rest[-5:]
    basis_copy = pltpu.make_async_copy(basis_far, basis, sem)
    basis_copy.start()
    exact = lax.Precision.HIGHEST
    full[...] = dot(mask[...].astype(f32), table[...], 0, 0, exact)
    quarter, side = same.shape
    mine = full[pl.ds(pl.multiple_of(lax.axis_index("freq") * quarter, quarter), quarter), :]
    entries = dot(mine[:, : choice.shape[0]], choice[...], 1, 0, exact)
    for n in range(side // quarter):
        block = entries[:, n * side : (n + 1) * side] * same[...]
        upper = block.astype(bf16)
        high[n * quarter : (n + 1) * quarter, :] = upper
        low[n * quarter : (n + 1) * quarter, :] = (block - upper.astype(f32)).astype(bf16)
    basis_copy.wait()


def mix_kernel(owners, high, low, *rest):
    arrived = rest[:owners]
    outs = rest[owners : 2 * owners]
    z, w = rest[2 * owners :]
    freqs, rows, span = arrived[0].shape
    me, mine = lax.axis_index("tile"), lax.axis_index("freq")
    size = freqs * rows
    places = [pl.multiple_of(owner(mine, me, slot) * size, 16) for slot in owner_slots(owners)]
    for r in range(owners):
        z[pl.ds(places[r], size), :] = arrived[r][...].reshape(size, span)
    w[...] = dot(high[...], z[...], 1, 0) + dot(low[...], z[...], 1, 0)
    for r in range(owners):
        block = w[pl.ds(places[r], size), :]
        outs[r][...] = block.reshape(freqs, rows, span).astype(bf16)


def forward_kernel(slots_out, owners, ranks_near, basis, *rest):
    devices = len(slots_out)
    arrived = rest[:owners]
    outs = rest[owners : owners + devices]
    ranks, w, stage, sem = rest[owners + devices :]
    freqs, _, rows, cols, _, slots, tile = basis.shape
    total = slots + slots // 6
    half = w.shape[2] // 2
    quarter = half // owners
    me, mine = lax.axis_index("tile"), lax.axis_index("freq")
    rank_copy = pltpu.make_async_copy(ranks_near, ranks, sem)
    rank_copy.start()
    for r, slot in enumerate(owner_slots(owners)):
        low = pl.multiple_of(owner(mine, me, slot) * quarter, quarter)
        for f in range(freqs):
            for c in range(cols):
                at = slice(c * tile, (c + 1) * tile)
                real, imag = arrived[r][f, :quarter, at], arrived[r][f, quarter:, at]
                w[f, c, pl.ds(low, quarter), :tile] = real
                w[f, c, pl.ds(half + low, quarter), :tile] = imag
                w[f, c, pl.ds(low, quarter), tile:] = imag
                w[f, c, pl.ds(half + low, quarter), tile:] = -real
    rank_copy.wait()
    for m in range(freqs // 2):
        for c in range(cols):
            pair = []
            for f in (2 * m, 2 * m + 1):
                both = side_by_side(basis[f, :, :, c, 0], basis[f, :, :, c, 1])
                pair.append(dot(both, w[f, c], 1, 1))
            for d in range(devices):
                for i in range(rows):
                    rank = ranks[0, (m * devices * rows + d * rows + i) * cols + c]
                    cut = slice((d * rows + i) * slots, (d * rows + i + 1) * slots)
                    slot = (m * devices + d) * cols + c
                    pack_rows(stage, slot, i * total, rank, pair[0][cut], pair[1][cut])
        unstage(outs, slots_out, stage, m, devices, cols, rows * total, me)


def result_kernel(slots_in, last, ranks_near, basis, *rest):
    count = len(slots_in)
    shifts, place = gathered(slots_in)
    packed, rest = rest[:count], rest[count:]
    out, ranks, stage, coeffs, sem = rest[-5:]
    freqs, rows, devices, cols, _, slots, tile = basis.shape
    total = slots + slots // 6
    size = rows * total
    first_rank = freqs // 2 * devices * rows * cols
    me = lax.axis_index("tile")
    rank_copy = pltpu.make_async_copy(ranks_near, ranks, sem)
    rank_copy.start()
    for m in range(freqs // 2):
        for n in range(count):
            for c in range(cols):
                block = packed[n][m, pl.ds(c * size, size), :]
                stage[(m * count + n) * cols + c, pl.ds(0, size), :] = block.astype(f32)
    rank_copy.wait()
    for m in range(freqs // 2):
        for i in range(rows):
            for n, slot in enumerate(slots_in):
                for c in range(cols):
                    col = partner(me, slot) * cols + c
                    rank = ranks[0, first_rank + (m * rows + i) * devices * cols + col]
                    base = (place(me, slot) * cols + c) * slots
                    unpack_rows(stage, (m * count + n) * cols + c, i * total, rank, total, coeffs.at[i], base)
            for n in range(2):
                f = 2 * m + n
                real = jnp.concatenate([basis[f, i, me ^ shift, :, 0] for shift in shifts], axis=0)
                imag = jnp.concatenate([basis[f, i, me ^ shift, :, 1] for shift in shifts], axis=0)
                part = plain_product(coeffs[i, n], side_by_side(real, imag))
                if last:
                    out[f, pl.ds(i * tile, tile), :] = (part + rest[0][f, i]).T.astype(bf16)
                else:
                    out[f, i] = part


def send(value, axis, slot):
    if slot[:2] == (0, 0):
        return value
    return lax.ppermute(value, axis, [(d, partner(d, slot)) for d in range(lax.axis_size(axis))])


def spread(values, axis, slots):
    return [(whole, send(value, axis, slot)) for value, slot in zip(values, slots)]


def to_owners(values):
    owners, devices = lax.axis_size("freq"), lax.axis_size("tile")
    landed = []
    for value, slot in zip(values, owner_slots(owners)):
        if slot != (0, 0):
            pairs = [
                (mine * devices + me, owner(mine, me, slot) * devices + me)
                for mine in range(owners)
                for me in range(devices)
            ]
            value = lax.ppermute(value, ("freq", "tile"), pairs)
        landed.append((whole, value))
    return landed


def local(u_data, u_basis, v_basis, ranks, time_mask):
    freqs, row_count, width = u_data.shape
    rows, col_tiles, _, slots, tile = u_basis.shape[1:]
    row_tiles, cols = v_basis.shape[1:3]
    total = slots // 6 + slots
    pairs = freqs // 2
    devices = lax.axis_size("tile")
    owners = lax.axis_size("freq")
    stage_rows = rows * total + 2 * slots
    quarter = width // 2 // owners
    count = owners * freqs
    side = count * 2 * quarter
    by_cols = u_basis.reshape(freqs, rows, devices, cols, 2, slots, tile)
    by_rows = v_basis.reshape(freqs, devices, rows, cols, 2, slots, tile)
    packed_kind = ((pairs, cols * rows * total, width), bf16)
    per_device = [packed_kind] * devices
    per_owner = [((freqs, 2 * quarter, cols * tile), bf16)] * owners
    work = {"flops": 4 * row_count * slots * width * col_tiles * freqs * 2, "moved": u_basis.size * 2}
    count_short = pairs * (row_tiles * cols + rows * col_tiles)
    ranks_here = pltpu.SMEM((1, count_short), jnp.int32)
    stage = pltpu.VMEM((pairs * devices * cols, stage_rows, width), f32)
    one = pltpu.SemaphoreType.DMA

    table = lag_tables(count, time_mask.shape[0], 128)
    choice, same = lag_choice(count, quarter)
    def share(partners):
        return {name: value * partners // devices for name, value in work.items()}

    early, late = exchange_slots(devices)
    slots_all = early + late
    *packed, data, basis, short = call(
        functools.partial(adjoint_kernel, early, cols),
        "adjoint",
        [(far, hold(x)) for x in (ranks, u_data, by_cols)],
        [packed_kind] * len(early)
        + [((freqs, rows, 2 * tile, width), bf16), (by_cols.shape, bf16), ((1, count_short), jnp.int32)],
        [
            pltpu.SMEM(ranks.shape, jnp.int32),
            ranks_here,
            pltpu.VMEM((freqs, row_count, width), bf16),
            stage,
            one((3 + freqs * rows * devices,)),
        ],
        **share(len(early)),
    )
    packed += call(
        functools.partial(adjoint_rest_kernel, late, pairs * row_tiles * cols),
        "adjoint",
        [(whole, short), (whole, data), (whole, basis)],
        [packed_kind] * len(late),
        [ranks_here, stage, one],
        **share(len(late)),
    )
    near, *window = call(
        prepare_kernel,
        "prepare",
        [(far, hold(by_rows))]
        + [(whole, jnp.asarray(x)) for x in (time_mask, table, choice, same)]
        + [(anywhere, packed[-1])],
        [(by_rows.shape, bf16)] + [((side, side), bf16)] * 2,
        [pltpu.VMEM((width // 2, 128), f32), one],
        flops=6 * quarter * 2 * count * 2 * count * side,
        moved=u_basis.size * 2,
    )
    cut = len(early) + len([slot for slot in late if slot[0] != slot[1]]) // 4 * 2
    own = len(slots_all) - 1
    groups = [list(range(cut)) + [own], list(range(cut, own))]

    def landed(packed):
        arrived = spread(packed, "tile", slots_all)
        return [[arrived[n] for n in group] for group in groups]

    def stage_for(partners):
        return pltpu.VMEM((pairs * partners * cols, stage_rows, width), f32)

    images = call(
        functools.partial(image_kernel, slots_all, owners),
        "image",
        [(whole, short), (whole, near)] + spread(packed, "tile", slots_all),
        per_owner,
        [
            ranks_here,
            stage,
            pltpu.VMEM((cols, 2, row_tiles * slots, width), bf16),
            pltpu.VMEM((freqs, width, cols * tile), f32),
            one,
        ],
        **work,
    )
    mixed = call(
        functools.partial(mix_kernel, owners),
        "mix",
        [(whole, x) for x in window] + to_owners(images),
        per_owner,
        [pltpu.VMEM((side, cols * tile), bf16), pltpu.VMEM((side, cols * tile), f32)],
        flops=4 * side * side * cols * tile,
    )
    packed = call(
        functools.partial(forward_kernel, slots_all, owners),
        "forward",
        [(whole, short), (whole, near)] + to_owners(mixed),
        per_device,
        [ranks_here, pltpu.VMEM((freqs, cols, width, 2 * tile), bf16), stage, one],
        **work,
    )
    out = []
    for group, arrived in zip(groups, landed(packed)):
        last = group is groups[-1]
        out = call(
            functools.partial(result_kernel, [slots_all[n] for n in group], last),
            "result",
            [(whole, short), (whole, basis)] + arrived + [(whole, x) for x in out],
            [((freqs, row_count, width), bf16) if last else ((freqs, rows, width, tile), f32)],
            [
                ranks_here,
                stage_for(len(group)),
                pltpu.VMEM((rows, 2, len(group) * cols * slots, width), bf16),
                one,
            ],
            **share(len(group)),
        )
    return out[0]


def solution(mesh):
    placed = (
        P("freq", "tile", None),
        P("freq", "tile", None, None, None, None),
        P("freq", None, "tile", None, None, None),
        P("freq", None, None),
        P(),
    )
    return jax.shard_map(
        local, mesh=mesh, in_specs=placed, out_specs=P("freq", "tile", None), check_vma=False
    )
```
